512 devices in a mesh: dp: 64 (over x, y, core), frame: 8 (over z).
Axes of the slice: x: 4, y: 8, z: 8, core: 2. Of those that a mesh axis runs over, the one named last changes fastest.
Arguments:
- video_tokens: bfloat16 [64, 8, 256, 1024], P('dp', 'frame'), may hold values from -6 to 6
- text_states: bfloat16 [64, 77, 768], P('dp'), may hold values from -6 to 6
- caption_ids: int32 [64, 77], P('dp'), may hold values from 0 to 49407, as said below
- pair_index: int32 [64], replicated, may hold values from 0 to 63, each once
- logit_scale: float32 [1], replicated, may hold values from 10 to 100
- gain_spatial: float32 [1024], replicated, may hold values from 0.25 to 1.75
- gain_temporal: float32 [1024], replicated, may hold values from 0.25 to 1.75
- gain_video: float32 [1024], replicated, may hold values from 0.25 to 1.75
- gain_text: float32 [768], replicated, may hold values from 0.25 to 1.75
- w_qkv_spatial: bfloat16 [1024, 1536], P('dp'), may hold values from -0.1875 to 0.1875
- w_out_spatial: bfloat16 [512, 1024], P('dp'), may hold values from -0.25 to 0.25
- w_qkv_temporal: bfloat16 [1024, 1536], P('dp'), may hold values from -0.1875 to 0.1875
- w_out_temporal: bfloat16 [512, 1024], P('dp'), may hold values from -0.25 to 0.25
- w_video: bfloat16 [1024, 768], P('dp'), may hold values from -0.1875 to 0.1875
- w_text: bfloat16 [768, 768], P('dp'), may hold values from -0.21875 to 0.21875
Outputs:
- layer_out: bfloat16 [64, 8, 256, 1024], P('dp', None, 'frame')
- video_loss: float32 [64], P('dp')
- text_loss: float32 [64], P('dp')
- grad_pooled: float32 [64, 1024], P('dp')
- grad_text: float32 [64, 768], P('dp')
The draws below stay inside these ranges and needn't reach their ends.
Inputs may be any that keep to these rules, and one draw needn't show every extreme that they name: `caption_ids`: in each row the ids before the end token lie in 1 to 49406, exactly one entry is the end token 49407, at position 1 to 75, and every entry after it is 0. `pair_index`: every number below 64 appears once.
All inputs are finite; a program needn't handle non-finite values.
Results may differ from the reference program's by a relative error of at most 0.012.
Values may be sent and summed in bfloat16 or wider, within the bound.
No kernel may reach another device: no remote copies, remote signals or barrier semaphores. Data moves between devices by JAX's collectives and lax.ppermute only.
A program may use at most 64 MiB of HBM per device.

```python
import math
import jax
import jax.numpy as jnp
from jax import lax

D = 1024
HEADS = 8
HD = 64
DT = 768
E = 768
P_SIZE = 256
L = 77
F = 8
B = 64


def draw_caption_ids(key, part):
    key = jax.random.fold_in(key, 7)
    length_key, word_key = jax.random.split(key)
    lengths = jax.random.randint(length_key, (B,), 2, L)
    words = jax.random.randint(word_key, (B, L), 1, 49407)
    places = jnp.arange(L)[None, :]
    ends = lengths[:, None] - 1
    ids = jnp.where(places == ends, 49407, jnp.where(places < ends, words, 0))
    return ids.astype(jnp.int32)


def levels(key, extent, pieces, least, high):
    level = 1.0
    for dim, blocks in pieces:
        heights = jax.random.uniform(jax.random.fold_in(jax.random.fold_in(key, 6), dim), (blocks,), jnp.float32, least / len(pieces), high / len(pieces))
        level = level * jnp.repeat(jnp.exp(heights), extent[dim] // blocks).reshape((-1,) + (1,) * (len(extent) - 1 - dim))
    return level


def bell_draw(key, extent, scale, bound, shards=(), kind=jnp.bfloat16):
    values = jax.random.normal(key, extent, jnp.float32) * scale
    if len(shards) > 0:
        values = levels(key, extent, shards, -0.22, 0.18) * values
    return jnp.clip(values, min=-bound, max=bound).astype(kind)


def setup_inputs(seed: int = 0) -> dict:
    streams_of = jax.random.split(jax.random.key(seed), 16)
    return {
        "video_tokens": bell_draw(streams_of[0], (B, F, P_SIZE, D), 1.0, 6.0, ((0, 64), (1, 8))),
        "text_states": bell_draw(streams_of[1], (B, L, DT), 1.0, 6.0, ((0, 64),)),
        "caption_ids": draw_caption_ids(jax.random.fold_in(streams_of[15], 71), 0),
        "pair_index": jax.random.permutation(streams_of[3], B).astype(jnp.int32),
        "logit_scale": jnp.clip(jnp.exp(jax.random.uniform(streams_of[4], (1,), jnp.float32, math.log(10.0), math.log(100.0))), 10.0, 100.0),
        "gain_spatial": jnp.clip(1.0 + 0.15 * jax.random.normal(streams_of[5], (D,), jnp.float32), 0.25, 1.75),
        "gain_temporal": jnp.clip(1.0 + 0.15 * jax.random.normal(streams_of[6], (D,), jnp.float32), 0.25, 1.75),
        "gain_video": jnp.clip(1.0 + 0.15 * jax.random.normal(streams_of[7], (D,), jnp.float32), 0.25, 1.75),
        "gain_text": jnp.clip(1.0 + 0.15 * jax.random.normal(streams_of[8], (DT,), jnp.float32), 0.25, 1.75),
        "w_qkv_spatial": bell_draw(streams_of[9], (D, 3 * HEADS * HD), D ** -0.5, 0.1875, ((0, 64),)),
        "w_out_spatial": bell_draw(streams_of[10], (HEADS * HD, D), (HEADS * HD) ** -0.5, 0.25, ((0, 64),)),
        "w_qkv_temporal": bell_draw(streams_of[11], (D, 3 * HEADS * HD), D ** -0.5, 0.1875, ((0, 64),)),
        "w_out_temporal": bell_draw(streams_of[12], (HEADS * HD, D), (HEADS * HD) ** -0.5, 0.25, ((0, 64),)),
        "w_video": bell_draw(streams_of[13], (D, E), D ** -0.5, 0.1875, ((0, 64),)),
        "w_text": bell_draw(streams_of[14], (DT, E), DT ** -0.5, 0.21875, ((0, 64),)),
    }


norm_eps = 1e-05
unit_eps = 1e-06

def layer_norm(values, gain):
    values = values.astype(jnp.float32)
    center = values - lax.optimization_barrier(jnp.mean(values, axis=-1, keepdims=True))
    spread = lax.optimization_barrier(jnp.mean(center * center, axis=-1, keepdims=True))
    return center * lax.rsqrt(spread + norm_eps) * gain

def unit_rows(values):
    return values * lax.rsqrt(lax.optimization_barrier(jnp.sum(values * values, axis=-1, keepdims=True)) + unit_eps)

def rounded(values):
    return lax.optimization_barrier(values.astype(jnp.bfloat16)).astype(jnp.float32)

def project(values, weight):
    flat = values.reshape(-1, values.shape[-1])
    result = jnp.dot(flat, weight, preferred_element_type=jnp.float32)
    return result.reshape(values.shape[:-1] + (weight.shape[1],))

def clip_layer(clip, gain_spatial, gain_temporal, w_qkv_spatial, w_out_spatial, w_qkv_temporal, w_out_temporal):
    frames, patches, width = clip.shape
    scaling = 1.0 / float(HD) ** 0.5
    normed = layer_norm(clip, gain_spatial).astype(jnp.bfloat16)
    packed = rounded(project(normed, w_qkv_spatial)).reshape(frames, patches, 3, HEADS, HD)
    scores = jnp.einsum('fqhe,fkhe->fhqk', packed[:, :, 0], packed[:, :, 1]) * scaling
    probs = rounded(jax.nn.softmax(scores, axis=-1))
    mixed = jnp.einsum('fhqk,fkhe->fqhe', probs, packed[:, :, 2]).astype(jnp.bfloat16)
    mixed = mixed.reshape(frames, patches, HEADS * HD)
    spatial = (clip.astype(jnp.float32) + project(mixed, w_out_spatial)).astype(jnp.bfloat16)
    normed = layer_norm(spatial, gain_temporal).astype(jnp.bfloat16)
    packed = rounded(project(normed, w_qkv_temporal)).reshape(frames, patches, 3, HEADS, HD)
    scores = jnp.einsum('qphe,kphe->phqk', packed[:, :, 0], packed[:, :, 1]) * scaling
    probs = rounded(jax.nn.softmax(scores, axis=-1))
    mixed = jnp.einsum('phqk,kphe->qphe', probs, packed[:, :, 2]).astype(jnp.bfloat16)
    mixed = mixed.reshape(frames, patches, HEADS * HD)
    output = (spatial.astype(jnp.float32) + project(mixed, w_out_temporal)).astype(jnp.bfloat16)
    pooled = lax.optimization_barrier(jnp.sum(output.astype(jnp.float32), axis=(0, 1))) / float(frames * patches)
    return (output, pooled)

def embed_head(values, gain, weight):
    mapped = jnp.dot(layer_norm(values, gain), weight.astype(jnp.float32), precision=lax.Precision.HIGHEST)
    return unit_rows(mapped)

def pair_losses(video_embed, text_embed, scale, pair_index):
    logits = scale * jnp.dot(video_embed, text_embed.T, precision=lax.Precision.HIGHEST)
    count = logits.shape[0]
    match = pair_index[:, None] == jnp.arange(count, dtype=jnp.int32)[None, :]
    positive = jnp.where(match, logits, jnp.zeros_like(logits))
    video_loss = 0.5 * (jax.nn.logsumexp(logits, axis=1) - lax.optimization_barrier(jnp.sum(positive, axis=1)))
    text_loss = 0.5 * (jax.nn.logsumexp(logits, axis=0) - lax.optimization_barrier(jnp.sum(positive, axis=0)))
    return (video_loss, text_loss)

def reference(video_tokens, text_states, caption_ids, pair_index, logit_scale, gain_spatial, gain_temporal, gain_video, gain_text, w_qkv_spatial, w_out_spatial, w_qkv_temporal, w_out_temporal, w_video, w_text):

    def one_clip(clip):
        return clip_layer(clip, gain_spatial, gain_temporal, w_qkv_spatial, w_out_spatial, w_qkv_temporal, w_out_temporal)
    layer_out, pooled = lax.map(one_clip, video_tokens)
    end_place = jnp.argmax(caption_ids, axis=1).astype(jnp.int32)
    rows_index = jnp.arange(text_states.shape[0], dtype=jnp.int32)
    text_pool = text_states[rows_index, end_place].astype(jnp.float32)
    scale = logit_scale[0]

    def total_loss(pooled_in, text_in):
        video_embed = embed_head(pooled_in, gain_video, w_video)
        text_embed = embed_head(text_in, gain_text, w_text)
        video_loss, text_loss = pair_losses(video_embed, text_embed, scale, pair_index)
        return (jnp.sum(video_loss) + jnp.sum(text_loss), (video_loss, text_loss))
    total, pullback, losses = jax.vjp(total_loss, pooled, text_pool, has_aux=True)
    grad_pooled, grad_text = pullback(jnp.ones_like(total))
    return (layer_out, losses[0], losses[1], grad_pooled, grad_text)
```

```python
import functools

import jax
import jax.numpy as jnp
from jax import lax
from jax.experimental import pallas as pl
from jax.experimental.pallas import tpu as pltpu
from jax.sharding import PartitionSpec as P

HEADS = 8
HD = 64
WIDTH = HEADS * HD
D = 1024
DT = 768
E = 768
NORM_EPS = 1e-05
UNIT_EPS = 1e-06
F32 = jnp.float32
BF16 = jnp.bfloat16
VMEM_LIMIT = 48 * 1024 * 1024

QKV_S = 0
QKV_T = 1536
W_VIDEO = 3072
W_TEXT = 3840
W_OUT = 4608
PACKED = 5632


def dot(a, b):
    return lax.dot_general(a, b, (((1,), (0,)), ((), ())), preferred_element_type=F32)


def dot_t(a, b):
    return lax.dot_general(a, b, (((1,), (1,)), ((), ())), preferred_element_type=F32)


def pieces(a):
    first = a.astype(BF16)
    rest = a - first.astype(F32)
    second = rest.astype(BF16)
    third = (rest - second.astype(F32)).astype(BF16)
    return first, second, third


def exact(dot_fn, a, weight):
    first, second, third = pieces(a)
    return dot_fn(third, weight) + dot_fn(second, weight) + dot_fn(first, weight)


def layer_norm(values, gain):
    center = values - jnp.mean(values, axis=-1, keepdims=True)
    spread = jnp.mean(center * center, axis=-1, keepdims=True)
    return center * lax.rsqrt(spread + NORM_EPS) * gain


def attend(packed_ref, mixed_ref, mask):
    rows = packed_ref.shape[0]
    low = lax.broadcasted_iota(jnp.int32, (rows, 2 * HD), 1) < HD
    for pair in range(HEADS // 2):
        at = pair * 2 * HD
        query = packed_ref[:, at : at + 2 * HD]
        key = packed_ref[:, WIDTH + at : WIDTH + at + 2 * HD]
        value = packed_ref[:, 2 * WIDTH + at : 2 * WIDTH + at + 2 * HD]
        mixed = []
        for lanes in (low, ~low):
            scores = dot_t(jnp.where(lanes, query, jnp.zeros_like(query)), key) * (HD**-0.5)
            if mask is not None:
                scores = jnp.where(mask, scores, -1e30)
            weight = jnp.exp(scores - jnp.max(scores, axis=-1, keepdims=True))
            probs = weight * (1.0 / jnp.sum(weight, axis=-1, keepdims=True))
            mixed.append(dot(probs.astype(BF16), value))
        mixed_ref[:, at : at + 2 * HD] = jnp.where(low, mixed[0], mixed[1]).astype(BF16)


def spatial_kernel(tokens_ref, gain_ref, weights_ref, mixed_ref, qkv, packed, sem):
    copy = pltpu.make_async_copy(weights_ref.at[:, QKV_S : QKV_S + 3 * WIDTH], qkv, sem)
    copy.start()
    normed = layer_norm(tokens_ref[...].astype(F32), gain_ref[...]).astype(BF16)
    copy.wait()
    packed[...] = dot(normed, qkv[...]).astype(BF16)
    attend(packed, mixed_ref, None)


def temporal_kernel(
    mixed_ref, tokens_ref, gain_ref, weights_ref, out_ref, pool_ref, qkv, outs, packed, mixed, sems
):
    copy_out = pltpu.make_async_copy(weights_ref.at[:, W_OUT : W_OUT + D], outs, sems.at[0])
    copy_qkv = pltpu.make_async_copy(
        weights_ref.at[:, QKV_T : QKV_T + 3 * WIDTH], qkv, sems.at[1]
    )
    copy_out.start()
    copy_qkv.start()
    copy_out.wait()
    both = outs[...].astype(F32).reshape(64, 2, 8, D)
    out_spatial = both[:, 0].reshape(WIDTH, D).astype(BF16)
    out_temporal = both[:, 1].reshape(WIDTH, D).astype(BF16)
    spatial = (tokens_ref[...].astype(F32) + dot(mixed_ref[...], out_spatial)).astype(BF16)
    normed = layer_norm(spatial.astype(F32), gain_ref[...]).astype(BF16)
    copy_qkv.wait()
    packed[...] = dot(normed, qkv[...]).astype(BF16)
    rows = packed.shape[0]
    patches = 32
    place = lax.broadcasted_iota(jnp.int32, (rows, rows), 0) % patches
    other = lax.broadcasted_iota(jnp.int32, (rows, rows), 1) % patches
    attend(packed, mixed, place == other)
    output = (spatial.astype(F32) + dot(mixed[...], out_temporal)).astype(BF16)
    out_ref[...] = output
    total = jnp.sum(output.astype(F32), axis=0, keepdims=True)
    for chunk in range(D // 128):
        pool_ref[:, chunk, :] = jnp.broadcast_to(total[:, chunk * 128 : (chunk + 1) * 128], (8, 128))


def spread_kernel(parts_ref, every_ref):
    mine = jnp.sum(parts_ref[...], axis=0) * (1.0 / (8 * 256))
    every_ref[...] = jnp.broadcast_to(mine[None], every_ref.shape)


def text_kernel(gain_ref, weights_ref, pool_ref, mapped_ref, weight_ref, packed, sem):
    copy = pltpu.make_async_copy(weights_ref.at[:, W_TEXT : W_TEXT + E], packed, sem)
    copy.start()
    copy.wait()
    column = lax.broadcasted_iota(jnp.int32, (DT, D), 1)
    place = column % 16
    row = jnp.where(place < 12, (column // 16) * 12 + place, -1)
    pick = (row == lax.broadcasted_iota(jnp.int32, (DT, D), 0)).astype(BF16)
    weight = dot(pick, packed[...]).astype(BF16)
    weight_ref[...] = weight
    column = lax.broadcasted_iota(jnp.int32, (64, D), 1)
    pick = (column == 16 * lax.broadcasted_iota(jnp.int32, (64, D), 0) + 12).astype(BF16)
    pool = dot(pick, packed[...])
    pool_ref[...] = pool
    mapped_ref[...] = exact(dot, layer_norm(pool, gain_ref[...]), weight)


def unit_rows(values):
    return values * lax.rsqrt(jnp.sum(values * values, axis=-1, keepdims=True) + UNIT_EPS)


def unit_back(mapped, grad):
    scale = lax.rsqrt(jnp.sum(mapped * mapped, axis=-1, keepdims=True) + UNIT_EPS)
    along = jnp.sum(mapped * grad, axis=-1, keepdims=True)
    return scale * grad - mapped * (scale * scale * scale * along)


def norm_back(values, gain, grad):
    center = values - jnp.mean(values, axis=-1, keepdims=True)
    scale = lax.rsqrt(jnp.mean(center * center, axis=-1, keepdims=True) + NORM_EPS)
    grad = grad * gain
    unit = center * scale
    along = jnp.mean(grad * unit, axis=-1, keepdims=True)
    return scale * (grad - jnp.mean(grad, axis=-1, keepdims=True) - unit * along)


def loss_kernel(
    place_ref,
    scale_ref,
    pairs_ref,
    pooled_ref,
    text_pool_ref,
    text_mapped_ref,
    text_weight_ref,
    gain_video_ref,
    gain_text_ref,
    weights_ref,
    video_loss_ref,
    text_loss_ref,
    grad_pooled_ref,
    grad_text_ref,
    weight,
    pooled_all,
    sem,
):
    copy = pltpu.make_async_copy(weights_ref.at[:, W_VIDEO : W_VIDEO + E], weight, sem)
    copy.start()
    me = place_ref[0]
    scale = scale_ref[0]
    for chunk in range(D // 128):
        pooled_all[:, chunk * 128 : (chunk + 1) * 128] = pooled_ref[:, chunk, :]
    gain = gain_video_ref[...]
    normed = layer_norm(pooled_all[...], gain)
    copy.wait()
    mapped = exact(dot, normed, weight[...])
    video = unit_rows(mapped)
    text_mapped = text_mapped_ref[...]
    text = unit_rows(text_mapped)
    logits = scale * lax.dot_general(
        video, text, (((1,), (1,)), ((), ())), precision=lax.Precision.HIGHEST,
        preferred_element_type=F32,
    )
    count = logits.shape[0]
    rows = lax.broadcasted_iota(jnp.int32, (count, count), 0)
    columns = lax.broadcasted_iota(jnp.int32, (count, count), 1)
    match = pairs_ref[...] == columns
    row_top = jnp.max(logits, axis=1, keepdims=True)
    row_exp = jnp.exp(logits - row_top)
    row_sum = jnp.sum(row_exp, axis=1, keepdims=True)
    col_top = jnp.max(logits, axis=0, keepdims=True)
    col_exp = jnp.exp(logits - col_top)
    col_sum = jnp.sum(col_exp, axis=0, keepdims=True)
    positive = jnp.where(match, logits, 0.0)
    video_loss = 0.5 * (row_top + jnp.log(row_sum) - jnp.sum(positive, axis=1, keepdims=True))
    text_loss = 0.5 * (col_top + jnp.log(col_sum) - jnp.sum(positive, axis=0, keepdims=True))
    mine_row = lax.broadcasted_iota(jnp.int32, (count, 1), 0) == me
    mine_col = lax.broadcasted_iota(jnp.int32, (1, count), 1) == me
    video_loss_ref[0] = jnp.sum(jnp.where(mine_row, video_loss, 0.0))
    text_loss_ref[0] = jnp.sum(jnp.where(mine_col, text_loss, 0.0))
    slope = (0.5 * scale) * (row_exp / row_sum + col_exp / col_sum - 2.0 * match.astype(F32))
    row_slope = jnp.sum(jnp.where(rows == me, slope, 0.0), axis=0, keepdims=True)
    row_slope = jnp.sum(jnp.where(rows == columns, row_slope, 0.0), axis=1, keepdims=True)
    col_slope = jnp.sum(jnp.where(columns == me, slope, 0.0), axis=1, keepdims=True)
    grad_video = jnp.sum(row_slope * text, axis=0, keepdims=True)
    grad_caption = jnp.sum(col_slope * video, axis=0, keepdims=True)
    mine_mapped = jnp.sum(jnp.where(mine_row, mapped, 0.0), axis=0, keepdims=True)
    mine_text_mapped = jnp.sum(jnp.where(mine_row, text_mapped, 0.0), axis=0, keepdims=True)
    mine_pooled = jnp.sum(jnp.where(mine_row, pooled_all[...], 0.0), axis=0, keepdims=True)
    mine_text_pool = jnp.sum(jnp.where(mine_row, text_pool_ref[...], 0.0), axis=0, keepdims=True)
    back = exact(dot_t, unit_back(mine_mapped, grad_video), weight[...])
    grad_pooled_ref[...] = norm_back(mine_pooled, gain, back)
    back = exact(dot_t, unit_back(mine_text_mapped, grad_caption), text_weight_ref[...])
    grad_text_ref[...] = norm_back(mine_text_pool, gain_text_ref[...], back)


def call(kernel, out_shape, in_spaces, scratch, out_spaces=None, cost=(0, 0)):
    many = isinstance(out_shape, (tuple, list))
    out_spaces = out_spaces or ([pltpu.VMEM] * (len(out_shape) if many else 1))
    out_specs = [pl.BlockSpec(memory_space=space) for space in out_spaces]
    return pl.pallas_call(
        kernel,
        out_shape=out_shape,
        in_specs=[pl.BlockSpec(memory_space=space) for space in in_spaces],
        out_specs=out_specs if many else out_specs[0],
        scratch_shapes=scratch,
        compiler_params=pltpu.CompilerParams(vmem_limit_bytes=VMEM_LIMIT),
        cost_estimate=pl.CostEstimate(flops=cost[0], bytes_accessed=cost[1], transcendentals=0),
    )


def shape(dims, dtype):
    return jax.ShapeDtypeStruct(dims, dtype)


def on_device(
    video_tokens,
    text_states,
    caption_ids,
    pair_index,
    logit_scale,
    gain_spatial,
    gain_temporal,
    gain_video,
    gain_text,
    w_qkv_spatial,
    w_out_spatial,
    w_qkv_temporal,
    w_out_temporal,
    w_video,
    w_text,
):
    V, S, A = pltpu.VMEM, pltpu.SMEM, pl.ANY
    DMA = pltpu.SemaphoreType.DMA
    tokens = video_tokens.reshape(256, D)
    end_place = jnp.argmax(caption_ids[0])
    text_row = lax.dynamic_slice_in_dim(text_states[0], end_place, 1, 0)
    text_part = jnp.concatenate([w_text, text_row, jnp.zeros((3, E), BF16)], axis=0)
    outs = jnp.concatenate([w_out_spatial, w_out_temporal], axis=0)
    mine = jnp.concatenate([w_qkv_spatial, w_qkv_temporal, w_video, text_part, outs], axis=1)
    weights = lax.all_gather(mine, "dp", axis=0, tiled=True)
    by_patch = lax.all_to_all(tokens.reshape(8, 32, D), "frame", 0, 0, tiled=True)

    mixed = call(
        spatial_kernel,
        shape((256, WIDTH), BF16),
        (V, V, A),
        [pltpu.VMEM((D, 3 * WIDTH), BF16), pltpu.VMEM((256, 3 * WIDTH), BF16), DMA],
    )(tokens, gain_spatial.reshape(1, D), weights)
    mixed = lax.all_to_all(mixed.reshape(8, 32, WIDTH), "frame", 0, 0, tiled=True)
    layer_out, pool = call(
        temporal_kernel,
        (shape((256, D), BF16), shape((8, 8, 128), F32)),
        (V, V, V, A),
        [
            pltpu.VMEM((D, 3 * WIDTH), BF16),
            pltpu.VMEM((D, D), BF16),
            pltpu.VMEM((256, 3 * WIDTH), BF16),
            pltpu.VMEM((256, WIDTH), BF16),
            DMA((2,)),
        ],
    )(mixed.reshape(256, WIDTH), by_patch.reshape(256, D), gain_temporal.reshape(1, D), weights)
    text_pool, text_mapped, text_weight = call(
        text_kernel,
        (shape((64, DT), F32), shape((64, E), F32), shape((DT, E), BF16)),
        (V, A),
        [pltpu.VMEM((D, E), BF16), DMA],
    )(gain_text.reshape(1, DT), weights)
    pool = lax.all_to_all(pool, "frame", 0, 0, tiled=True)
    pool = call(spread_kernel, shape((64, 8, 128), F32), (V,), [])(pool)
    pooled = lax.all_to_all(pool, "dp", 0, 0, tiled=True)
    place = lax.axis_index("dp").astype(jnp.int32).reshape(1)
    video_loss, text_loss, grad_pooled, grad_text = call(
        loss_kernel,
        (shape((1,), F32), shape((1,), F32), shape((1, D), F32), shape((1, DT), F32)),
        (S, S, V, V, V, V, V, V, V, A),
        [pltpu.VMEM((D, E), BF16), pltpu.VMEM((64, D), F32), DMA],
        (S, S, V, V),
    )(
        place,
        logit_scale,
        pair_index.reshape(64, 1),
        pooled,
        text_pool,
        text_mapped,
        text_weight,
        gain_video.reshape(1, D),
        gain_text.reshape(1, DT),
        weights,
    )
    return (layer_out.reshape(1, 8, 32, D), video_loss, text_loss, grad_pooled, grad_text)


def solution(mesh):
    placed = (
        P("dp", "frame", None, None),
        P("dp", None, None),
        P("dp", None),
        P(),
        P(),
        P(),
        P(),
        P(),
        P(),
        P("dp", None),
        P("dp", None),
        P("dp", None),
        P("dp", None),
        P("dp", None),
        P("dp", None),
    )
    return jax.shard_map(
        on_device,
        mesh=mesh,
        in_specs=placed,
        out_specs=(P("dp", None, "frame", None), P("dp"), P("dp"), P("dp", None), P("dp", None)),
        check_vma=False,
    )
```

```python
import functools

import jax
import jax.numpy as jnp
from jax import lax
from jax.experimental import pallas as pl
from jax.experimental.pallas import tpu as pltpu
from jax.sharding import PartitionSpec as P

HEADS = 8
HD = 64
WIDTH = HEADS * HD
D = 1024
DT = 768
E = 768
NORM_EPS = 1e-05
UNIT_EPS = 1e-06
F32 = jnp.float32
BF16 = jnp.bfloat16
VMEM_LIMIT = 48 * 1024 * 1024

QKV_T = 0
W_TEXT = 1536
W_OUT = 2304
W_VIDEO = 3328
PACKED = 4096

X, Y = 4, 8
ROWS_OF_X = [[(x * Y + y) * 2 + c for x in range(X)] for y in range(Y) for c in range(2)]
ROWS_OF_Y = [[(x * Y + y) * 2 + c for y in range(Y)] for x in range(X) for c in range(2)]
ROWS_OF_YC = [[(x * Y + y) * 2 + c for y in range(Y) for c in range(2)] for x in range(X)]
CHIPS_OF_CORE = [[i * 2 + c for i in range(X * Y)] for c in range(2)]
OTHER_CORE = [(i, i ^ 1) for i in range(2 * X * Y)]
FRAMES = 8
CORES_AND_FRAMES = [
    [(2 * i + c) * FRAMES + f for c in range(2) for f in range(FRAMES)] for i in range(X * Y)
]


def dot(a, b):
    return lax.dot_general(a, b, (((1,), (0,)), ((), ())), preferred_element_type=F32)


def dot_t(a, b):
    return lax.dot_general(a, b, (((1,), (1,)), ((), ())), preferred_element_type=F32)


def pieces(a):
    first = a.astype(BF16)
    rest = a - first.astype(F32)
    second = rest.astype(BF16)
    third = (rest - second.astype(F32)).astype(BF16)
    return first, second, third


def exact(dot_fn, a, weight):
    first, second, third = pieces(a)
    return dot_fn(third, weight) + dot_fn(second, weight) + dot_fn(first, weight)


def layer_norm(values, gain):
    center = values - jnp.mean(values, axis=-1, keepdims=True)
    spread = jnp.mean(center * center, axis=-1, keepdims=True)
    return center * lax.rsqrt(spread + NORM_EPS) * gain


def attend(packed_ref, mixed_ref, mask):
    rows = packed_ref.shape[0]
    low = lax.broadcasted_iota(jnp.int32, (rows, 2 * HD), 1) < HD
    for pair in range(HEADS // 2):
        at = pair * 2 * HD
        query = packed_ref[:, at : at + 2 * HD]
        key = packed_ref[:, WIDTH + at : WIDTH + at + 2 * HD]
        value = packed_ref[:, 2 * WIDTH + at : 2 * WIDTH + at + 2 * HD]
        mixed = []
        for lanes in (low, ~low):
            scores = dot_t(jnp.where(lanes, query, jnp.zeros_like(query)), key) * (HD**-0.5)
            if mask is not None:
                scores = jnp.where(mask, scores, -1e30)
            weight = jnp.exp(scores - jnp.max(scores, axis=-1, keepdims=True))
            probs = weight * (1.0 / jnp.sum(weight, axis=-1, keepdims=True))
            mixed.append(dot(probs.astype(BF16), value))
        mixed_ref[:, at : at + 2 * HD] = jnp.where(low, mixed[0], mixed[1]).astype(BF16)


def spatial_kernel(core_ref, tokens_ref, gain_ref, own_ref, other_ref, mixed_ref, qkv, packed, sems):
    core = core_ref[0]
    copy_own = pltpu.make_async_copy(own_ref, qkv.at[:, core], sems.at[0])
    copy_other = pltpu.make_async_copy(other_ref, qkv.at[:, 1 - core], sems.at[1])
    copy_own.start()
    copy_other.start()
    normed = layer_norm(tokens_ref[...].astype(F32), gain_ref[...]).astype(BF16)
    copy_own.wait()
    copy_other.wait()
    packed[...] = dot(normed, qkv[...].reshape(D, 3 * WIDTH)).astype(BF16)
    attend(packed, mixed_ref, None)
    mixed_ref[:, WIDTH:] = tokens_ref[...]


def gather_rows(weights_ref, first, target, sems):
    width = target.shape[-1]
    return [
        pltpu.make_async_copy(
            weights_ref.at[y, c, :, :, first : first + width], target.at[:, y, c], sems.at[2 * y + c]
        )
        for y in range(Y)
        for c in range(2)
    ]


def pack_kernel(ids_ref, states_ref, qkv_ref, text_ref, out_s_ref, out_t_ref, video_ref, packed_ref):
    ids = ids_ref[...]
    positions = lax.broadcasted_iota(jnp.int32, ids.shape, 1)
    end_place = jnp.min(jnp.where(ids == jnp.max(ids), positions, ids.shape[1]))
    states = states_ref[...].astype(F32)
    rows = lax.broadcasted_iota(jnp.int32, states.shape, 0)
    text_row = jnp.sum(jnp.where(rows == end_place, states, 0.0), axis=0, keepdims=True)
    text = jnp.concatenate([text_ref[...].astype(F32), jnp.zeros((4, E), F32)], axis=0)
    place = lax.broadcasted_iota(jnp.int32, text.shape, 0)
    text = jnp.where(place < 12, text, jnp.where(place == 12, text_row, 0.0))
    packed_ref[:, QKV_T : QKV_T + 3 * WIDTH] = qkv_ref[...]
    packed_ref[:, W_TEXT : W_TEXT + E] = text.astype(BF16)
    outs = jnp.concatenate([out_s_ref[...].astype(F32), out_t_ref[...].astype(F32)], axis=0)
    packed_ref[:, W_OUT : W_OUT + D] = outs.astype(BF16)
    packed_ref[:, W_VIDEO : W_VIDEO + E] = video_ref[...]


def temporal_kernel(
    arrived_ref, gain_ref, weights_ref, out_ref, pool_ref, qkv, outs, packed, mixed, sems
):
    copies_out = gather_rows(weights_ref, W_OUT, outs, sems.at[0])
    copies_qkv = gather_rows(weights_ref, QKV_T, qkv, sems.at[1])
    for copy in copies_out + copies_qkv:
        copy.start()
    for copy in copies_out:
        copy.wait()
    both = outs[...].astype(F32).reshape(64, 2, 8, D)
    out_spatial = both[:, 0].reshape(WIDTH, D).astype(BF16)
    out_temporal = both[:, 1].reshape(WIDTH, D).astype(BF16)
    spatial = arrived_ref[:, WIDTH:].astype(F32) + dot(arrived_ref[:, :WIDTH], out_spatial)
    spatial = spatial.astype(BF16)
    normed = layer_norm(spatial.astype(F32), gain_ref[...]).astype(BF16)
    for copy in copies_qkv:
        copy.wait()
    packed[...] = dot(normed, qkv[...].reshape(D, 3 * WIDTH)).astype(BF16)
    rows = packed.shape[0]
    patches = 32
    place = lax.broadcasted_iota(jnp.int32, (rows, rows), 0) % patches
    other = lax.broadcasted_iota(jnp.int32, (rows, rows), 1) % patches
    attend(packed, mixed, place == other)
    output = (spatial.astype(F32) + dot(mixed[...], out_temporal)).astype(BF16)
    out_ref[...] = output
    total = jnp.sum(output.astype(F32), axis=0, keepdims=True)
    for chunk in range(D // 128):
        pool_ref[:, chunk, :] = jnp.broadcast_to(
            total[:, chunk * 128 : (chunk + 1) * 128], (2 * FRAMES, 128)
        )


def spread_kernel(parts_ref, every_ref):
    for c in range(2):
        total = jnp.sum(parts_ref[c * FRAMES : (c + 1) * FRAMES], axis=0) * (1.0 / (8 * 256))
        every_ref[:, c] = jnp.broadcast_to(total[None], (X * Y,) + total.shape)


def text_kernel(
    gain_ref, weights_ref, pool_ref, mapped_ref, weight_ref, gathered, sems
):
    copies = gather_rows(weights_ref, W_TEXT, gathered, sems)
    for copy in copies:
        copy.start()
    for copy in copies:
        copy.wait()
    packed = gathered[...].reshape(D, E)
    column = lax.broadcasted_iota(jnp.int32, (DT, D), 1)
    place = column % 16
    row = jnp.where(place < 12, (column // 16) * 12 + place, -1)
    pick = (row == lax.broadcasted_iota(jnp.int32, (DT, D), 0)).astype(BF16)
    weight = dot(pick, packed).astype(BF16)
    weight_ref[...] = weight
    column = lax.broadcasted_iota(jnp.int32, (64, D), 1)
    pick = (column == 16 * lax.broadcasted_iota(jnp.int32, (64, D), 0) + 12).astype(BF16)
    pool = dot(pick, packed)
    pool_ref[...] = pool
    mapped_ref[...] = exact(dot, layer_norm(pool, gain_ref[...]), weight)


def unit_rows(values):
    return values * lax.rsqrt(jnp.sum(values * values, axis=-1, keepdims=True) + UNIT_EPS)


def unit_back(mapped, grad):
    scale = lax.rsqrt(jnp.sum(mapped * mapped, axis=-1, keepdims=True) + UNIT_EPS)
    along = jnp.sum(mapped * grad, axis=-1, keepdims=True)
    return scale * grad - mapped * (scale * scale * scale * along)


def norm_back(values, gain, grad):
    center = values - jnp.mean(values, axis=-1, keepdims=True)
    scale = lax.rsqrt(jnp.mean(center * center, axis=-1, keepdims=True) + NORM_EPS)
    grad = grad * gain
    unit = center * scale
    along = jnp.mean(grad * unit, axis=-1, keepdims=True)
    return scale * (grad - jnp.mean(grad, axis=-1, keepdims=True) - unit * along)


def loss_kernel(
    place_ref,
    scale_ref,
    pairs_ref,
    pooled_ref,
    text_pool_ref,
    text_mapped_ref,
    text_weight_ref,
    gain_video_ref,
    gain_text_ref,
    weights_ref,
    video_loss_ref,
    text_loss_ref,
    grad_pooled_ref,
    grad_text_ref,
    gathered,
    pooled_all,
    sems,
):
    me = place_ref[0]
    copies = gather_rows(weights_ref, W_VIDEO, gathered, sems)
    for copy in copies:
        copy.start()
    scale = scale_ref[0]
    for chunk in range(D // 128):
        pooled_all[:, chunk * 128 : (chunk + 1) * 128] = pooled_ref[:, chunk, :]
    gain = gain_video_ref[...]
    normed = layer_norm(pooled_all[...], gain)
    for copy in copies:
        copy.wait()
    weight = gathered[...].reshape(D, E)
    mapped = exact(dot, normed, weight)
    video = unit_rows(mapped)
    text_mapped = text_mapped_ref[...]
    text = unit_rows(text_mapped)
    logits = scale * lax.dot_general(
        video, text, (((1,), (1,)), ((), ())), precision=lax.Precision.HIGHEST,
        preferred_element_type=F32,
    )
    count = logits.shape[0]
    rows = lax.broadcasted_iota(jnp.int32, (count, count), 0)
    columns = lax.broadcasted_iota(jnp.int32, (count, count), 1)
    match = pairs_ref[...] == columns
    row_top = jnp.max(logits, axis=1, keepdims=True)
    row_exp = jnp.exp(logits - row_top)
    row_sum = jnp.sum(row_exp, axis=1, keepdims=True)
    col_top = jnp.max(logits, axis=0, keepdims=True)
    col_exp = jnp.exp(logits - col_top)
    col_sum = jnp.sum(col_exp, axis=0, keepdims=True)
    positive = jnp.where(match, logits, 0.0)
    video_loss = 0.5 * (row_top + jnp.log(row_sum) - jnp.sum(positive, axis=1, keepdims=True))
    text_loss = 0.5 * (col_top + jnp.log(col_sum) - jnp.sum(positive, axis=0, keepdims=True))
    mine_row = lax.broadcasted_iota(jnp.int32, (count, 1), 0) == me
    mine_col = lax.broadcasted_iota(jnp.int32, (1, count), 1) == me
    video_loss_ref[0] = jnp.sum(jnp.where(mine_row, video_loss, 0.0))
    text_loss_ref[0] = jnp.sum(jnp.where(mine_col, text_loss, 0.0))
    slope = (0.5 * scale) * (row_exp / row_sum + col_exp / col_sum - 2.0 * match.astype(F32))
    row_slope = jnp.sum(jnp.where(rows == me, slope, 0.0), axis=0, keepdims=True)
    row_slope = jnp.sum(jnp.where(rows == columns, row_slope, 0.0), axis=1, keepdims=True)
    col_slope = jnp.sum(jnp.where(columns == me, slope, 0.0), axis=1, keepdims=True)
    grad_video = jnp.sum(row_slope * text, axis=0, keepdims=True)
    grad_caption = jnp.sum(col_slope * video, axis=0, keepdims=True)
    mine_mapped = jnp.sum(jnp.where(mine_row, mapped, 0.0), axis=0, keepdims=True)
    mine_text_mapped = jnp.sum(jnp.where(mine_row, text_mapped, 0.0), axis=0, keepdims=True)
    mine_pooled = jnp.sum(jnp.where(mine_row, pooled_all[...], 0.0), axis=0, keepdims=True)
    mine_text_pool = jnp.sum(jnp.where(mine_row, text_pool_ref[...], 0.0), axis=0, keepdims=True)
    back = exact(dot_t, unit_back(mine_mapped, grad_video), weight)
    grad_pooled_ref[...] = norm_back(mine_pooled, gain, back)
    back = exact(dot_t, unit_back(mine_text_mapped, grad_caption), text_weight_ref[...])
    grad_text_ref[...] = norm_back(mine_text_pool, gain_text_ref[...], back)


def call(kernel, out_shape, in_spaces, scratch, out_spaces=None, cost=(0, 0)):
    many = isinstance(out_shape, (tuple, list))
    out_spaces = out_spaces or ([pltpu.VMEM] * (len(out_shape) if many else 1))
    out_specs = [pl.BlockSpec(memory_space=space) for space in out_spaces]
    return pl.pallas_call(
        kernel,
        out_shape=out_shape,
        in_specs=[pl.BlockSpec(memory_space=space) for space in in_spaces],
        out_specs=out_specs if many else out_specs[0],
        scratch_shapes=scratch,
        compiler_params=pltpu.CompilerParams(vmem_limit_bytes=VMEM_LIMIT),
        cost_estimate=pl.CostEstimate(flops=cost[0], bytes_accessed=cost[1], transcendentals=0),
    )


def shape(dims, dtype):
    return jax.ShapeDtypeStruct(dims, dtype)


def send_all(block, groups):
    copies = jnp.broadcast_to(block[None], (len(groups[0]),) + block.shape)
    return lax.all_to_all(copies, "dp", 0, 0, tiled=True, axis_index_groups=groups)


def on_device(
    video_tokens,
    text_states,
    caption_ids,
    pair_index,
    logit_scale,
    gain_spatial,
    gain_temporal,
    gain_video,
    gain_text,
    w_qkv_spatial,
    w_out_spatial,
    w_qkv_temporal,
    w_out_temporal,
    w_video,
    w_text,
):
    V, S, A = pltpu.VMEM, pltpu.SMEM, pl.ANY
    DMA = pltpu.SemaphoreType.DMA
    halves = (X, Y, 2, 16)
    tokens = video_tokens.reshape(256, D)
    place = lax.axis_index("dp").astype(jnp.int32).reshape(1)
    core = place % 2
    packed = call(pack_kernel, shape((16, PACKED), BF16), (V,) * 7, [])(
        caption_ids,
        text_states.reshape(text_states.shape[1:]),
        w_qkv_temporal,
        w_text,
        w_out_spatial,
        w_out_temporal,
        w_video,
    )
    own = send_all(w_qkv_spatial, ROWS_OF_Y)
    packed = lax.all_gather(packed, "dp", axis=0, tiled=True, axis_index_groups=ROWS_OF_X)
    own, packed = lax.optimization_barrier((own, packed))
    weights = lax.all_gather(packed, "dp", axis=0, tiled=True, axis_index_groups=ROWS_OF_YC)
    weights = weights.reshape(Y, 2, X, 16, PACKED)
    own = send_all(own.reshape(Y * 16, 3 * WIDTH), ROWS_OF_X).reshape(X * Y, 16, 3 * WIDTH)
    other = lax.ppermute(own, "dp", OTHER_CORE)

    mixed = call(
        spatial_kernel,
        shape((256, WIDTH + D), BF16),
        (S, V, V, A, A),
        [pltpu.VMEM((X * Y, 2, 16, 3 * WIDTH), BF16), pltpu.VMEM((256, 3 * WIDTH), BF16), DMA((2,))],
    )(core, tokens, gain_spatial.reshape(1, D), own, other)
    mixed = lax.all_to_all(mixed.reshape(8, 32, WIDTH + D), "frame", 0, 0, tiled=True)
    layer_out, pool = call(
        temporal_kernel,
        (shape((256, D), BF16), shape((2 * FRAMES, 8, 128), F32)),
        (V, V, A),
        [
            pltpu.VMEM(halves + (3 * WIDTH,), BF16),
            pltpu.VMEM(halves + (D,), BF16),
            pltpu.VMEM((256, 3 * WIDTH), BF16),
            pltpu.VMEM((256, WIDTH), BF16),
            DMA((2, 2 * Y)),
        ],
    )(mixed.reshape(256, WIDTH + D), gain_temporal.reshape(1, D), weights)
    text_pool, text_mapped, text_weight = call(
        text_kernel,
        (shape((64, DT), F32), shape((64, E), F32), shape((DT, E), BF16)),
        (V, A),
        [pltpu.VMEM(halves + (E,), BF16), DMA((2 * Y,))],
    )(gain_text.reshape(1, DT), weights)
    pool = lax.all_to_all(
        pool, ("dp", "frame"), 0, 0, tiled=True, axis_index_groups=CORES_AND_FRAMES
    )
    pool = call(spread_kernel, shape((X * Y, 2, 8, 128), F32), (V,), [])(pool)
    pooled = lax.all_to_all(pool, "dp", 0, 0, tiled=True, axis_index_groups=CHIPS_OF_CORE)
    video_loss, text_loss, grad_pooled, grad_text = call(
        loss_kernel,
        (shape((1,), F32), shape((1,), F32), shape((1, D), F32), shape((1, DT), F32)),
        (S, S, V, V, V, V, V, V, V, A),
        [pltpu.VMEM(halves + (E,), BF16), pltpu.VMEM((64, D), F32), DMA((2 * Y,))],
        (S, S, V, V),
    )(
        place,
        logit_scale,
        pair_index.reshape(64, 1),
        pooled.reshape(64, 8, 128),
        text_pool,
        text_mapped,
        text_weight,
        gain_video.reshape(1, D),
        gain_text.reshape(1, DT),
        weights,
    )
    return (layer_out.reshape(1, 8, 32, D), video_loss, text_loss, grad_pooled, grad_text)


def solution(mesh):
    placed = (
        P("dp", "frame", None, None),
        P("dp", None, None),
        P("dp", None),
        P(),
        P(),
        P(),
        P(),
        P(),
        P(),
        P("dp", None),
        P("dp", None),
        P("dp", None),
        P("dp", None),
        P("dp", None),
        P("dp", None),
    )
    return jax.shard_map(
        on_device,
        mesh=mesh,
        in_specs=placed,
        out_specs=(P("dp", None, "frame", None), P("dp"), P("dp"), P("dp", None), P("dp", None)),
        check_vma=False,
    )
```

```python
import functools

import jax
import jax.numpy as jnp
from jax import lax
from jax.experimental import pallas as pl
from jax.experimental.pallas import tpu as pltpu
from jax.sharding import PartitionSpec as P

HEADS = 8
HD = 64
WIDTH = HEADS * HD
D = 1024
DT = 768
E = 768
NORM_EPS = 1e-05
UNIT_EPS = 1e-06
F32 = jnp.float32
BF16 = jnp.bfloat16
MIB = 1024 * 1024
VMEM_LIMIT = 48 * MIB
VMEM_WHOLE = 63 * MIB
VMEM_MOST = 52 * MIB

QKV_T = 0
W_TEXT = 1536
W_OUT = 2304
W_VIDEO = 3328
PACKED = 4096

X, Y = 4, 8
ROWS_OF_X = [[(x * Y + y) * 2 + c for x in range(X)] for y in range(Y) for c in range(2)]
ROWS_OF_Y = [[(x * Y + y) * 2 + c for y in range(Y)] for x in range(X) for c in range(2)]
ROWS_OF_YC = [[(x * Y + y) * 2 + c for y in range(Y) for c in range(2)] for x in range(X)]
OTHER_CORE = [(i, i ^ 1) for i in range(2 * X * Y)]
FRAMES = 8


def dot(a, b):
    return lax.dot_general(a, b, (((1,), (0,)), ((), ())), preferred_element_type=F32)


def dot_t(a, b):
    return lax.dot_general(a, b, (((1,), (1,)), ((), ())), preferred_element_type=F32)


def pieces(a):
    first = a.astype(BF16)
    rest = a - first.astype(F32)
    second = rest.astype(BF16)
    third = (rest - second.astype(F32)).astype(BF16)
    return first, second, third


def exact(dot_fn, a, weight):
    rows = a.shape[0]
    parts = dot_fn(jnp.concatenate(pieces(a), axis=0), weight)
    return parts[2 * rows :] + parts[rows : 2 * rows] + parts[:rows]


def exact_row(dot_fn, a, weight):
    rows = lax.broadcasted_iota(jnp.int32, (16, a.shape[1]), 0)
    first, second, third = (piece.astype(F32) for piece in pieces(a))
    block = jnp.where(rows == 0, third, jnp.where(rows == 1, second, jnp.where(rows == 2, first, 0.0)))
    return jnp.sum(dot_fn(block.astype(BF16), weight), axis=0, keepdims=True)


def layer_norm(values, gain):
    center = values - jnp.mean(values, axis=-1, keepdims=True)
    spread = jnp.mean(center * center, axis=-1, keepdims=True)
    return center * lax.rsqrt(spread + NORM_EPS) * gain


def attend_pair(query, key, value, mask):
    low = lax.broadcasted_iota(jnp.int32, query.shape, 1) < HD
    mixed = []
    for lanes in (low, ~low):
        scores = dot_t(jnp.where(lanes, query, jnp.zeros_like(query)), key) * (HD**-0.5)
        if mask is not None:
            scores = jnp.where(mask, scores, -1e30)
        weight = jnp.exp(scores - jnp.max(scores, axis=-1, keepdims=True))
        probs = weight * (1.0 / jnp.sum(weight, axis=-1, keepdims=True))
        mixed.append(dot(probs.astype(BF16), value))
    return jnp.where(low, mixed[0], mixed[1]).astype(BF16)


def attend(packed_ref, mixed_ref):
    for at in range(0, WIDTH, 2 * HD):
        query, key, value = (
            packed_ref[:, part * WIDTH + at : part * WIDTH + at + 2 * HD] for part in range(3)
        )
        mixed_ref[:, at : at + 2 * HD] = attend_pair(query, key, value, None)


def attend_frames(packed_ref, mixed_ref):
    frames, patches, _ = packed_ref.shape
    block = 16
    rows = frames * block
    place = lax.broadcasted_iota(jnp.int32, (rows, rows), 0) % block
    mask = place == lax.broadcasted_iota(jnp.int32, (rows, rows), 1) % block
    for first in range(0, patches, block):
        for at in range(0, WIDTH, 2 * HD):
            query, key, value = (
                packed_ref[
                    :, first : first + block, part * WIDTH + at : part * WIDTH + at + 2 * HD
                ].reshape(rows, 2 * HD)
                for part in range(3)
            )
            mixed = attend_pair(query, key, value, mask)
            mixed_ref[:, first : first + block, at : at + 2 * HD] = mixed.reshape(
                frames, block, 2 * HD
            )


def spatial_kernel(
    core_ref, tokens_ref, gain_ref, own_ref, other_ref, mixed_ref, tokens, qkv, packed, sems
):
    core = core_ref[0]
    copy_tokens = pltpu.make_async_copy(tokens_ref, tokens, sems.at[2])
    copy_own = pltpu.make_async_copy(own_ref, qkv.at[:, core], sems.at[0])
    copy_other = pltpu.make_async_copy(other_ref, qkv.at[:, 1 - core], sems.at[1])
    copy_tokens.start()
    copy_own.start()
    copy_other.start()
    copy_tokens.wait()
    normed = layer_norm(tokens[...].astype(F32), gain_ref[...]).astype(BF16)
    copy_own.wait()
    copy_other.wait()
    packed[...] = dot(normed, qkv[...].reshape(D, 3 * WIDTH)).astype(BF16)
    attend(packed, mixed_ref)


def gather_rows(weights_ref, first, target, sems):
    width = target.shape[-1]
    return [
        pltpu.make_async_copy(
            weights_ref.at[y, c, :, :, first : first + width], target.at[:, y, c], sems.at[2 * y + c]
        )
        for y in range(Y)
        for c in range(2)
    ]


def pack_kernel(
    ids_ref, states_ref, qkv_ref, text_ref, out_s_ref, out_t_ref, video_ref, packed_ref,
    ids_here, states_here, text_here, out_s_here, out_t_here, sems,
):
    pairs = (
        (ids_ref, ids_here),
        (states_ref, states_here),
        (text_ref, text_here),
        (out_s_ref, out_s_here),
        (out_t_ref, out_t_here),
        (qkv_ref, packed_ref.at[:, QKV_T : QKV_T + 3 * WIDTH]),
        (video_ref, packed_ref.at[:, W_VIDEO : W_VIDEO + E]),
    )
    copies = [pltpu.make_async_copy(*pair, sems.at[i]) for i, pair in enumerate(pairs)]
    for copy in copies:
        copy.start()
    for copy in copies:
        copy.wait()
    ids = ids_here[...]
    positions = lax.broadcasted_iota(jnp.int32, ids.shape, 1)
    end_place = jnp.min(jnp.where(ids == jnp.max(ids), positions, ids.shape[1]))
    states = states_here[...].astype(F32)
    rows = lax.broadcasted_iota(jnp.int32, states.shape, 0)
    text_row = jnp.sum(jnp.where(rows == end_place, states, 0.0), axis=0, keepdims=True)
    text = jnp.concatenate([text_here[...].astype(F32), jnp.zeros((4, E), F32)], axis=0)
    place = lax.broadcasted_iota(jnp.int32, text.shape, 0)
    text = jnp.where(place < 12, text, jnp.where(place == 12, text_row, 0.0))
    packed_ref[:, W_TEXT : W_TEXT + E] = text.astype(BF16)
    outs = jnp.concatenate([out_s_here[...].astype(F32), out_t_here[...].astype(F32)], axis=0)
    packed_ref[:, W_OUT : W_OUT + D] = outs.astype(BF16)


def deal_kernel(frame_ref, tokens_ref, *rest):
    dealt, sems = rest[:-1], rest[-1]
    copies = [
        pltpu.make_async_copy(
            tokens_ref.at[(frame_ref[0] + step) % FRAMES], dealt[step - 1], sems.at[step - 1]
        )
        for step in range(1, FRAMES)
    ]
    for copy in copies:
        copy.start()
    for copy in copies:
        copy.wait()


def temporal_kernel(frame_ref, mixed_ref, gain_ref, weights_ref, tokens_ref, *rest):
    dealt, rest = rest[: FRAMES - 1], rest[FRAMES - 1 :]
    out_ref, pool_ref, tokens, qkv, outs, packed, mixed, sems = rest
    frame = frame_ref[0]
    copies_tokens = [pltpu.make_async_copy(tokens_ref.at[frame], tokens.at[frame], sems.at[2, 0])]
    for step in range(1, FRAMES):
        source = (frame + FRAMES - step) % FRAMES
        copies_tokens.append(
            pltpu.make_async_copy(dealt[step - 1], tokens.at[source], sems.at[2, step])
        )
    copies_out = gather_rows(weights_ref, W_OUT, outs, sems.at[0])
    copies_qkv = gather_rows(weights_ref, QKV_T, qkv, sems.at[1])
    for copy in copies_out + copies_tokens + copies_qkv:
        copy.start()
    for copy in copies_out:
        copy.wait()
    both = outs[...].astype(F32).reshape(64, 2, 8, D)
    out_spatial = both[:, 0].reshape(WIDTH, D).astype(BF16)
    out_temporal = both[:, 1].reshape(WIDTH, D).astype(BF16)
    for copy in copies_tokens:
        copy.wait()
    rows = tokens.shape[0] * tokens.shape[1]
    spatial = tokens[...].reshape(rows, D).astype(F32) + dot(mixed_ref[...], out_spatial)
    spatial = spatial.astype(BF16)
    normed = layer_norm(spatial.astype(F32), gain_ref[...]).astype(BF16)
    for copy in copies_qkv:
        copy.wait()
    projected = dot(normed, qkv[...].reshape(D, 3 * WIDTH)).astype(BF16)
    packed[...] = projected.reshape(packed.shape)
    attend_frames(packed, mixed)
    output = spatial.astype(F32) + dot(mixed[...].reshape(rows, WIDTH), out_temporal)
    output = output.astype(BF16)
    out_ref[...] = output
    total = jnp.sum(output.astype(F32), axis=0, keepdims=True)
    for chunk in range(D // 128):
        pool_ref[:, chunk, :] = jnp.broadcast_to(
            total[:, chunk * 128 : (chunk + 1) * 128], (FRAMES, 128)
        )


def spread_kernel(parts_ref, every_ref):
    mine = jnp.sum(parts_ref[...], axis=0) * (1.0 / (8 * 256))
    every_ref[...] = jnp.broadcast_to(mine[None], every_ref.shape)


def text_kernel(
    gain_ref, weights_ref, pool_ref, mapped_ref, weight_ref, gathered, sems
):
    copies = gather_rows(weights_ref, W_TEXT, gathered, sems)
    for copy in copies:
        copy.start()
    for copy in copies:
        copy.wait()
    packed = gathered[...].reshape(D, E)
    column = lax.broadcasted_iota(jnp.int32, (DT, D), 1)
    place = column % 16
    row = jnp.where(place < 12, (column // 16) * 12 + place, -1)
    pick = (row == lax.broadcasted_iota(jnp.int32, (DT, D), 0)).astype(BF16)
    weight = dot(pick, packed).astype(BF16)
    weight_ref[...] = weight
    column = lax.broadcasted_iota(jnp.int32, (64, D), 1)
    pick = (column == 16 * lax.broadcasted_iota(jnp.int32, (64, D), 0) + 12).astype(BF16)
    pool = dot(pick, packed)
    pool_ref[...] = pool
    mapped_ref[...] = exact(dot, layer_norm(pool, gain_ref[...]), weight)


def unit_rows(values):
    return values * lax.rsqrt(jnp.sum(values * values, axis=-1, keepdims=True) + UNIT_EPS)


def unit_back(mapped, grad):
    scale = lax.rsqrt(jnp.sum(mapped * mapped, axis=-1, keepdims=True) + UNIT_EPS)
    along = jnp.sum(mapped * grad, axis=-1, keepdims=True)
    return scale * grad - mapped * (scale * scale * scale * along)


def norm_back(values, gain, grad):
    center = values - jnp.mean(values, axis=-1, keepdims=True)
    scale = lax.rsqrt(jnp.mean(center * center, axis=-1, keepdims=True) + NORM_EPS)
    grad = grad * gain
    unit = center * scale
    along = jnp.mean(grad * unit, axis=-1, keepdims=True)
    return scale * (grad - jnp.mean(grad, axis=-1, keepdims=True) - unit * along)


def loss_kernel(
    place_ref,
    scale_ref,
    pairs_ref,
    pooled_ref,
    text_pool_ref,
    text_mapped_ref,
    text_weight_ref,
    gain_video_ref,
    gain_text_ref,
    weights_ref,
    video_loss_ref,
    text_loss_ref,
    grad_pooled_ref,
    grad_text_ref,
    gathered,
    text_weight,
    pooled_all,
    sems,
):
    me = place_ref[0]
    copies = gather_rows(weights_ref, 0, gathered, sems)
    copy_text = pltpu.make_async_copy(text_weight_ref, text_weight, sems.at[2 * Y])
    for copy in copies + [copy_text]:
        copy.start()
    scale = scale_ref[0]
    for chunk in range(D // 128):
        pooled_all[:, chunk * 128 : (chunk + 1) * 128] = pooled_ref[:, chunk, :]
    gain = gain_video_ref[...]
    normed = layer_norm(pooled_all[...], gain)
    for copy in copies:
        copy.wait()
    weight = gathered[...].reshape(D, E)
    mapped = exact(dot, normed, weight)
    video = unit_rows(mapped)
    text_mapped = text_mapped_ref[...]
    text = unit_rows(text_mapped)
    logits = scale * lax.dot_general(
        video, text, (((1,), (1,)), ((), ())), precision=lax.Precision.HIGHEST,
        preferred_element_type=F32,
    )
    count = logits.shape[0]
    rows = lax.broadcasted_iota(jnp.int32, (count, count), 0)
    columns = lax.broadcasted_iota(jnp.int32, (count, count), 1)
    match = pairs_ref[...] == columns
    row_top = jnp.max(logits, axis=1, keepdims=True)
    row_exp = jnp.exp(logits - row_top)
    row_sum = jnp.sum(row_exp, axis=1, keepdims=True)
    col_top = jnp.max(logits, axis=0, keepdims=True)
    col_exp = jnp.exp(logits - col_top)
    col_sum = jnp.sum(col_exp, axis=0, keepdims=True)
    positive = jnp.where(match, logits, 0.0)
    video_loss = 0.5 * (row_top + jnp.log(row_sum) - jnp.sum(positive, axis=1, keepdims=True))
    text_loss = 0.5 * (col_top + jnp.log(col_sum) - jnp.sum(positive, axis=0, keepdims=True))
    mine_row = lax.broadcasted_iota(jnp.int32, (count, 1), 0) == me
    mine_col = lax.broadcasted_iota(jnp.int32, (1, count), 1) == me
    video_loss_ref[0] = jnp.sum(jnp.where(mine_row, video_loss, 0.0))
    text_loss_ref[0] = jnp.sum(jnp.where(mine_col, text_loss, 0.0))
    slope = (0.5 * scale) * (row_exp / row_sum + col_exp / col_sum - 2.0 * match.astype(F32))
    row_slope = jnp.sum(jnp.where(rows == me, slope, 0.0), axis=0, keepdims=True)
    row_slope = jnp.sum(jnp.where(rows == columns, row_slope, 0.0), axis=1, keepdims=True)
    col_slope = jnp.sum(jnp.where(columns == me, slope, 0.0), axis=1, keepdims=True)
    grad_video = jnp.sum(row_slope * text, axis=0, keepdims=True)
    grad_caption = jnp.sum(col_slope * video, axis=0, keepdims=True)
    mine_mapped = jnp.sum(jnp.where(mine_row, mapped, 0.0), axis=0, keepdims=True)
    mine_text_mapped = jnp.sum(jnp.where(mine_row, text_mapped, 0.0), axis=0, keepdims=True)
    mine_pooled = jnp.sum(jnp.where(mine_row, pooled_all[...], 0.0), axis=0, keepdims=True)
    mine_text_pool = jnp.sum(jnp.where(mine_row, text_pool_ref[...], 0.0), axis=0, keepdims=True)
    back = exact_row(dot_t, unit_back(mine_mapped, grad_video), weight)
    grad_pooled_ref[...] = norm_back(mine_pooled, gain, back)
    copy_text.wait()
    back = exact_row(dot_t, unit_back(mine_text_mapped, grad_caption), text_weight[...])
    grad_text_ref[...] = norm_back(mine_text_pool, gain_text_ref[...], back)


def call(kernel, out_shape, in_spaces, scratch, out_spaces=None, vmem=VMEM_LIMIT):
    many = isinstance(out_shape, (tuple, list))
    out_spaces = out_spaces or ([pltpu.VMEM] * (len(out_shape) if many else 1))
    out_specs = [pl.BlockSpec(memory_space=space) for space in out_spaces]
    return pl.pallas_call(
        kernel,
        out_shape=out_shape,
        in_specs=[pl.BlockSpec(memory_space=space) for space in in_spaces],
        out_specs=out_specs if many else out_specs[0],
        scratch_shapes=scratch,
        compiler_params=pltpu.CompilerParams(vmem_limit_bytes=vmem),
    )


def shape(dims, dtype):
    return jax.ShapeDtypeStruct(dims, dtype)


def send_all(block, groups):
    copies = jnp.broadcast_to(block[None], (len(groups[0]),) + block.shape)
    return lax.all_to_all(copies, "dp", 0, 0, tiled=True, axis_index_groups=groups)


def on_device(
    video_tokens,
    text_states,
    caption_ids,
    pair_index,
    logit_scale,
    gain_spatial,
    gain_temporal,
    gain_video,
    gain_text,
    w_qkv_spatial,
    w_out_spatial,
    w_qkv_temporal,
    w_out_temporal,
    w_video,
    w_text,
):
    V, S, A = pltpu.VMEM, pltpu.SMEM, pl.ANY
    DMA = pltpu.SemaphoreType.DMA
    halves = (X, Y, 2, 16)
    tokens = video_tokens.reshape(256, D)
    dealing = video_tokens.reshape(FRAMES, 32, D)
    place = lax.axis_index("dp").astype(jnp.int32).reshape(1)
    frame = lax.axis_index("frame").astype(jnp.int32).reshape(1)
    packed = call(
        pack_kernel,
        shape((16, PACKED), BF16),
        (A,) * 7,
        [
            pltpu.VMEM(caption_ids.shape, jnp.int32),
            pltpu.VMEM(text_states.shape[1:], BF16),
            pltpu.VMEM(w_text.shape, BF16),
            pltpu.VMEM(w_out_spatial.shape, BF16),
            pltpu.VMEM(w_out_temporal.shape, BF16),
            DMA((7,)),
        ],
        vmem=VMEM_WHOLE,
    )(
        caption_ids,
        text_states.reshape(text_states.shape[1:]),
        w_qkv_temporal,
        w_text,
        w_out_spatial,
        w_out_temporal,
        w_video,
    )
    own = send_all(w_qkv_spatial, ROWS_OF_Y)
    packed = lax.all_gather(packed, "dp", axis=0, tiled=True, axis_index_groups=ROWS_OF_X)
    own, packed = lax.optimization_barrier((own, packed))
    early = lax.all_gather(
        packed[:, :W_VIDEO], "dp", axis=0, tiled=True, axis_index_groups=ROWS_OF_YC
    ).reshape(Y, 2, X, 16, W_VIDEO)
    late = lax.all_gather(
        packed[:, W_VIDEO:], "dp", axis=0, tiled=True, axis_index_groups=ROWS_OF_YC
    ).reshape(Y, 2, X, 16, E)
    own = send_all(own.reshape(Y * 16, 3 * WIDTH), ROWS_OF_X).reshape(X * Y, 16, 3 * WIDTH)
    dealt = call(
        deal_kernel, (shape((32, D), BF16),) * (FRAMES - 1), (S, A), [DMA((FRAMES,))],
        (A,) * (FRAMES - 1),
    )(frame, dealing)
    dealt = [
        lax.ppermute(block, "frame", [(i, (i + 1 + step) % FRAMES) for i in range(FRAMES)])
        for step, block in enumerate(dealt)
    ]
    other = lax.ppermute(own, "dp", OTHER_CORE)

    mixed = call(
        spatial_kernel,
        shape((256, WIDTH), BF16),
        (S, A, V, A, A),
        [
            pltpu.VMEM((256, D), BF16),
            pltpu.VMEM((X * Y, 2, 16, 3 * WIDTH), BF16),
            pltpu.VMEM((256, 3 * WIDTH), BF16),
            DMA((3,)),
        ],
    )(place % 2, tokens, gain_spatial.reshape(1, D), own, other)
    mixed = lax.all_to_all(mixed.reshape(8, 32, WIDTH), "frame", 0, 0, tiled=True)
    layer_out, pool = call(
        temporal_kernel,
        (shape((256, D), BF16), shape((FRAMES, 8, 128), F32)),
        (S, V, V, A, A) + (A,) * (FRAMES - 1),
        [
            pltpu.VMEM((FRAMES, 32, D), BF16),
            pltpu.VMEM(halves + (3 * WIDTH,), BF16),
            pltpu.VMEM(halves + (D,), BF16),
            pltpu.VMEM((FRAMES, 32, 3 * WIDTH), BF16),
            pltpu.VMEM((FRAMES, 32, WIDTH), BF16),
            DMA((3, 2 * Y)),
        ],
    )(frame, mixed.reshape(256, WIDTH), gain_temporal.reshape(1, D), early, dealing, *dealt)
    text_pool, text_mapped, text_weight = call(
        text_kernel,
        (shape((64, DT), F32), shape((64, E), F32), shape((DT, E), BF16)),
        (V, A),
        [pltpu.VMEM(halves + (E,), BF16), DMA((2 * Y,))],
    )(gain_text.reshape(1, DT), early)
    pool = lax.all_to_all(pool, "frame", 0, 0, tiled=True)
    pool = call(spread_kernel, shape((64, 8, 128), F32), (V,), [])(pool)
    pooled = lax.all_to_all(pool, "dp", 0, 0, tiled=True)
    video_loss, text_loss, grad_pooled, grad_text = call(
        loss_kernel,
        (shape((1,), F32), shape((1,), F32), shape((1, D), F32), shape((1, DT), F32)),
        (S, S, V, V, V, V, A, V, V, A),
        [
            pltpu.VMEM(halves + (E,), BF16),
            pltpu.VMEM((DT, E), BF16),
            pltpu.VMEM((64, D), F32),
            DMA((2 * Y + 1,)),
        ],
        (S, S, V, V),
        vmem=VMEM_MOST,
    )(
        place,
        logit_scale,
        pair_index.reshape(64, 1),
        pooled,
        text_pool,
        text_mapped,
        text_weight,
        gain_video.reshape(1, D),
        gain_text.reshape(1, DT),
        late,
    )
    return (layer_out.reshape(1, 8, 32, D), video_loss, text_loss, grad_pooled, grad_text)


def solution(mesh):
    placed = (
        P("dp", "frame", None, None),
        P("dp", None, None),
        P("dp", None),
        P(),
        P(),
        P(),
        P(),
        P(),
        P(),
        P("dp", None),
        P("dp", None),
        P("dp", None),
        P("dp", None),
        P("dp", None),
        P("dp", None),
    )
    return jax.shard_map(
        on_device,
        mesh=mesh,
        in_specs=placed,
        out_specs=(P("dp", None, "frame", None), P("dp"), P("dp"), P("dp", None), P("dp", None)),
        check_vma=False,
    )
```

```python
import functools

import jax
import jax.numpy as jnp
from jax import lax
from jax.experimental import pallas as pl
from jax.experimental.pallas import tpu as pltpu
from jax.sharding import PartitionSpec as P

HEADS = 8
HD = 64
WIDTH = HEADS * HD
D = 1024
DT = 768
E = 768
NORM_EPS = 1e-05
UNIT_EPS = 1e-06
F32 = jnp.float32
BF16 = jnp.bfloat16
MIB = 1024 * 1024
VMEM_LIMIT = 48 * MIB
VMEM_WHOLE = 63 * MIB
VMEM_MOST = 52 * MIB

QKV_T = 0
W_TEXT = 1536
W_OUT = 2304
W_VIDEO = 3328
PACKED = 4096

X, Y = 4, 8
ROWS_OF_X = [[(x * Y + y) * 2 + c for x in range(X)] for y in range(Y) for c in range(2)]
ROWS_OF_Y = [[(x * Y + y) * 2 + c for y in range(Y)] for x in range(X) for c in range(2)]
ROWS_OF_YC = [[(x * Y + y) * 2 + c for y in range(Y) for c in range(2)] for x in range(X)]
OTHER_CORE = [(i, i ^ 1) for i in range(2 * X * Y)]
FRAMES = 8


def dot(a, b):
    return lax.dot_general(a, b, (((1,), (0,)), ((), ())), preferred_element_type=F32)


def dot_t(a, b):
    return lax.dot_general(a, b, (((1,), (1,)), ((), ())), preferred_element_type=F32)


def pieces(a):
    first = a.astype(BF16)
    rest = a - first.astype(F32)
    second = rest.astype(BF16)
    third = (rest - second.astype(F32)).astype(BF16)
    return first, second, third


def exact(dot_fn, a, weight):
    rows = a.shape[0]
    parts = dot_fn(jnp.concatenate(pieces(a), axis=0), weight)
    return parts[2 * rows :] + parts[rows : 2 * rows] + parts[:rows]


def exact_row(dot_fn, a, weight):
    rows = lax.broadcasted_iota(jnp.int32, (16, a.shape[1]), 0)
    first, second, third = (piece.astype(F32) for piece in pieces(a))
    block = jnp.where(rows == 0, third, jnp.where(rows == 1, second, jnp.where(rows == 2, first, 0.0)))
    return jnp.sum(dot_fn(block.astype(BF16), weight), axis=0, keepdims=True)


def layer_norm(values, gain):
    center = values - jnp.mean(values, axis=-1, keepdims=True)
    spread = jnp.mean(center * center, axis=-1, keepdims=True)
    return center * lax.rsqrt(spread + NORM_EPS) * gain


def attend_pair(query, key, value, mask):
    low = lax.broadcasted_iota(jnp.int32, query.shape, 1) < HD
    mixed = []
    for lanes in (low, ~low):
        scores = dot_t(jnp.where(lanes, query, jnp.zeros_like(query)), key) * (HD**-0.5)
        if mask is not None:
            scores = jnp.where(mask, scores, -1e30)
        weight = jnp.exp(scores - jnp.max(scores, axis=-1, keepdims=True))
        probs = weight * (1.0 / jnp.sum(weight, axis=-1, keepdims=True))
        mixed.append(dot(probs.astype(BF16), value))
    return jnp.where(low, mixed[0], mixed[1]).astype(BF16)


def attend(packed_ref, mixed_ref, mask):
    for at in range(0, WIDTH, 2 * HD):
        query, key, value = (
            packed_ref[:, part * WIDTH + at : part * WIDTH + at + 2 * HD] for part in range(3)
        )
        mixed_ref[:, at : at + 2 * HD] = attend_pair(query, key, value, mask)


def spatial_kernel(
    core_ref, tokens_ref, gain_ref, own_ref, other_ref, mixed_ref, tokens, qkv, packed, sems
):
    core = core_ref[0]
    copy_tokens = pltpu.make_async_copy(tokens_ref, tokens, sems.at[2])
    copy_own = pltpu.make_async_copy(own_ref, qkv.at[:, core], sems.at[0])
    copy_other = pltpu.make_async_copy(other_ref, qkv.at[:, 1 - core], sems.at[1])
    copy_tokens.start()
    copy_own.start()
    copy_other.start()
    copy_tokens.wait()
    normed = layer_norm(tokens[...].astype(F32), gain_ref[...]).astype(BF16)
    copy_own.wait()
    copy_other.wait()
    packed[...] = dot(normed, qkv[...].reshape(D, 3 * WIDTH)).astype(BF16)
    attend(packed, mixed_ref, None)


def gather_rows(weights_ref, first, target, sems):
    width = target.shape[-1]
    return [
        pltpu.make_async_copy(
            weights_ref.at[y, c, :, :, first : first + width], target.at[:, y, c], sems.at[2 * y + c]
        )
        for y in range(Y)
        for c in range(2)
    ]


def pack_kernel(
    ids_ref, states_ref, qkv_ref, text_ref, out_s_ref, out_t_ref, video_ref, packed_ref,
    ids_here, states_here, text_here, out_s_here, out_t_here, sems,
):
    pairs = (
        (ids_ref, ids_here),
        (states_ref, states_here),
        (text_ref, text_here),
        (out_s_ref, out_s_here),
        (out_t_ref, out_t_here),
        (qkv_ref, packed_ref.at[:, QKV_T : QKV_T + 3 * WIDTH]),
        (video_ref, packed_ref.at[:, W_VIDEO : W_VIDEO + E]),
    )
    copies = [pltpu.make_async_copy(*pair, sems.at[i]) for i, pair in enumerate(pairs)]
    for copy in copies:
        copy.start()
    for copy in copies:
        copy.wait()
    ids = ids_here[...]
    positions = lax.broadcasted_iota(jnp.int32, ids.shape, 1)
    end_place = jnp.min(jnp.where(ids == jnp.max(ids), positions, ids.shape[1]))
    states = states_here[...].astype(F32)
    rows = lax.broadcasted_iota(jnp.int32, states.shape, 0)
    text_row = jnp.sum(jnp.where(rows == end_place, states, 0.0), axis=0, keepdims=True)
    text = jnp.concatenate([text_here[...].astype(F32), jnp.zeros((4, E), F32)], axis=0)
    place = lax.broadcasted_iota(jnp.int32, text.shape, 0)
    text = jnp.where(place < 12, text, jnp.where(place == 12, text_row, 0.0))
    packed_ref[:, W_TEXT : W_TEXT + E] = text.astype(BF16)
    outs = jnp.concatenate([out_s_here[...].astype(F32), out_t_here[...].astype(F32)], axis=0)
    packed_ref[:, W_OUT : W_OUT + D] = outs.astype(BF16)


def deal_kernel(frame_ref, tokens_ref, *rest):
    dealt, sems = rest[:-1], rest[-1]
    copies = [
        pltpu.make_async_copy(
            tokens_ref.at[(frame_ref[0] + step) % FRAMES], dealt[step - 1], sems.at[step - 1]
        )
        for step in range(1, FRAMES)
    ]
    for copy in copies:
        copy.start()
    for copy in copies:
        copy.wait()


def temporal_kernel(frame_ref, mixed_ref, gain_ref, weights_ref, tokens_ref, *rest):
    dealt, rest = rest[: FRAMES - 1], rest[FRAMES - 1 :]
    out_ref, pool_ref, tokens, qkv, outs, packed, mixed, sems = rest
    frame = frame_ref[0]
    copies_tokens = [pltpu.make_async_copy(tokens_ref.at[frame], tokens.at[frame], sems.at[2, 0])]
    for step in range(1, FRAMES):
        source = (frame + FRAMES - step) % FRAMES
        copies_tokens.append(
            pltpu.make_async_copy(dealt[step - 1], tokens.at[source], sems.at[2, step])
        )
    copies_out = gather_rows(weights_ref, W_OUT, outs, sems.at[0])
    copies_qkv = gather_rows(weights_ref, QKV_T, qkv, sems.at[1])
    for copy in copies_out + copies_tokens + copies_qkv:
        copy.start()
    for copy in copies_out:
        copy.wait()
    both = outs[...].astype(F32).reshape(64, 2, 8, D)
    out_spatial = both[:, 0].reshape(WIDTH, D).astype(BF16)
    out_temporal = both[:, 1].reshape(WIDTH, D).astype(BF16)
    for copy in copies_tokens:
        copy.wait()
    rows = tokens.shape[0] * tokens.shape[1]
    spatial = tokens[...].reshape(rows, D).astype(F32) + dot(mixed_ref[...], out_spatial)
    spatial = spatial.astype(BF16)
    normed = layer_norm(spatial.astype(F32), gain_ref[...]).astype(BF16)
    for copy in copies_qkv:
        copy.wait()
    packed[...] = dot(normed, qkv[...].reshape(D, 3 * WIDTH)).astype(BF16)
    patches = tokens.shape[1]
    place = lax.broadcasted_iota(jnp.int32, (rows, rows), 0) % patches
    attend(packed, mixed, place == lax.broadcasted_iota(jnp.int32, (rows, rows), 1) % patches)
    output = spatial.astype(F32) + dot(mixed[...], out_temporal)
    output = output.astype(BF16)
    out_ref[...] = output
    total = jnp.sum(output.astype(F32), axis=0, keepdims=True)
    for chunk in range(D // 128):
        pool_ref[:, chunk, :] = jnp.broadcast_to(
            total[:, chunk * 128 : (chunk + 1) * 128], (FRAMES, 128)
        )


def spread_kernel(parts_ref, every_ref):
    mine = jnp.sum(parts_ref[...], axis=0) * (1.0 / (8 * 256))
    every_ref[...] = jnp.broadcast_to(mine[None], every_ref.shape)


def text_kernel(
    gain_ref, weights_ref, pool_ref, mapped_ref, weight_ref, gathered, sems
):
    copies = gather_rows(weights_ref, W_TEXT, gathered, sems)
    for copy in copies:
        copy.start()
    for copy in copies:
        copy.wait()
    packed = gathered[...].reshape(D, E)
    column = lax.broadcasted_iota(jnp.int32, (DT, D), 1)
    place = column % 16
    row = jnp.where(place < 12, (column // 16) * 12 + place, -1)
    pick = (row == lax.broadcasted_iota(jnp.int32, (DT, D), 0)).astype(BF16)
    weight = dot(pick, packed).astype(BF16)
    weight_ref[...] = weight
    column = lax.broadcasted_iota(jnp.int32, (64, D), 1)
    pick = (column == 16 * lax.broadcasted_iota(jnp.int32, (64, D), 0) + 12).astype(BF16)
    pool = dot(pick, packed)
    pool_ref[...] = pool
    mapped_ref[...] = exact(dot, layer_norm(pool, gain_ref[...]), weight)


def unit_rows(values):
    return values * lax.rsqrt(jnp.sum(values * values, axis=-1, keepdims=True) + UNIT_EPS)


def unit_back(mapped, grad):
    scale = lax.rsqrt(jnp.sum(mapped * mapped, axis=-1, keepdims=True) + UNIT_EPS)
    along = jnp.sum(mapped * grad, axis=-1, keepdims=True)
    return scale * grad - mapped * (scale * scale * scale * along)


def norm_back(values, gain, grad):
    center = values - jnp.mean(values, axis=-1, keepdims=True)
    scale = lax.rsqrt(jnp.mean(center * center, axis=-1, keepdims=True) + NORM_EPS)
    grad = grad * gain
    unit = center * scale
    along = jnp.mean(grad * unit, axis=-1, keepdims=True)
    return scale * (grad - jnp.mean(grad, axis=-1, keepdims=True) - unit * along)


def loss_kernel(
    place_ref,
    scale_ref,
    pairs_ref,
    pooled_ref,
    text_pool_ref,
    text_mapped_ref,
    text_weight_ref,
    gain_video_ref,
    gain_text_ref,
    weights_ref,
    video_loss_ref,
    text_loss_ref,
    grad_pooled_ref,
    grad_text_ref,
    gathered,
    text_weight,
    pooled_all,
    sems,
):
    me = place_ref[0]
    copies = gather_rows(weights_ref, 0, gathered, sems)
    copy_text = pltpu.make_async_copy(text_weight_ref, text_weight, sems.at[2 * Y])
    for copy in copies + [copy_text]:
        copy.start()
    scale = scale_ref[0]
    for chunk in range(D // 128):
        pooled_all[:, chunk * 128 : (chunk + 1) * 128] = pooled_ref[:, chunk, :]
    gain = gain_video_ref[...]
    normed = layer_norm(pooled_all[...], gain)
    for copy in copies:
        copy.wait()
    weight = gathered[...].reshape(D, E)
    mapped = exact(dot, normed, weight)
    video = unit_rows(mapped)
    text_mapped = text_mapped_ref[...]
    text = unit_rows(text_mapped)
    logits = scale * lax.dot_general(
        video, text, (((1,), (1,)), ((), ())), precision=lax.Precision.HIGHEST,
        preferred_element_type=F32,
    )
    count = logits.shape[0]
    rows = lax.broadcasted_iota(jnp.int32, (count, count), 0)
    columns = lax.broadcasted_iota(jnp.int32, (count, count), 1)
    match = pairs_ref[...] == columns
    row_top = jnp.max(logits, axis=1, keepdims=True)
    row_exp = jnp.exp(logits - row_top)
    row_sum = jnp.sum(row_exp, axis=1, keepdims=True)
    col_top = jnp.max(logits, axis=0, keepdims=True)
    col_exp = jnp.exp(logits - col_top)
    col_sum = jnp.sum(col_exp, axis=0, keepdims=True)
    positive = jnp.where(match, logits, 0.0)
    video_loss = 0.5 * (row_top + jnp.log(row_sum) - jnp.sum(positive, axis=1, keepdims=True))
    text_loss = 0.5 * (col_top + jnp.log(col_sum) - jnp.sum(positive, axis=0, keepdims=True))
    mine_row = lax.broadcasted_iota(jnp.int32, (count, 1), 0) == me
    mine_col = lax.broadcasted_iota(jnp.int32, (1, count), 1) == me
    video_loss_ref[0] = jnp.sum(jnp.where(mine_row, video_loss, 0.0))
    text_loss_ref[0] = jnp.sum(jnp.where(mine_col, text_loss, 0.0))
    slope = (0.5 * scale) * (row_exp / row_sum + col_exp / col_sum - 2.0 * match.astype(F32))
    row_slope = jnp.sum(jnp.where(rows == me, slope, 0.0), axis=0, keepdims=True)
    row_slope = jnp.sum(jnp.where(rows == columns, row_slope, 0.0), axis=1, keepdims=True)
    col_slope = jnp.sum(jnp.where(columns == me, slope, 0.0), axis=1, keepdims=True)
    grad_video = jnp.sum(row_slope * text, axis=0, keepdims=True)
    grad_caption = jnp.sum(col_slope * video, axis=0, keepdims=True)
    mine_mapped = jnp.sum(jnp.where(mine_row, mapped, 0.0), axis=0, keepdims=True)
    mine_text_mapped = jnp.sum(jnp.where(mine_row, text_mapped, 0.0), axis=0, keepdims=True)
    mine_pooled = jnp.sum(jnp.where(mine_row, pooled_all[...], 0.0), axis=0, keepdims=True)
    mine_text_pool = jnp.sum(jnp.where(mine_row, text_pool_ref[...], 0.0), axis=0, keepdims=True)
    back = exact_row(dot_t, unit_back(mine_mapped, grad_video), weight)
    grad_pooled_ref[...] = norm_back(mine_pooled, gain, back)
    copy_text.wait()
    back = exact_row(dot_t, unit_back(mine_text_mapped, grad_caption), text_weight[...])
    grad_text_ref[...] = norm_back(mine_text_pool, gain_text_ref[...], back)


def call(kernel, out_shape, in_spaces, scratch, out_spaces=None, vmem=VMEM_LIMIT):
    many = isinstance(out_shape, (tuple, list))
    out_spaces = out_spaces or ([pltpu.VMEM] * (len(out_shape) if many else 1))
    out_specs = [pl.BlockSpec(memory_space=space) for space in out_spaces]
    return pl.pallas_call(
        kernel,
        out_shape=out_shape,
        in_specs=[pl.BlockSpec(memory_space=space) for space in in_spaces],
        out_specs=out_specs if many else out_specs[0],
        scratch_shapes=scratch,
        compiler_params=pltpu.CompilerParams(vmem_limit_bytes=vmem),
    )


def shape(dims, dtype):
    return jax.ShapeDtypeStruct(dims, dtype)


def send_all(block, groups):
    copies = jnp.broadcast_to(block[None], (len(groups[0]),) + block.shape)
    return lax.all_to_all(copies, "dp", 0, 0, tiled=True, axis_index_groups=groups)


def on_device(
    video_tokens,
    text_states,
    caption_ids,
    pair_index,
    logit_scale,
    gain_spatial,
    gain_temporal,
    gain_video,
    gain_text,
    w_qkv_spatial,
    w_out_spatial,
    w_qkv_temporal,
    w_out_temporal,
    w_video,
    w_text,
):
    V, S, A = pltpu.VMEM, pltpu.SMEM, pl.ANY
    DMA = pltpu.SemaphoreType.DMA
    halves = (X, Y, 2, 16)
    tokens = video_tokens.reshape(256, D)
    dealing = video_tokens.reshape(FRAMES, 32, D)
    place = lax.axis_index("dp").astype(jnp.int32).reshape(1)
    frame = lax.axis_index("frame").astype(jnp.int32).reshape(1)
    packed = call(
        pack_kernel,
        shape((16, PACKED), BF16),
        (A,) * 7,
        [
            pltpu.VMEM(caption_ids.shape, jnp.int32),
            pltpu.VMEM(text_states.shape[1:], BF16),
            pltpu.VMEM(w_text.shape, BF16),
            pltpu.VMEM(w_out_spatial.shape, BF16),
            pltpu.VMEM(w_out_temporal.shape, BF16),
            DMA((7,)),
        ],
        vmem=VMEM_WHOLE,
    )(
        caption_ids,
        text_states.reshape(text_states.shape[1:]),
        w_qkv_temporal,
        w_text,
        w_out_spatial,
        w_out_temporal,
        w_video,
    )
    own = send_all(w_qkv_spatial, ROWS_OF_Y)
    packed = lax.all_gather(packed, "dp", axis=0, tiled=True, axis_index_groups=ROWS_OF_X)
    own, packed = lax.optimization_barrier((own, packed))
    early = lax.all_gather(
        packed[:, :W_VIDEO], "dp", axis=0, tiled=True, axis_index_groups=ROWS_OF_YC
    ).reshape(Y, 2, X, 16, W_VIDEO)
    late = lax.all_gather(
        packed[:, W_VIDEO:], "dp", axis=0, tiled=True, axis_index_groups=ROWS_OF_YC
    ).reshape(Y, 2, X, 16, E)
    own = send_all(own.reshape(Y * 16, 3 * WIDTH), ROWS_OF_X).reshape(X * Y, 16, 3 * WIDTH)
    dealt = call(
        deal_kernel, (shape((32, D), BF16),) * (FRAMES - 1), (S, A), [DMA((FRAMES,))],
        (A,) * (FRAMES - 1),
    )(frame, dealing)
    dealt = [
        lax.ppermute(block, "frame", [(i, (i + 1 + step) % FRAMES) for i in range(FRAMES)])
        for step, block in enumerate(dealt)
    ]
    own, dealt[:4] = lax.optimization_barrier((own, dealt[:4]))
    other = lax.ppermute(own, "dp", OTHER_CORE)

    mixed = call(
        spatial_kernel,
        shape((256, WIDTH), BF16),
        (S, A, V, A, A),
        [
            pltpu.VMEM((256, D), BF16),
            pltpu.VMEM((X * Y, 2, 16, 3 * WIDTH), BF16),
            pltpu.VMEM((256, 3 * WIDTH), BF16),
            DMA((3,)),
        ],
    )(place % 2, tokens, gain_spatial.reshape(1, D), own, other)
    mixed = lax.all_to_all(mixed.reshape(8, 32, WIDTH), "frame", 0, 0, tiled=True)
    layer_out, pool = call(
        temporal_kernel,
        (shape((256, D), BF16), shape((FRAMES, 8, 128), F32)),
        (S, V, V, A, A) + (A,) * (FRAMES - 1),
        [
            pltpu.VMEM((FRAMES, 32, D), BF16),
            pltpu.VMEM(halves + (3 * WIDTH,), BF16),
            pltpu.VMEM(halves + (D,), BF16),
            pltpu.VMEM((256, 3 * WIDTH), BF16),
            pltpu.VMEM((256, WIDTH), BF16),
            DMA((3, 2 * Y)),
        ],
    )(frame, mixed.reshape(256, WIDTH), gain_temporal.reshape(1, D), early, dealing, *dealt)
    text_pool, text_mapped, text_weight = call(
        text_kernel,
        (shape((64, DT), F32), shape((64, E), F32), shape((DT, E), BF16)),
        (V, A),
        [pltpu.VMEM(halves + (E,), BF16), DMA((2 * Y,))],
    )(gain_text.reshape(1, DT), early)
    pool = lax.all_to_all(pool, "frame", 0, 0, tiled=True)
    pool = call(spread_kernel, shape((64, 8, 128), F32), (V,), [])(pool)
    pooled = lax.all_to_all(pool, "dp", 0, 0, tiled=True)
    video_loss, text_loss, grad_pooled, grad_text = call(
        loss_kernel,
        (shape((1,), F32), shape((1,), F32), shape((1, D), F32), shape((1, DT), F32)),
        (S, S, V, V, V, V, A, V, V, A),
        [
            pltpu.VMEM(halves + (E,), BF16),
            pltpu.VMEM((DT, E), BF16),
            pltpu.VMEM((64, D), F32),
            DMA((2 * Y + 1,)),
        ],
        (S, S, V, V),
        vmem=VMEM_MOST,
    )(
        place,
        logit_scale,
        pair_index.reshape(64, 1),
        pooled,
        text_pool,
        text_mapped,
        text_weight,
        gain_video.reshape(1, D),
        gain_text.reshape(1, DT),
        late,
    )
    return (layer_out.reshape(1, 8, 32, D), video_loss, text_loss, grad_pooled, grad_text)


def solution(mesh):
    placed = (
        P("dp", "frame", None, None),
        P("dp", None, None),
        P("dp", None),
        P(),
        P(),
        P(),
        P(),
        P(),
        P(),
        P("dp", None),
        P("dp", None),
        P("dp", None),
        P("dp", None),
        P("dp", None),
        P("dp", None),
    )
    return jax.shard_map(
        on_device,
        mesh=mesh,
        in_specs=placed,
        out_specs=(P("dp", None, "frame", None), P("dp"), P("dp"), P("dp", None), P("dp", None)),
        check_vma=False,
    )
```

```python
import functools

import jax
import jax.numpy as jnp
from jax import lax
from jax.experimental import pallas as pl
from jax.experimental.pallas import tpu as pltpu
from jax.sharding import PartitionSpec as P

HEADS = 8
HD = 64
WIDTH = HEADS * HD
D = 1024
DT = 768
E = 768
NORM_EPS = 1e-05
UNIT_EPS = 1e-06
F32 = jnp.float32
BF16 = jnp.bfloat16
MIB = 1024 * 1024
VMEM_LIMIT = 48 * MIB
VMEM_WHOLE = 63 * MIB
VMEM_MOST = 52 * MIB

QKV_T = 0
W_TEXT = 1536
W_OUT = 2304
PACKED = 3328

X, Y = 4, 8
ROWS_OF_X = [[(x * Y + y) * 2 + c for x in range(X)] for y in range(Y) for c in range(2)]
ROWS_OF_Y = [[(x * Y + y) * 2 + c for y in range(Y)] for x in range(X) for c in range(2)]
ROWS_OF_YC = [[(x * Y + y) * 2 + c for y in range(Y) for c in range(2)] for x in range(X)]
OTHER_CORE = [(i, i ^ 1) for i in range(2 * X * Y)]
FRAMES = 8


def dot(a, b):
    return lax.dot_general(a, b, (((1,), (0,)), ((), ())), preferred_element_type=F32)


def dot_t(a, b):
    return lax.dot_general(a, b, (((1,), (1,)), ((), ())), preferred_element_type=F32)


def pieces(a):
    first = a.astype(BF16)
    rest = a - first.astype(F32)
    second = rest.astype(BF16)
    third = (rest - second.astype(F32)).astype(BF16)
    return first, second, third


def exact(dot_fn, a, weight):
    rows = a.shape[0]
    parts = dot_fn(jnp.concatenate(pieces(a), axis=0), weight)
    return parts[2 * rows :] + parts[rows : 2 * rows] + parts[:rows]


def exact_row(dot_fn, a, weight):
    rows = lax.broadcasted_iota(jnp.int32, (16, a.shape[1]), 0)
    first, second, third = (piece.astype(F32) for piece in pieces(a))
    block = jnp.where(rows == 0, third, jnp.where(rows == 1, second, jnp.where(rows == 2, first, 0.0)))
    return jnp.sum(dot_fn(block.astype(BF16), weight), axis=0, keepdims=True)


def layer_norm(values, gain):
    center = values - jnp.mean(values, axis=-1, keepdims=True)
    spread = jnp.mean(center * center, axis=-1, keepdims=True)
    return center * lax.rsqrt(spread + NORM_EPS) * gain


def attend_pair(query, key, value, mask):
    low = lax.broadcasted_iota(jnp.int32, query.shape, 1) < HD
    mixed = []
    for lanes in (low, ~low):
        scores = dot_t(jnp.where(lanes, query, jnp.zeros_like(query)), key) * (HD**-0.5)
        if mask is not None:
            scores = jnp.where(mask, scores, -1e30)
        weight = jnp.exp(scores - jnp.max(scores, axis=-1, keepdims=True))
        probs = weight * (1.0 / jnp.sum(weight, axis=-1, keepdims=True))
        mixed.append(dot(probs.astype(BF16), value))
    return jnp.where(low, mixed[0], mixed[1]).astype(BF16)


def attend(packed_ref, mixed_ref, mask):
    for at in range(0, WIDTH, 2 * HD):
        query, key, value = (
            packed_ref[:, part * WIDTH + at : part * WIDTH + at + 2 * HD] for part in range(3)
        )
        mixed_ref[:, at : at + 2 * HD] = attend_pair(query, key, value, mask)


def spatial_kernel(
    core_ref, tokens_ref, gain_ref, own_ref, other_ref, mixed_ref, tokens, qkv, packed, sems
):
    core = core_ref[0]
    copy_tokens = pltpu.make_async_copy(tokens_ref, tokens, sems.at[2])
    copy_own = pltpu.make_async_copy(own_ref, qkv.at[:, core], sems.at[0])
    copy_other = pltpu.make_async_copy(other_ref, qkv.at[:, 1 - core], sems.at[1])
    copy_tokens.start()
    copy_own.start()
    copy_other.start()
    copy_tokens.wait()
    normed = layer_norm(tokens[...].astype(F32), gain_ref[...]).astype(BF16)
    copy_own.wait()
    copy_other.wait()
    packed[...] = dot(normed, qkv[...].reshape(D, 3 * WIDTH)).astype(BF16)
    attend(packed, mixed_ref, None)


def gather_rows(weights_ref, first, target, sems):
    width = target.shape[-1]
    return [
        pltpu.make_async_copy(
            weights_ref.at[y, c, :, :, first : first + width], target.at[:, y, c], sems.at[2 * y + c]
        )
        for y in range(Y)
        for c in range(2)
    ]


def pack_kernel(
    ids_ref, states_ref, qkv_ref, text_ref, out_s_ref, out_t_ref, spatial_ref, packed_ref, copies_ref,
    ids_here, states_here, text_here, out_s_here, out_t_here, spatial_here, sems,
):
    pairs = (
        (spatial_ref, spatial_here),
        (ids_ref, ids_here),
        (states_ref, states_here),
        (text_ref, text_here),
        (out_s_ref, out_s_here),
        (out_t_ref, out_t_here),
        (qkv_ref, packed_ref.at[:, QKV_T : QKV_T + 3 * WIDTH]),
    )
    copies = [pltpu.make_async_copy(*pair, sems.at[i]) for i, pair in enumerate(pairs)]
    for copy in copies:
        copy.start()
    for copy in copies:
        copy.wait()
    copies_ref[...] = jnp.broadcast_to(spatial_here[...][None], copies_ref.shape)
    ids = ids_here[...]
    positions = lax.broadcasted_iota(jnp.int32, ids.shape, 1)
    end_place = jnp.min(jnp.where(ids == jnp.max(ids), positions, ids.shape[1]))
    states = states_here[...].astype(F32)
    rows = lax.broadcasted_iota(jnp.int32, states.shape, 0)
    text_row = jnp.sum(jnp.where(rows == end_place, states, 0.0), axis=0, keepdims=True)
    text = jnp.concatenate([text_here[...].astype(F32), jnp.zeros((4, E), F32)], axis=0)
    place = lax.broadcasted_iota(jnp.int32, text.shape, 0)
    text = jnp.where(place < 12, text, jnp.where(place == 12, text_row, 0.0))
    packed_ref[:, W_TEXT : W_TEXT + E] = text.astype(BF16)
    outs = jnp.concatenate([out_s_here[...].astype(F32), out_t_here[...].astype(F32)], axis=0)
    packed_ref[:, W_OUT : W_OUT + D] = outs.astype(BF16)


def temporal_kernel(
    mixed_ref, tokens_ref, gain_ref, weights_ref, out_ref, pool_ref, qkv, outs, packed, mixed, sems
):
    copies_out = gather_rows(weights_ref, W_OUT, outs, sems.at[0])
    copies_qkv = gather_rows(weights_ref, QKV_T, qkv, sems.at[1])
    for copy in copies_out + copies_qkv:
        copy.start()
    for copy in copies_out:
        copy.wait()
    both = outs[...].astype(F32).reshape(64, 2, 8, D)
    out_spatial = both[:, 0].reshape(WIDTH, D).astype(BF16)
    out_temporal = both[:, 1].reshape(WIDTH, D).astype(BF16)
    rows = tokens_ref.shape[0]
    spatial = (tokens_ref[...].astype(F32) + dot(mixed_ref[...], out_spatial)).astype(BF16)
    normed = layer_norm(spatial.astype(F32), gain_ref[...]).astype(BF16)
    for copy in copies_qkv:
        copy.wait()
    packed[...] = dot(normed, qkv[...].reshape(D, 3 * WIDTH)).astype(BF16)
    patches = rows // FRAMES
    place = lax.broadcasted_iota(jnp.int32, (rows, rows), 0) % patches
    attend(packed, mixed, place == lax.broadcasted_iota(jnp.int32, (rows, rows), 1) % patches)
    output = spatial.astype(F32) + dot(mixed[...], out_temporal)
    output = output.astype(BF16)
    out_ref[...] = output
    total = jnp.sum(output.astype(F32), axis=0, keepdims=True)
    for chunk in range(D // 128):
        pool_ref[:, chunk, :] = jnp.broadcast_to(
            total[:, chunk * 128 : (chunk + 1) * 128], (FRAMES, 128)
        )


def spread_kernel(parts_ref, every_ref):
    mine = jnp.sum(parts_ref[...], axis=0) * (1.0 / (8 * 256))
    every_ref[...] = jnp.broadcast_to(mine[None], every_ref.shape)


def text_kernel(
    gain_ref, weights_ref, pool_ref, mapped_ref, weight_ref, gathered, sems
):
    copies = gather_rows(weights_ref, W_TEXT, gathered, sems)
    for copy in copies:
        copy.start()
    for copy in copies:
        copy.wait()
    packed = gathered[...].reshape(D, E)
    column = lax.broadcasted_iota(jnp.int32, (DT, D), 1)
    place = column % 16
    row = jnp.where(place < 12, (column // 16) * 12 + place, -1)
    pick = (row == lax.broadcasted_iota(jnp.int32, (DT, D), 0)).astype(BF16)
    weight = dot(pick, packed).astype(BF16)
    weight_ref[...] = weight
    column = lax.broadcasted_iota(jnp.int32, (64, D), 1)
    pick = (column == 16 * lax.broadcasted_iota(jnp.int32, (64, D), 0) + 12).astype(BF16)
    pool = dot(pick, packed)
    pool_ref[...] = pool
    mapped_ref[...] = exact(dot, layer_norm(pool, gain_ref[...]), weight)


def unit_rows(values):
    return values * lax.rsqrt(jnp.sum(values * values, axis=-1, keepdims=True) + UNIT_EPS)


def unit_back(mapped, grad):
    scale = lax.rsqrt(jnp.sum(mapped * mapped, axis=-1, keepdims=True) + UNIT_EPS)
    along = jnp.sum(mapped * grad, axis=-1, keepdims=True)
    return scale * grad - mapped * (scale * scale * scale * along)


def norm_back(values, gain, grad):
    center = values - jnp.mean(values, axis=-1, keepdims=True)
    scale = lax.rsqrt(jnp.mean(center * center, axis=-1, keepdims=True) + NORM_EPS)
    grad = grad * gain
    unit = center * scale
    along = jnp.mean(grad * unit, axis=-1, keepdims=True)
    return scale * (grad - jnp.mean(grad, axis=-1, keepdims=True) - unit * along)


def loss_kernel(
    place_ref,
    scale_ref,
    pairs_ref,
    pooled_ref,
    text_pool_ref,
    text_mapped_ref,
    text_weight_ref,
    gain_video_ref,
    gain_text_ref,
    weights_ref,
    video_loss_ref,
    text_loss_ref,
    grad_pooled_ref,
    grad_text_ref,
    gathered,
    text_weight,
    pooled_all,
    sems,
):
    me = place_ref[0]
    copies = gather_rows(weights_ref, 0, gathered, sems)
    copy_text = pltpu.make_async_copy(text_weight_ref, text_weight, sems.at[2 * Y])
    for copy in copies + [copy_text]:
        copy.start()
    scale = scale_ref[0]
    for chunk in range(D // 128):
        pooled_all[:, chunk * 128 : (chunk + 1) * 128] = pooled_ref[:, chunk, :]
    gain = gain_video_ref[...]
    normed = layer_norm(pooled_all[...], gain)
    for copy in copies:
        copy.wait()
    weight = gathered[...].reshape(D, E)
    mapped = exact(dot, normed, weight)
    video = unit_rows(mapped)
    text_mapped = text_mapped_ref[...]
    text = unit_rows(text_mapped)
    logits = scale * lax.dot_general(
        video, text, (((1,), (1,)), ((), ())), precision=lax.Precision.HIGHEST,
        preferred_element_type=F32,
    )
    count = logits.shape[0]
    rows = lax.broadcasted_iota(jnp.int32, (count, count), 0)
    columns = lax.broadcasted_iota(jnp.int32, (count, count), 1)
    match = pairs_ref[...] == columns
    row_top = jnp.max(logits, axis=1, keepdims=True)
    row_exp = jnp.exp(logits - row_top)
    row_sum = jnp.sum(row_exp, axis=1, keepdims=True)
    col_top = jnp.max(logits, axis=0, keepdims=True)
    col_exp = jnp.exp(logits - col_top)
    col_sum = jnp.sum(col_exp, axis=0, keepdims=True)
    positive = jnp.where(match, logits, 0.0)
    video_loss = 0.5 * (row_top + jnp.log(row_sum) - jnp.sum(positive, axis=1, keepdims=True))
    text_loss = 0.5 * (col_top + jnp.log(col_sum) - jnp.sum(positive, axis=0, keepdims=True))
    mine_row = lax.broadcasted_iota(jnp.int32, (count, 1), 0) == me
    mine_col = lax.broadcasted_iota(jnp.int32, (1, count), 1) == me
    video_loss_ref[0] = jnp.sum(jnp.where(mine_row, video_loss, 0.0))
    text_loss_ref[0] = jnp.sum(jnp.where(mine_col, text_loss, 0.0))
    slope = (0.5 * scale) * (row_exp / row_sum + col_exp / col_sum - 2.0 * match.astype(F32))
    row_slope = jnp.sum(jnp.where(rows == me, slope, 0.0), axis=0, keepdims=True)
    row_slope = jnp.sum(jnp.where(rows == columns, row_slope, 0.0), axis=1, keepdims=True)
    col_slope = jnp.sum(jnp.where(columns == me, slope, 0.0), axis=1, keepdims=True)
    grad_video = jnp.sum(row_slope * text, axis=0, keepdims=True)
    grad_caption = jnp.sum(col_slope * video, axis=0, keepdims=True)
    mine_mapped = jnp.sum(jnp.where(mine_row, mapped, 0.0), axis=0, keepdims=True)
    mine_text_mapped = jnp.sum(jnp.where(mine_row, text_mapped, 0.0), axis=0, keepdims=True)
    mine_pooled = jnp.sum(jnp.where(mine_row, pooled_all[...], 0.0), axis=0, keepdims=True)
    mine_text_pool = jnp.sum(jnp.where(mine_row, text_pool_ref[...], 0.0), axis=0, keepdims=True)
    back = exact_row(dot_t, unit_back(mine_mapped, grad_video), weight)
    grad_pooled_ref[...] = norm_back(mine_pooled, gain, back)
    copy_text.wait()
    back = exact_row(dot_t, unit_back(mine_text_mapped, grad_caption), text_weight[...])
    grad_text_ref[...] = norm_back(mine_text_pool, gain_text_ref[...], back)


def call(kernel, out_shape, in_spaces, scratch, out_spaces=None, vmem=VMEM_LIMIT):
    many = isinstance(out_shape, (tuple, list))
    out_spaces = out_spaces or ([pltpu.VMEM] * (len(out_shape) if many else 1))
    out_specs = [pl.BlockSpec(memory_space=space) for space in out_spaces]
    return pl.pallas_call(
        kernel,
        out_shape=out_shape,
        in_specs=[pl.BlockSpec(memory_space=space) for space in in_spaces],
        out_specs=out_specs if many else out_specs[0],
        scratch_shapes=scratch,
        compiler_params=pltpu.CompilerParams(vmem_limit_bytes=vmem),
    )


def shape(dims, dtype):
    return jax.ShapeDtypeStruct(dims, dtype)


def send_all(copies, groups):
    return lax.all_to_all(copies, "dp", 0, 0, tiled=True, axis_index_groups=groups)


def on_device(
    video_tokens,
    text_states,
    caption_ids,
    pair_index,
    logit_scale,
    gain_spatial,
    gain_temporal,
    gain_video,
    gain_text,
    w_qkv_spatial,
    w_out_spatial,
    w_qkv_temporal,
    w_out_temporal,
    w_video,
    w_text,
):
    V, S, A = pltpu.VMEM, pltpu.SMEM, pl.ANY
    DMA = pltpu.SemaphoreType.DMA
    halves = (X, Y, 2, 16)
    tokens = video_tokens.reshape(256, D)
    place = lax.axis_index("dp").astype(jnp.int32).reshape(1)
    packed, own = call(
        pack_kernel,
        (shape((16, PACKED), BF16), shape((Y, 16, 3 * WIDTH), BF16)),
        (A,) * 7,
        [
            pltpu.VMEM(caption_ids.shape, jnp.int32),
            pltpu.VMEM(text_states.shape[1:], BF16),
            pltpu.VMEM(w_text.shape, BF16),
            pltpu.VMEM(w_out_spatial.shape, BF16),
            pltpu.VMEM(w_out_temporal.shape, BF16),
            pltpu.VMEM(w_qkv_spatial.shape, BF16),
            DMA((7,)),
        ],
        vmem=VMEM_WHOLE,
    )(
        caption_ids,
        text_states.reshape(text_states.shape[1:]),
        w_qkv_temporal,
        w_text,
        w_out_spatial,
        w_out_temporal,
        w_qkv_spatial,
    )
    barrier = lax.optimization_barrier
    gather = functools.partial(lax.all_gather, axis_name="dp", axis=0, tiled=True)
    own = send_all(own, ROWS_OF_Y)
    packed = gather(packed, axis_index_groups=ROWS_OF_X)
    own, packed, w_video = barrier((own, packed, w_video))
    early = gather(packed, axis_index_groups=ROWS_OF_YC).reshape(Y, 2, X, 16, PACKED)
    own = jnp.broadcast_to(own.reshape(1, Y * 16, 3 * WIDTH), (X, Y * 16, 3 * WIDTH))
    own = send_all(own, ROWS_OF_X)
    late = gather(w_video, axis_index_groups=ROWS_OF_X)
    own, late, dealing = barrier((own, late, tokens.reshape(FRAMES, 32, D)))
    late = gather(late, axis_index_groups=ROWS_OF_YC).reshape(Y, 2, X, 16, E)
    by_patch = lax.all_to_all(dealing, "frame", 0, 0, tiled=True)
    own = own.reshape(X * Y, 16, 3 * WIDTH)
    other = lax.ppermute(own, "dp", OTHER_CORE)

    mixed = call(
        spatial_kernel,
        shape((256, WIDTH), BF16),
        (S, A, V, A, A),
        [
            pltpu.VMEM((256, D), BF16),
            pltpu.VMEM((X * Y, 2, 16, 3 * WIDTH), BF16),
            pltpu.VMEM((256, 3 * WIDTH), BF16),
            DMA((3,)),
        ],
    )(place % 2, tokens, gain_spatial.reshape(1, D), own, other)
    mixed, by_patch = barrier((mixed, by_patch))
    mixed = lax.all_to_all(mixed.reshape(FRAMES, 32, WIDTH), "frame", 0, 0, tiled=True)
    layer_out, pool = call(
        temporal_kernel,
        (shape((256, D), BF16), shape((FRAMES, 8, 128), F32)),
        (V, V, V, A),
        [
            pltpu.VMEM(halves + (3 * WIDTH,), BF16),
            pltpu.VMEM(halves + (D,), BF16),
            pltpu.VMEM((256, 3 * WIDTH), BF16),
            pltpu.VMEM((256, WIDTH), BF16),
            DMA((2, 2 * Y)),
        ],
    )(mixed.reshape(256, WIDTH), by_patch.reshape(256, D), gain_temporal.reshape(1, D), early)
    text_pool, text_mapped, text_weight = call(
        text_kernel,
        (shape((64, DT), F32), shape((64, E), F32), shape((DT, E), BF16)),
        (V, A),
        [pltpu.VMEM(halves + (E,), BF16), DMA((2 * Y,))],
    )(gain_text.reshape(1, DT), early)
    pool = lax.all_to_all(pool, "frame", 0, 0, tiled=True)
    pool = call(spread_kernel, shape((64, 8, 128), F32), (V,), [])(pool)
    pooled = lax.all_to_all(pool, "dp", 0, 0, tiled=True)
    video_loss, text_loss, grad_pooled, grad_text = call(
        loss_kernel,
        (shape((1,), F32), shape((1,), F32), shape((1, D), F32), shape((1, DT), F32)),
        (S, S, V, V, V, V, A, V, V, A),
        [
            pltpu.VMEM(halves + (E,), BF16),
            pltpu.VMEM((DT, E), BF16),
            pltpu.VMEM((64, D), F32),
            DMA((2 * Y + 1,)),
        ],
        (S, S, V, V),
        vmem=VMEM_MOST,
    )(
        place,
        logit_scale,
        pair_index.reshape(64, 1),
        pooled,
        text_pool,
        text_mapped,
        text_weight,
        gain_video.reshape(1, D),
        gain_text.reshape(1, DT),
        late,
    )
    return (layer_out.reshape(1, 8, 32, D), video_loss, text_loss, grad_pooled, grad_text)


def solution(mesh):
    placed = (
        P("dp", "frame", None, None),
        P("dp", None, None),
        P("dp", None),
        P(),
        P(),
        P(),
        P(),
        P(),
        P(),
        P("dp", None),
        P("dp", None),
        P("dp", None),
        P("dp", None),
        P("dp", None),
        P("dp", None),
    )
    return jax.shard_map(
        on_device,
        mesh=mesh,
        in_specs=placed,
        out_specs=(P("dp", None, "frame", None), P("dp"), P("dp"), P("dp", None), P("dp", None)),
        check_vma=False,
    )
```

```python
import functools

import jax
import jax.numpy as jnp
from jax import lax
from jax.experimental import pallas as pl
from jax.experimental.pallas import tpu as pltpu
from jax.sharding import PartitionSpec as P

HEADS = 8
HD = 64
WIDTH = HEADS * HD
D = 1024
DT = 768
E = 768
NORM_EPS = 1e-05
UNIT_EPS = 1e-06
F32 = jnp.float32
BF16 = jnp.bfloat16
MIB = 1024 * 1024
VMEM_LIMIT = 48 * MIB
VMEM_WHOLE = 63 * MIB
VMEM_MOST = 52 * MIB

QKV = 0
OUT = 1536
PACKED_S = 2048
W_TEXT = 2048
W_VIDEO = 2816
PACKED_T = 3584

X, Y = 4, 8
ROWS_OF_X = [[(x * Y + y) * 2 + c for x in range(X)] for y in range(Y) for c in range(2)]
ROWS_OF_Y = [[(x * Y + y) * 2 + c for y in range(Y)] for x in range(X) for c in range(2)]
ROWS_OF_YC = [[(x * Y + y) * 2 + c for y in range(Y) for c in range(2)] for x in range(X)]
OTHER_CORE = [(i, i ^ 1) for i in range(2 * X * Y)]
FRAMES = 8


def dot(a, b):
    return lax.dot_general(a, b, (((1,), (0,)), ((), ())), preferred_element_type=F32)


def dot_t(a, b):
    return lax.dot_general(a, b, (((1,), (1,)), ((), ())), preferred_element_type=F32)


def pieces(a):
    first = a.astype(BF16)
    rest = a - first.astype(F32)
    second = rest.astype(BF16)
    third = (rest - second.astype(F32)).astype(BF16)
    return first, second, third


def exact(dot_fn, a, weight):
    rows = a.shape[0]
    parts = dot_fn(jnp.concatenate(pieces(a), axis=0), weight)
    return parts[2 * rows :] + parts[rows : 2 * rows] + parts[:rows]


def exact_row(dot_fn, a, weight):
    rows = lax.broadcasted_iota(jnp.int32, (16, a.shape[1]), 0)
    first, second, third = (piece.astype(F32) for piece in pieces(a))
    block = jnp.where(rows == 0, third, jnp.where(rows == 1, second, jnp.where(rows == 2, first, 0.0)))
    return jnp.sum(dot_fn(block.astype(BF16), weight), axis=0, keepdims=True)


def layer_norm(values, gain):
    center = values - jnp.mean(values, axis=-1, keepdims=True)
    spread = jnp.mean(center * center, axis=-1, keepdims=True)
    return center * lax.rsqrt(spread + NORM_EPS) * gain


def attend_pair(query, key, value, mask):
    low = lax.broadcasted_iota(jnp.int32, query.shape, 1) < HD
    mixed = []
    for lanes in (low, ~low):
        scores = dot_t(jnp.where(lanes, query, jnp.zeros_like(query)), key) * (HD**-0.5)
        if mask is not None:
            scores = jnp.where(mask, scores, -1e30)
        weight = jnp.exp(scores - jnp.max(scores, axis=-1, keepdims=True))
        probs = weight * (1.0 / jnp.sum(weight, axis=-1, keepdims=True))
        mixed.append(dot(probs.astype(BF16), value))
    return jnp.where(low, mixed[0], mixed[1]).astype(BF16)


def attend(packed_ref, mixed_ref, mask):
    for at in range(0, WIDTH, 2 * HD):
        query, key, value = (
            packed_ref[:, part * WIDTH + at : part * WIDTH + at + 2 * HD] for part in range(3)
        )
        mixed_ref[:, at : at + 2 * HD] = attend_pair(query, key, value, mask)


def out_halves(gathered):
    halves = gathered.astype(F32).reshape(64, 2, 8, D // 2)
    return [halves[:, side].reshape(WIDTH, D // 2).astype(BF16) for side in range(2)]


def spatial_kernel(
    core_ref, tokens_ref, gain_ref, own_ref, other_ref, spatial_ref, qkv, outs, packed, mixed, sems
):
    core = core_ref[0]
    copies = []
    for half, (ref, place) in enumerate(((own_ref, core), (other_ref, 1 - core))):
        for part, (first, target) in enumerate(((QKV, qkv), (OUT, outs))):
            copies.append(
                pltpu.make_async_copy(
                    ref.at[:, :, first : first + target.shape[-1]],
                    target.at[:, place],
                    sems.at[2 * half + part],
                )
            )
    for copy in copies:
        copy.start()
    tokens = tokens_ref[...].astype(F32)
    normed = layer_norm(tokens, gain_ref[...]).astype(BF16)
    copies[0].wait()
    copies[2].wait()
    packed[...] = dot(normed, qkv[...].reshape(D, 3 * WIDTH)).astype(BF16)
    attend(packed, mixed, None)
    copies[1].wait()
    copies[3].wait()
    for side, weight in enumerate(out_halves(outs[...])):
        columns = slice(side * (D // 2), (side + 1) * (D // 2))
        spatial_ref[:, columns] = (
            tokens_ref[:, columns].astype(F32) + dot(mixed[...], weight)
        ).astype(BF16)


def gather_rows(weights_ref, first, target, sems):
    width = target.shape[-1]
    return [
        pltpu.make_async_copy(
            weights_ref.at[y, c, :, :, first : first + width], target.at[:, y, c], sems.at[2 * y + c]
        )
        for y in range(Y)
        for c in range(2)
    ]


def pack_kernel(
    ids_ref, states_ref, qkv_ref, text_ref, out_s_ref, out_t_ref, video_ref, spatial_ref,
    packed_ref, copies_ref,
    ids_here, states_here, text_here, out_s_here, out_t_here, sems,
):
    pairs = (
        (spatial_ref, copies_ref.at[0, :, QKV : QKV + 3 * WIDTH]),
        (ids_ref, ids_here),
        (states_ref, states_here),
        (text_ref, text_here),
        (out_s_ref, out_s_here),
        (out_t_ref, out_t_here),
        (qkv_ref, packed_ref.at[:, QKV : QKV + 3 * WIDTH]),
        (video_ref, packed_ref.at[:, W_VIDEO : W_VIDEO + E]),
    )
    copies = [pltpu.make_async_copy(*pair, sems.at[i]) for i, pair in enumerate(pairs)]
    for copy in copies:
        copy.start()
    for copy in copies:
        copy.wait()
    for source, target in ((out_s_here, copies_ref.at[0]), (out_t_here, packed_ref)):
        rows = source[...].astype(F32)
        rows = jnp.concatenate([rows[:, : D // 2], rows[:, D // 2 :]], axis=0)
        target[:, OUT : OUT + D // 2] = rows.astype(BF16)
    for copy in range(1, Y):
        copies_ref[copy] = copies_ref[0]
    ids = ids_here[...]
    positions = lax.broadcasted_iota(jnp.int32, ids.shape, 1)
    end_place = jnp.min(jnp.where(ids == jnp.max(ids), positions, ids.shape[1]))
    states = states_here[...].astype(F32)
    rows = lax.broadcasted_iota(jnp.int32, states.shape, 0)
    text_row = jnp.sum(jnp.where(rows == end_place, states, 0.0), axis=0, keepdims=True)
    text = jnp.concatenate([text_here[...].astype(F32), jnp.zeros((4, E), F32)], axis=0)
    place = lax.broadcasted_iota(jnp.int32, text.shape, 0)
    text = jnp.where(place < 12, text, jnp.where(place == 12, text_row, 0.0))
    packed_ref[:, W_TEXT : W_TEXT + E] = text.astype(BF16)


def temporal_kernel(
    spatial_ref, gain_ref, weights_ref, out_ref, pool_ref, qkv, outs, packed, mixed, sems
):
    copies_qkv = gather_rows(weights_ref, QKV, qkv, sems.at[0])
    copies_out = gather_rows(weights_ref, OUT, outs, sems.at[1])
    for copy in copies_qkv + copies_out:
        copy.start()
    rows = spatial_ref.shape[0]
    spatial = spatial_ref[...].astype(F32)
    normed = layer_norm(spatial, gain_ref[...]).astype(BF16)
    for copy in copies_qkv:
        copy.wait()
    packed[...] = dot(normed, qkv[...].reshape(D, 3 * WIDTH)).astype(BF16)
    patches = rows // FRAMES
    place = lax.broadcasted_iota(jnp.int32, (rows, rows), 0) % patches
    attend(packed, mixed, place == lax.broadcasted_iota(jnp.int32, (rows, rows), 1) % patches)
    for copy in copies_out:
        copy.wait()
    half = D // 2
    for side, weight in enumerate(out_halves(outs[...])):
        columns = slice(side * half, (side + 1) * half)
        output = (spatial_ref[:, columns].astype(F32) + dot(mixed[...], weight)).astype(BF16)
        out_ref[:, columns] = output
        total = jnp.sum(output.astype(F32), axis=0, keepdims=True)
        for chunk in range(half // 128):
            pool_ref[:, side * (half // 128) + chunk, :] = jnp.broadcast_to(
                total[:, chunk * 128 : (chunk + 1) * 128], (FRAMES, 128)
            )


def spread_kernel(parts_ref, every_ref):
    mine = jnp.sum(parts_ref[...], axis=0) * (1.0 / (8 * 256))
    every_ref[...] = jnp.broadcast_to(mine[None], every_ref.shape)


def text_kernel(
    gain_ref, weights_ref, pool_ref, mapped_ref, weight_ref, gathered, sems
):
    copies = gather_rows(weights_ref, W_TEXT, gathered, sems)
    for copy in copies:
        copy.start()
    for copy in copies:
        copy.wait()
    packed = gathered[...].reshape(D, E)
    column = lax.broadcasted_iota(jnp.int32, (DT, D), 1)
    place = column % 16
    row = jnp.where(place < 12, (column // 16) * 12 + place, -1)
    pick = (row == lax.broadcasted_iota(jnp.int32, (DT, D), 0)).astype(BF16)
    weight = dot(pick, packed).astype(BF16)
    weight_ref[...] = weight
    column = lax.broadcasted_iota(jnp.int32, (64, D), 1)
    pick = (column == 16 * lax.broadcasted_iota(jnp.int32, (64, D), 0) + 12).astype(BF16)
    pool = dot(pick, packed)
    pool_ref[...] = pool
    mapped_ref[...] = exact(dot, layer_norm(pool, gain_ref[...]), weight)


def unit_rows(values):
    return values * lax.rsqrt(jnp.sum(values * values, axis=-1, keepdims=True) + UNIT_EPS)


def unit_back(mapped, grad):
    scale = lax.rsqrt(jnp.sum(mapped * mapped, axis=-1, keepdims=True) + UNIT_EPS)
    along = jnp.sum(mapped * grad, axis=-1, keepdims=True)
    return scale * grad - mapped * (scale * scale * scale * along)


def norm_back(values, gain, grad):
    center = values - jnp.mean(values, axis=-1, keepdims=True)
    scale = lax.rsqrt(jnp.mean(center * center, axis=-1, keepdims=True) + NORM_EPS)
    grad = grad * gain
    unit = center * scale
    along = jnp.mean(grad * unit, axis=-1, keepdims=True)
    return scale * (grad - jnp.mean(grad, axis=-1, keepdims=True) - unit * along)


def loss_kernel(
    place_ref,
    scale_ref,
    pairs_ref,
    pooled_ref,
    text_pool_ref,
    text_mapped_ref,
    text_weight_ref,
    gain_video_ref,
    gain_text_ref,
    weights_ref,
    video_loss_ref,
    text_loss_ref,
    grad_pooled_ref,
    grad_text_ref,
    gathered,
    text_weight,
    pooled_all,
    sems,
):
    me = place_ref[0]
    copies = gather_rows(weights_ref, W_VIDEO, gathered, sems)
    copy_text = pltpu.make_async_copy(text_weight_ref, text_weight, sems.at[2 * Y])
    for copy in copies + [copy_text]:
        copy.start()
    scale = scale_ref[0]
    for chunk in range(D // 128):
        pooled_all[:, chunk * 128 : (chunk + 1) * 128] = pooled_ref[:, chunk, :]
    gain = gain_video_ref[...]
    normed = layer_norm(pooled_all[...], gain)
    for copy in copies:
        copy.wait()
    weight = gathered[...].reshape(D, E)
    mapped = exact(dot, normed, weight)
    video = unit_rows(mapped)
    text_mapped = text_mapped_ref[...]
    text = unit_rows(text_mapped)
    logits = scale * lax.dot_general(
        video, text, (((1,), (1,)), ((), ())), precision=lax.Precision.HIGHEST,
        preferred_element_type=F32,
    )
    count = logits.shape[0]
    rows = lax.broadcasted_iota(jnp.int32, (count, count), 0)
    columns = lax.broadcasted_iota(jnp.int32, (count, count), 1)
    match = pairs_ref[...] == columns
    row_top = jnp.max(logits, axis=1, keepdims=True)
    row_exp = jnp.exp(logits - row_top)
    row_sum = jnp.sum(row_exp, axis=1, keepdims=True)
    col_top = jnp.max(logits, axis=0, keepdims=True)
    col_exp = jnp.exp(logits - col_top)
    col_sum = jnp.sum(col_exp, axis=0, keepdims=True)
    positive = jnp.where(match, logits, 0.0)
    video_loss = 0.5 * (row_top + jnp.log(row_sum) - jnp.sum(positive, axis=1, keepdims=True))
    text_loss = 0.5 * (col_top + jnp.log(col_sum) - jnp.sum(positive, axis=0, keepdims=True))
    mine_row = lax.broadcasted_iota(jnp.int32, (count, 1), 0) == me
    mine_col = lax.broadcasted_iota(jnp.int32, (1, count), 1) == me
    video_loss_ref[0] = jnp.sum(jnp.where(mine_row, video_loss, 0.0))
    text_loss_ref[0] = jnp.sum(jnp.where(mine_col, text_loss, 0.0))
    slope = (0.5 * scale) * (row_exp / row_sum + col_exp / col_sum - 2.0 * match.astype(F32))
    row_slope = jnp.sum(jnp.where(rows == me, slope, 0.0), axis=0, keepdims=True)
    row_slope = jnp.sum(jnp.where(rows == columns, row_slope, 0.0), axis=1, keepdims=True)
    col_slope = jnp.sum(jnp.where(columns == me, slope, 0.0), axis=1, keepdims=True)
    grad_video = jnp.sum(row_slope * text, axis=0, keepdims=True)
    grad_caption = jnp.sum(col_slope * video, axis=0, keepdims=True)
    mine_mapped = jnp.sum(jnp.where(mine_row, mapped, 0.0), axis=0, keepdims=True)
    mine_text_mapped = jnp.sum(jnp.where(mine_row, text_mapped, 0.0), axis=0, keepdims=True)
    mine_pooled = jnp.sum(jnp.where(mine_row, pooled_all[...], 0.0), axis=0, keepdims=True)
    mine_text_pool = jnp.sum(jnp.where(mine_row, text_pool_ref[...], 0.0), axis=0, keepdims=True)
    back = exact_row(dot_t, unit_back(mine_mapped, grad_video), weight)
    grad_pooled_ref[...] = norm_back(mine_pooled, gain, back)
    copy_text.wait()
    back = exact_row(dot_t, unit_back(mine_text_mapped, grad_caption), text_weight[...])
    grad_text_ref[...] = norm_back(mine_text_pool, gain_text_ref[...], back)


def call(kernel, out_shape, in_spaces, scratch, out_spaces=None, vmem=VMEM_LIMIT):
    many = isinstance(out_shape, (tuple, list))
    out_spaces = out_spaces or ([pltpu.VMEM] * (len(out_shape) if many else 1))
    out_specs = [pl.BlockSpec(memory_space=space) for space in out_spaces]
    return pl.pallas_call(
        kernel,
        out_shape=out_shape,
        in_specs=[pl.BlockSpec(memory_space=space) for space in in_spaces],
        out_specs=out_specs if many else out_specs[0],
        scratch_shapes=scratch,
        compiler_params=pltpu.CompilerParams(vmem_limit_bytes=vmem),
    )


def shape(dims, dtype):
    return jax.ShapeDtypeStruct(dims, dtype)


def send_all(copies, groups):
    return lax.all_to_all(copies, "dp", 0, 0, tiled=True, axis_index_groups=groups)


def on_device(
    video_tokens,
    text_states,
    caption_ids,
    pair_index,
    logit_scale,
    gain_spatial,
    gain_temporal,
    gain_video,
    gain_text,
    w_qkv_spatial,
    w_out_spatial,
    w_qkv_temporal,
    w_out_temporal,
    w_video,
    w_text,
):
    V, S, A = pltpu.VMEM, pltpu.SMEM, pl.ANY
    DMA = pltpu.SemaphoreType.DMA
    halves = (X, Y, 2, 16)
    tokens = video_tokens.reshape(256, D)
    place = lax.axis_index("dp").astype(jnp.int32).reshape(1)
    packed, own = call(
        pack_kernel,
        (shape((16, PACKED_T), BF16), shape((Y, 16, PACKED_S), BF16)),
        (A,) * 8,
        [
            pltpu.VMEM(caption_ids.shape, jnp.int32),
            pltpu.VMEM(text_states.shape[1:], BF16),
            pltpu.VMEM(w_text.shape, BF16),
            pltpu.VMEM(w_out_spatial.shape, BF16),
            pltpu.VMEM(w_out_temporal.shape, BF16),
            DMA((8,)),
        ],
        vmem=VMEM_WHOLE,
    )(
        caption_ids,
        text_states.reshape(text_states.shape[1:]),
        w_qkv_temporal,
        w_text,
        w_out_spatial,
        w_out_temporal,
        w_video,
        w_qkv_spatial,
    )
    barrier = lax.optimization_barrier
    gather = functools.partial(lax.all_gather, axis_name="dp", axis=0, tiled=True)
    own = send_all(own, ROWS_OF_Y)
    packed = gather(packed, axis_index_groups=ROWS_OF_X)
    own, packed = barrier((own, packed))
    weights = gather(packed, axis_index_groups=ROWS_OF_YC).reshape(Y, 2, X, 16, PACKED_T)
    own = jnp.broadcast_to(own.reshape(1, Y * 16, PACKED_S), (X, Y * 16, PACKED_S))
    own = send_all(own, ROWS_OF_X).reshape(X * Y, 16, PACKED_S)
    other = lax.ppermute(own, "dp", OTHER_CORE)

    spatial = call(
        spatial_kernel,
        shape((256, D), BF16),
        (S, V, V, A, A),
        [
            pltpu.VMEM((X * Y, 2, 16, 3 * WIDTH), BF16),
            pltpu.VMEM((X * Y, 2, 16, D // 2), BF16),
            pltpu.VMEM((256, 3 * WIDTH), BF16),
            pltpu.VMEM((256, WIDTH), BF16),
            DMA((4,)),
        ],
    )(place % 2, tokens, gain_spatial.reshape(1, D), own, other)
    spatial = lax.all_to_all(spatial.reshape(FRAMES, 32, D), "frame", 0, 0, tiled=True)
    layer_out, pool = call(
        temporal_kernel,
        (shape((256, D), BF16), shape((FRAMES, 8, 128), F32)),
        (V, V, A),
        [
            pltpu.VMEM(halves + (3 * WIDTH,), BF16),
            pltpu.VMEM(halves + (D // 2,), BF16),
            pltpu.VMEM((256, 3 * WIDTH), BF16),
            pltpu.VMEM((256, WIDTH), BF16),
            DMA((2, 2 * Y)),
        ],
    )(spatial.reshape(256, D), gain_temporal.reshape(1, D), weights)
    text_pool, text_mapped, text_weight = call(
        text_kernel,
        (shape((64, DT), F32), shape((64, E), F32), shape((DT, E), BF16)),
        (V, A),
        [pltpu.VMEM(halves + (E,), BF16), DMA((2 * Y,))],
    )(gain_text.reshape(1, DT), weights)
    pool = lax.all_to_all(pool, "frame", 0, 0, tiled=True)
    pool = call(spread_kernel, shape((64, 8, 128), F32), (V,), [])(pool)
    pooled = lax.all_to_all(pool, "dp", 0, 0, tiled=True)
    video_loss, text_loss, grad_pooled, grad_text = call(
        loss_kernel,
        (shape((1,), F32), shape((1,), F32), shape((1, D), F32), shape((1, DT), F32)),
        (S, S, V, V, V, V, A, V, V, A),
        [
            pltpu.VMEM(halves + (E,), BF16),
            pltpu.VMEM((DT, E), BF16),
            pltpu.VMEM((64, D), F32),
            DMA((2 * Y + 1,)),
        ],
        (S, S, V, V),
        vmem=VMEM_MOST,
    )(
        place,
        logit_scale,
        pair_index.reshape(64, 1),
        pooled,
        text_pool,
        text_mapped,
        text_weight,
        gain_video.reshape(1, D),
        gain_text.reshape(1, DT),
        weights,
    )
    return (layer_out.reshape(1, 8, 32, D), video_loss, text_loss, grad_pooled, grad_text)


def solution(mesh):
    placed = (
        P("dp", "frame", None, None),
        P("dp", None, None),
        P("dp", None),
        P(),
        P(),
        P(),
        P(),
        P(),
        P(),
        P("dp", None),
        P("dp", None),
        P("dp", None),
        P("dp", None),
        P("dp", None),
        P("dp", None),
    )
    return jax.shard_map(
        on_device,
        mesh=mesh,
        in_specs=placed,
        out_specs=(P("dp", None, "frame", None), P("dp"), P("dp"), P("dp", None), P("dp", None)),
        check_vma=False,
    )
```

```python
import functools

import jax
import jax.numpy as jnp
from jax import lax
from jax.experimental import pallas as pl
from jax.experimental.pallas import tpu as pltpu
from jax.sharding import PartitionSpec as P

HEADS = 8
HD = 64
WIDTH = HEADS * HD
D = 1024
DT = 768
E = 768
NORM_EPS = 1e-05
UNIT_EPS = 1e-06
F32 = jnp.float32
BF16 = jnp.bfloat16
MIB = 1024 * 1024
VMEM_LIMIT = 48 * MIB
VMEM_WHOLE = 63 * MIB
VMEM_SMALL = 24 * MIB

QKV = 0
OUT = 1536
PACKED_S = 2048
W_TEXT = 2048
W_VIDEO = 2816
PACKED_T = 3584

X, Y = 4, 8
ROWS_OF_X = [[(x * Y + y) * 2 + c for x in range(X)] for y in range(Y) for c in range(2)]
ROWS_OF_Y = [[(x * Y + y) * 2 + c for y in range(Y)] for x in range(X) for c in range(2)]
ROWS_OF_YC = [[(x * Y + y) * 2 + c for y in range(Y) for c in range(2)] for x in range(X)]
OTHER_CORE = [(i, i ^ 1) for i in range(2 * X * Y)]
FRAMES = 8


def dot(a, b):
    return lax.dot_general(a, b, (((1,), (0,)), ((), ())), preferred_element_type=F32)


def dot_t(a, b):
    return lax.dot_general(a, b, (((1,), (1,)), ((), ())), preferred_element_type=F32)


def pieces(a):
    first = a.astype(BF16)
    rest = a - first.astype(F32)
    second = rest.astype(BF16)
    third = (rest - second.astype(F32)).astype(BF16)
    return first, second, third


def exact(dot_fn, a, weight):
    rows = a.shape[0]
    parts = dot_fn(jnp.concatenate(pieces(a), axis=0), weight)
    return parts[2 * rows :] + parts[rows : 2 * rows] + parts[:rows]


def exact_row(dot_fn, a, weight):
    rows = lax.broadcasted_iota(jnp.int32, (16, a.shape[1]), 0)
    first, second, third = (piece.astype(F32) for piece in pieces(a))
    block = jnp.where(rows == 0, third, jnp.where(rows == 1, second, jnp.where(rows == 2, first, 0.0)))
    return jnp.sum(dot_fn(block.astype(BF16), weight), axis=0, keepdims=True)


def layer_norm(values, gain):
    center = values - jnp.mean(values, axis=-1, keepdims=True)
    spread = jnp.mean(center * center, axis=-1, keepdims=True)
    return center * lax.rsqrt(spread + NORM_EPS) * gain


def attend_pair(query, key, value, mask):
    low = lax.broadcasted_iota(jnp.int32, query.shape, 1) < HD
    mixed = []
    for lanes in (low, ~low):
        scores = dot_t(jnp.where(lanes, query, jnp.zeros_like(query)), key) * (HD**-0.5)
        if mask is not None:
            scores = jnp.where(mask, scores, -1e30)
        weight = jnp.exp(scores - jnp.max(scores, axis=-1, keepdims=True))
        probs = weight * (1.0 / jnp.sum(weight, axis=-1, keepdims=True))
        mixed.append(dot(probs.astype(BF16), value))
    return jnp.where(low, mixed[0], mixed[1]).astype(BF16)


def attend(packed_ref, mixed_ref, mask):
    for at in range(0, WIDTH, 2 * HD):
        query, key, value = (
            packed_ref[:, part * WIDTH + at : part * WIDTH + at + 2 * HD] for part in range(3)
        )
        mixed_ref[:, at : at + 2 * HD] = attend_pair(query, key, value, mask)


def out_halves(gathered):
    halves = gathered.astype(F32).reshape(64, 2, 8, D // 2)
    return [halves[:, side].reshape(WIDTH, D // 2).astype(BF16) for side in range(2)]


def norm_kernel(core_ref, tokens_ref, gain_ref, own_ref, other_ref):
    normed = layer_norm(tokens_ref[...].astype(F32), gain_ref[...]).astype(BF16)
    for half, target in enumerate((own_ref, other_ref)):
        core = core_ref[0] if half == 0 else 1 - core_ref[0]
        row = lax.broadcasted_iota(jnp.int32, (D, D // 2), 0)
        column = lax.broadcasted_iota(jnp.int32, (D, D // 2), 1)
        pick = row == (column // 16) * 32 + core * 16 + column % 16
        target[...] = dot(normed, pick.astype(BF16)).astype(BF16)


def own_kernel(normed_ref, own_ref, part_ref):
    part_ref[...] = dot(
        normed_ref[...], own_ref[:, :, QKV : QKV + 3 * WIDTH].reshape(D // 2, 3 * WIDTH)
    )


def spatial_kernel(
    core_ref, tokens_ref, normed_ref, part_ref, own_ref, other_ref, spatial_ref, packed, mixed
):
    other = other_ref[:, :, QKV : QKV + 3 * WIDTH].reshape(D // 2, 3 * WIDTH)
    packed[...] = (part_ref[...] + dot(normed_ref[...], other)).astype(BF16)
    attend(packed, mixed, None)
    halves = (X * Y, 2, 8, D // 2)
    own = own_ref[:, :, OUT : OUT + D // 2].astype(F32).reshape(halves)
    other = other_ref[:, :, OUT : OUT + D // 2].astype(F32).reshape(halves)
    first = core_ref[0] == 0
    outs = jnp.stack([jnp.where(first, own, other), jnp.where(first, other, own)], axis=1)
    for side in range(2):
        columns = slice(side * (D // 2), (side + 1) * (D // 2))
        weight = outs[:, :, side].reshape(WIDTH, D // 2).astype(BF16)
        spatial_ref[:, columns] = (
            tokens_ref[:, columns].astype(F32) + dot(mixed[...], weight)
        ).astype(BF16)


def gather_rows(weights_ref, first, target, sems):
    width = target.shape[-1]
    return [
        pltpu.make_async_copy(
            weights_ref.at[y, c, :, :, first : first + width], target.at[:, y, c], sems.at[2 * y + c]
        )
        for y in range(Y)
        for c in range(2)
    ]


def pack_kernel(
    ids_ref, states_ref, qkv_ref, text_ref, out_s_ref, out_t_ref, video_ref, spatial_ref,
    packed_ref, copies_ref,
    ids_here, states_here, text_here, out_s_here, out_t_here, sems,
):
    pairs = (
        (spatial_ref, copies_ref.at[0, :, QKV : QKV + 3 * WIDTH]),
        (ids_ref, ids_here),
        (states_ref, states_here),
        (text_ref, text_here),
        (out_s_ref, out_s_here),
        (out_t_ref, out_t_here),
        (qkv_ref, packed_ref.at[:, QKV : QKV + 3 * WIDTH]),
        (video_ref, packed_ref.at[:, W_VIDEO : W_VIDEO + E]),
    )
    copies = [pltpu.make_async_copy(*pair, sems.at[i]) for i, pair in enumerate(pairs)]
    for copy in copies:
        copy.start()
    for copy in copies:
        copy.wait()
    for source, target in ((out_s_here, copies_ref.at[0]), (out_t_here, packed_ref)):
        rows = source[...].astype(F32)
        rows = jnp.concatenate([rows[:, : D // 2], rows[:, D // 2 :]], axis=0)
        target[:, OUT : OUT + D // 2] = rows.astype(BF16)
    for copy in range(1, Y):
        copies_ref[copy] = copies_ref[0]
    ids = ids_here[...]
    positions = lax.broadcasted_iota(jnp.int32, ids.shape, 1)
    end_place = jnp.min(jnp.where(ids == jnp.max(ids), positions, ids.shape[1]))
    states = states_here[...].astype(F32)
    rows = lax.broadcasted_iota(jnp.int32, states.shape, 0)
    text_row = jnp.sum(jnp.where(rows == end_place, states, 0.0), axis=0, keepdims=True)
    text = jnp.concatenate([text_here[...].astype(F32), jnp.zeros((4, E), F32)], axis=0)
    place = lax.broadcasted_iota(jnp.int32, text.shape, 0)
    text = jnp.where(place < 12, text, jnp.where(place == 12, text_row, 0.0))
    packed_ref[:, W_TEXT : W_TEXT + E] = text.astype(BF16)


def temporal_kernel(
    spatial_ref, gain_ref, weights_ref, out_ref, pool_ref, qkv, outs, packed, mixed, sems
):
    copies_qkv = gather_rows(weights_ref, QKV, qkv, sems.at[0])
    copies_out = gather_rows(weights_ref, OUT, outs, sems.at[1])
    for copy in copies_qkv + copies_out:
        copy.start()
    rows = spatial_ref.shape[0]
    spatial = spatial_ref[...].astype(F32)
    normed = layer_norm(spatial, gain_ref[...]).astype(BF16)
    for copy in copies_qkv:
        copy.wait()
    packed[...] = dot(normed, qkv[...].reshape(D, 3 * WIDTH)).astype(BF16)
    patches = rows // FRAMES
    place = lax.broadcasted_iota(jnp.int32, (rows, rows), 0) % patches
    attend(packed, mixed, place == lax.broadcasted_iota(jnp.int32, (rows, rows), 1) % patches)
    for copy in copies_out:
        copy.wait()
    half = D // 2
    for side, weight in enumerate(out_halves(outs[...])):
        columns = slice(side * half, (side + 1) * half)
        output = (spatial_ref[:, columns].astype(F32) + dot(mixed[...], weight)).astype(BF16)
        out_ref[:, columns] = output
        total = jnp.sum(output.astype(F32), axis=0, keepdims=True)
        for chunk in range(half // 128):
            pool_ref[:, side * (half // 128) + chunk, :] = jnp.broadcast_to(
                total[:, chunk * 128 : (chunk + 1) * 128], (FRAMES, 128)
            )


def spread_kernel(parts_ref, every_ref):
    mine = jnp.sum(parts_ref[...], axis=0) * (1.0 / (8 * 256))
    every_ref[...] = jnp.broadcast_to(mine[None], every_ref.shape)


def text_kernel(
    gain_ref, weights_ref, pool_ref, mapped_ref, weight_ref, video_ref, gathered, sems
):
    copies = gather_rows(weights_ref, W_TEXT, gathered, sems.at[0])
    copies_video = gather_rows(weights_ref, W_VIDEO, video_ref, sems.at[1])
    for copy in copies + copies_video:
        copy.start()
    for copy in copies:
        copy.wait()
    packed = gathered[...].reshape(D, E)
    column = lax.broadcasted_iota(jnp.int32, (DT, D), 1)
    place = column % 16
    row = jnp.where(place < 12, (column // 16) * 12 + place, -1)
    pick = (row == lax.broadcasted_iota(jnp.int32, (DT, D), 0)).astype(BF16)
    weight = dot(pick, packed).astype(BF16)
    weight_ref[...] = weight
    column = lax.broadcasted_iota(jnp.int32, (64, D), 1)
    pick = (column == 16 * lax.broadcasted_iota(jnp.int32, (64, D), 0) + 12).astype(BF16)
    pool = dot(pick, packed)
    pool_ref[...] = pool
    mapped_ref[...] = exact(dot, layer_norm(pool, gain_ref[...]), weight)
    for copy in copies_video:
        copy.wait()


def unit_rows(values):
    return values * lax.rsqrt(jnp.sum(values * values, axis=-1, keepdims=True) + UNIT_EPS)


def unit_back(mapped, grad):
    scale = lax.rsqrt(jnp.sum(mapped * mapped, axis=-1, keepdims=True) + UNIT_EPS)
    along = jnp.sum(mapped * grad, axis=-1, keepdims=True)
    return scale * grad - mapped * (scale * scale * scale * along)


def norm_back(values, gain, grad):
    center = values - jnp.mean(values, axis=-1, keepdims=True)
    scale = lax.rsqrt(jnp.mean(center * center, axis=-1, keepdims=True) + NORM_EPS)
    grad = grad * gain
    unit = center * scale
    along = jnp.mean(grad * unit, axis=-1, keepdims=True)
    return scale * (grad - jnp.mean(grad, axis=-1, keepdims=True) - unit * along)


def loss_kernel(
    place_ref,
    scale_ref,
    pairs_ref,
    pooled_ref,
    text_pool_ref,
    text_mapped_ref,
    text_weight_ref,
    gain_video_ref,
    gain_text_ref,
    video_weight_ref,
    video_loss_ref,
    text_loss_ref,
    grad_pooled_ref,
    grad_text_ref,
    pooled_all,
):
    me = place_ref[0]
    scale = scale_ref[0]
    for chunk in range(D // 128):
        pooled_all[:, chunk * 128 : (chunk + 1) * 128] = pooled_ref[:, chunk, :]
    gain = gain_video_ref[...]
    normed = layer_norm(pooled_all[...], gain)
    weight = video_weight_ref[...].reshape(D, E)
    mapped = exact(dot, normed, weight)
    video = unit_rows(mapped)
    text_mapped = text_mapped_ref[...]
    text = unit_rows(text_mapped)
    logits = scale * lax.dot_general(
        video, text, (((1,), (1,)), ((), ())), precision=lax.Precision.HIGHEST,
        preferred_element_type=F32,
    )
    count = logits.shape[0]
    rows = lax.broadcasted_iota(jnp.int32, (count, count), 0)
    columns = lax.broadcasted_iota(jnp.int32, (count, count), 1)
    match = pairs_ref[...] == columns
    row_top = jnp.max(logits, axis=1, keepdims=True)
    row_exp = jnp.exp(logits - row_top)
    row_sum = jnp.sum(row_exp, axis=1, keepdims=True)
    col_top = jnp.max(logits, axis=0, keepdims=True)
    col_exp = jnp.exp(logits - col_top)
    col_sum = jnp.sum(col_exp, axis=0, keepdims=True)
    positive = jnp.where(match, logits, 0.0)
    video_loss = 0.5 * (row_top + jnp.log(row_sum) - jnp.sum(positive, axis=1, keepdims=True))
    text_loss = 0.5 * (col_top + jnp.log(col_sum) - jnp.sum(positive, axis=0, keepdims=True))
    mine_row = lax.broadcasted_iota(jnp.int32, (count, 1), 0) == me
    mine_col = lax.broadcasted_iota(jnp.int32, (1, count), 1) == me
    video_loss_ref[0] = jnp.sum(jnp.where(mine_row, video_loss, 0.0))
    text_loss_ref[0] = jnp.sum(jnp.where(mine_col, text_loss, 0.0))
    slope = (0.5 * scale) * (row_exp / row_sum + col_exp / col_sum - 2.0 * match.astype(F32))
    row_slope = jnp.sum(jnp.where(rows == me, slope, 0.0), axis=0, keepdims=True)
    row_slope = jnp.sum(jnp.where(rows == columns, row_slope, 0.0), axis=1, keepdims=True)
    col_slope = jnp.sum(jnp.where(columns == me, slope, 0.0), axis=1, keepdims=True)
    grad_video = jnp.sum(row_slope * text, axis=0, keepdims=True)
    grad_caption = jnp.sum(col_slope * video, axis=0, keepdims=True)
    mine_mapped = jnp.sum(jnp.where(mine_row, mapped, 0.0), axis=0, keepdims=True)
    mine_text_mapped = jnp.sum(jnp.where(mine_row, text_mapped, 0.0), axis=0, keepdims=True)
    mine_pooled = jnp.sum(jnp.where(mine_row, pooled_all[...], 0.0), axis=0, keepdims=True)
    mine_text_pool = jnp.sum(jnp.where(mine_row, text_pool_ref[...], 0.0), axis=0, keepdims=True)
    back = exact_row(dot_t, unit_back(mine_mapped, grad_video), weight)
    grad_pooled_ref[...] = norm_back(mine_pooled, gain, back)
    back = exact_row(dot_t, unit_back(mine_text_mapped, grad_caption), text_weight_ref[...])
    grad_text_ref[...] = norm_back(mine_text_pool, gain_text_ref[...], back)


def call(kernel, out_shape, in_spaces, scratch, out_spaces=None, vmem=VMEM_LIMIT, flops=0):
    many = isinstance(out_shape, (tuple, list))
    out_spaces = out_spaces or ([pltpu.VMEM] * (len(out_shape) if many else 1))
    out_specs = [pl.BlockSpec(memory_space=space) for space in out_spaces]
    return pl.pallas_call(
        kernel,
        out_shape=out_shape,
        in_specs=[pl.BlockSpec(memory_space=space) for space in in_spaces],
        out_specs=out_specs if many else out_specs[0],
        scratch_shapes=scratch,
        compiler_params=pltpu.CompilerParams(vmem_limit_bytes=vmem),
        cost_estimate=pl.CostEstimate(flops=flops, bytes_accessed=0, transcendentals=0),
    )


def shape(dims, dtype):
    return jax.ShapeDtypeStruct(dims, dtype)


def send_all(copies, groups):
    return lax.all_to_all(copies, "dp", 0, 0, tiled=True, axis_index_groups=groups)


def on_device(
    video_tokens,
    text_states,
    caption_ids,
    pair_index,
    logit_scale,
    gain_spatial,
    gain_temporal,
    gain_video,
    gain_text,
    w_qkv_spatial,
    w_out_spatial,
    w_qkv_temporal,
    w_out_temporal,
    w_video,
    w_text,
):
    V, S, A = pltpu.VMEM, pltpu.SMEM, pl.ANY
    DMA = pltpu.SemaphoreType.DMA
    halves = (X, Y, 2, 16)
    tokens = video_tokens.reshape(256, D)
    place = lax.axis_index("dp").astype(jnp.int32).reshape(1)
    packed, own = call(
        pack_kernel,
        (shape((16, PACKED_T), BF16), shape((Y, 16, PACKED_S), BF16)),
        (A,) * 8,
        [
            pltpu.VMEM(caption_ids.shape, jnp.int32),
            pltpu.VMEM(text_states.shape[1:], BF16),
            pltpu.VMEM(w_text.shape, BF16),
            pltpu.VMEM(w_out_spatial.shape, BF16),
            pltpu.VMEM(w_out_temporal.shape, BF16),
            DMA((8,)),
        ],
        vmem=VMEM_WHOLE,
    )(
        caption_ids,
        text_states.reshape(text_states.shape[1:]),
        w_qkv_temporal,
        w_text,
        w_out_spatial,
        w_out_temporal,
        w_video,
        w_qkv_spatial,
    )
    barrier = lax.optimization_barrier
    gather = functools.partial(lax.all_gather, axis_name="dp", axis=0, tiled=True)
    own = send_all(own, ROWS_OF_Y)
    packed = gather(packed, axis_index_groups=ROWS_OF_X)
    own, packed = barrier((own, packed))
    weights = gather(packed, axis_index_groups=ROWS_OF_YC).reshape(Y, 2, X, 16, PACKED_T)
    own = jnp.broadcast_to(own.reshape(1, Y * 16, PACKED_S), (X, Y * 16, PACKED_S))
    own = send_all(own, ROWS_OF_X).reshape(X * Y, 16, PACKED_S)

    core = place % 2
    normed = call(
        norm_kernel, (shape((256, D // 2), BF16),) * 2, (S, V, V), [], flops=1 << 30
    )(core, tokens, gain_spatial.reshape(1, D))
    own, normed = barrier((own, normed))
    other = lax.ppermute(own, "dp", OTHER_CORE)
    part = call(own_kernel, shape((256, 3 * WIDTH), F32), (V, V), [], vmem=VMEM_SMALL, flops=1 << 30)(
        normed[0], own
    )
    spatial = call(
        spatial_kernel,
        shape((256, D), BF16),
        (S, V, V, V, V, V),
        [pltpu.VMEM((256, 3 * WIDTH), BF16), pltpu.VMEM((256, WIDTH), BF16)],
        vmem=VMEM_SMALL,
    )(core, tokens, normed[1], part, own, other)
    spatial = lax.all_to_all(spatial.reshape(FRAMES, 32, D), "frame", 0, 0, tiled=True)
    layer_out, pool = call(
        temporal_kernel,
        (shape((256, D), BF16), shape((FRAMES, 8, 128), F32)),
        (V, V, A),
        [
            pltpu.VMEM(halves + (3 * WIDTH,), BF16),
            pltpu.VMEM(halves + (D // 2,), BF16),
            pltpu.VMEM((256, 3 * WIDTH), BF16),
            pltpu.VMEM((256, WIDTH), BF16),
            DMA((2, 2 * Y)),
        ],
    )(spatial.reshape(256, D), gain_temporal.reshape(1, D), weights)
    text_pool, text_mapped, text_weight, video_weight = call(
        text_kernel,
        (
            shape((64, DT), F32),
            shape((64, E), F32),
            shape((DT, E), BF16),
            shape(halves + (E,), BF16),
        ),
        (V, A),
        [pltpu.VMEM(halves + (E,), BF16), DMA((2, 2 * Y))],
    )(gain_text.reshape(1, DT), weights)
    pool = lax.all_to_all(pool, "frame", 0, 0, tiled=True)
    pool = call(spread_kernel, shape((64, 8, 128), F32), (V,), [])(pool)
    pooled = lax.all_to_all(pool, "dp", 0, 0, tiled=True)
    video_loss, text_loss, grad_pooled, grad_text = call(
        loss_kernel,
        (shape((1,), F32), shape((1,), F32), shape((1, D), F32), shape((1, DT), F32)),
        (S, S, V, V, V, V, V, V, V, V),
        [pltpu.VMEM((64, D), F32)],
        (S, S, V, V),
        vmem=VMEM_SMALL,
    )(
        place,
        logit_scale,
        pair_index.reshape(64, 1),
        pooled,
        text_pool,
        text_mapped,
        text_weight,
        gain_video.reshape(1, D),
        gain_text.reshape(1, DT),
        video_weight,
    )
    return (layer_out.reshape(1, 8, 32, D), video_loss, text_loss, grad_pooled, grad_text)


def solution(mesh):
    placed = (
        P("dp", "frame", None, None),
        P("dp", None, None),
        P("dp", None),
        P(),
        P(),
        P(),
        P(),
        P(),
        P(),
        P("dp", None),
        P("dp", None),
        P("dp", None),
        P("dp", None),
        P("dp", None),
        P("dp", None),
    )
    return jax.shard_map(
        on_device,
        mesh=mesh,
        in_specs=placed,
        out_specs=(P("dp", None, "frame", None), P("dp"), P("dp"), P("dp", None), P("dp", None)),
        check_vma=False,
    )
```

```python
import functools

import jax
import jax.numpy as jnp
from jax import lax
from jax.experimental import pallas as pl
from jax.experimental.pallas import tpu as pltpu
from jax.sharding import PartitionSpec as P

HEADS = 8
HD = 64
WIDTH = HEADS * HD
D = 1024
DT = 768
E = 768
NORM_EPS = 1e-05
UNIT_EPS = 1e-06
F32 = jnp.float32
BF16 = jnp.bfloat16
MIB = 1024 * 1024
VMEM_LIMIT = 48 * MIB
VMEM_WHOLE = 63 * MIB
VMEM_SMALL = 24 * MIB

QKV = 0
OUT = 1536
PACKED_S = 2048
W_TEXT = 2048
W_VIDEO = 2816
PACKED_T = 3584

X, Y = 4, 8
ROWS_OF_X = [[(x * Y + y) * 2 + c for x in range(X)] for y in range(Y) for c in range(2)]
ROWS_OF_Y = [[(x * Y + y) * 2 + c for y in range(Y)] for x in range(X) for c in range(2)]
ROWS_OF_YC = [[(x * Y + y) * 2 + c for y in range(Y) for c in range(2)] for x in range(X)]
OTHER_CORE = [(i, i ^ 1) for i in range(2 * X * Y)]
X_UP = [(i, (i + 2 * Y) % (2 * X * Y)) for i in range(2 * X * Y)]
X_DOWN = [(i, (i - 2 * Y) % (2 * X * Y)) for i in range(2 * X * Y)]
STEPS = (0, X - 1, 1, 2)
BLOCK = Y * 16
FRAMES = 8


def dot(a, b):
    return lax.dot_general(a, b, (((1,), (0,)), ((), ())), preferred_element_type=F32)


def dot_t(a, b):
    return lax.dot_general(a, b, (((1,), (1,)), ((), ())), preferred_element_type=F32)


def pieces(a):
    first = a.astype(BF16)
    rest = a - first.astype(F32)
    second = rest.astype(BF16)
    third = (rest - second.astype(F32)).astype(BF16)
    return first, second, third


def exact(dot_fn, a, weight):
    rows = a.shape[0]
    parts = dot_fn(jnp.concatenate(pieces(a), axis=0), weight)
    return parts[2 * rows :] + parts[rows : 2 * rows] + parts[:rows]


def exact_row(dot_fn, a, weight):
    rows = lax.broadcasted_iota(jnp.int32, (16, a.shape[1]), 0)
    first, second, third = (piece.astype(F32) for piece in pieces(a))
    block = jnp.where(rows == 0, third, jnp.where(rows == 1, second, jnp.where(rows == 2, first, 0.0)))
    return jnp.sum(dot_fn(block.astype(BF16), weight), axis=0, keepdims=True)


def layer_norm(values, gain):
    center = values - jnp.mean(values, axis=-1, keepdims=True)
    spread = jnp.mean(center * center, axis=-1, keepdims=True)
    return center * lax.rsqrt(spread + NORM_EPS) * gain


def attend_pair(query, key, value, mask):
    low = lax.broadcasted_iota(jnp.int32, query.shape, 1) < HD
    mixed = []
    for lanes in (low, ~low):
        scores = dot_t(jnp.where(lanes, query, jnp.zeros_like(query)), key) * (HD**-0.5)
        if mask is not None:
            scores = jnp.where(mask, scores, -1e30)
        weight = jnp.exp(scores - jnp.max(scores, axis=-1, keepdims=True))
        probs = weight * (1.0 / jnp.sum(weight, axis=-1, keepdims=True))
        mixed.append(dot(probs.astype(BF16), value))
    return jnp.where(low, mixed[0], mixed[1]).astype(BF16)


def attend(packed_ref, mixed_ref, mask):
    for at in range(0, WIDTH, 2 * HD):
        query, key, value = (
            packed_ref[:, part * WIDTH + at : part * WIDTH + at + 2 * HD] for part in range(3)
        )
        mixed_ref[:, at : at + 2 * HD] = attend_pair(query, key, value, mask)


def out_halves(gathered):
    halves = gathered.astype(F32).reshape(64, 2, 8, D // 2)
    return [halves[:, side].reshape(WIDTH, D // 2).astype(BF16) for side in range(2)]


def sorted_rows(place_ref, half, depth, column):
    block = column // (Y * depth)
    step = jnp.zeros_like(block)
    for number, value in enumerate(STEPS):
        step = jnp.where(block == number, value, step)
    x = (place_ref[0] + step) % X
    core = place_ref[1] if half == 0 else 1 - place_ref[1]
    y = column // depth % Y
    return ((x * Y + y) * 2 + core) * depth + column % depth


def norm_kernel(place_ref, tokens_ref, gain_ref, own_ref, other_ref, pick_ref):
    normed = layer_norm(tokens_ref[...].astype(F32), gain_ref[...]).astype(BF16)
    for half, target in enumerate((own_ref, other_ref)):
        row = lax.broadcasted_iota(jnp.int32, (D, D // 2), 0)
        column = lax.broadcasted_iota(jnp.int32, (D, D // 2), 1)
        pick = row == sorted_rows(place_ref, half, 16, column)
        target[...] = dot(normed, pick.astype(BF16)).astype(BF16)
        row = lax.broadcasted_iota(jnp.int32, (WIDTH, WIDTH // 2), 0)
        column = lax.broadcasted_iota(jnp.int32, (WIDTH, WIDTH // 2), 1)
        pick = row == sorted_rows(place_ref, half, 8, column)
        pick_ref[:, half * (WIDTH // 2) : (half + 1) * (WIDTH // 2)] = pick.astype(BF16)


def blocks_product(normed_refs, first, block_refs):
    total, starts = None, [first, first]
    for number, ref in enumerate(block_refs):
        half, depth = number % 2, ref.shape[0]
        rows = slice(starts[half], starts[half] + depth)
        starts[half] += depth
        part = dot(normed_refs[half][:, rows], ref[:, QKV : QKV + 3 * WIDTH])
        total = part if total is None else total + part
    return total


def spatial_kernel(tokens_ref, own_ref, other_ref, pick_ref, *rest):
    block_refs, (spatial_ref, packed, mixed) = rest[:-3], rest[-3:]
    packed[...] = blocks_product((own_ref, other_ref), 0, block_refs).astype(BF16)
    attend(packed, mixed, None)
    sorted_mixed = dot(mixed[...], pick_ref[...]).astype(BF16)
    halves = [
        ref[:, OUT : OUT + D // 2].astype(F32).reshape(ref.shape[0] // 16, 2, 8, D // 2)
        for ref in block_refs[0::2] + block_refs[1::2]
    ]
    for side in range(2):
        columns = slice(side * (D // 2), (side + 1) * (D // 2))
        weight = jnp.concatenate([half[:, side].reshape(-1, D // 2) for half in halves], axis=0)
        spatial_ref[:, columns] = (
            tokens_ref[:, columns].astype(F32) + dot(sorted_mixed, weight.astype(BF16))
        ).astype(BF16)


def gather_rows(weights_ref, first, target, sems):
    width = target.shape[-1]
    return [
        pltpu.make_async_copy(
            weights_ref.at[y, c, :, :, first : first + width], target.at[:, y, c], sems.at[2 * y + c]
        )
        for y in range(Y)
        for c in range(2)
    ]


def pack_kernel(
    ids_ref, states_ref, qkv_ref, text_ref, out_s_ref, out_t_ref, video_ref, spatial_ref,
    packed_ref, copies_ref,
    ids_here, states_here, text_here, out_s_here, out_t_here, sems,
):
    pairs = (
        (spatial_ref, copies_ref.at[0, :, QKV : QKV + 3 * WIDTH]),
        (ids_ref, ids_here),
        (states_ref, states_here),
        (text_ref, text_here),
        (out_s_ref, out_s_here),
        (out_t_ref, out_t_here),
        (qkv_ref, packed_ref.at[:, QKV : QKV + 3 * WIDTH]),
        (video_ref, packed_ref.at[:, W_VIDEO : W_VIDEO + E]),
    )
    copies = [pltpu.make_async_copy(*pair, sems.at[i]) for i, pair in enumerate(pairs)]
    for copy in copies:
        copy.start()
    for copy in copies:
        copy.wait()
    for source, target in ((out_s_here, copies_ref.at[0]), (out_t_here, packed_ref)):
        rows = source[...].astype(F32)
        rows = jnp.concatenate([rows[:, : D // 2], rows[:, D // 2 :]], axis=0)
        target[:, OUT : OUT + D // 2] = rows.astype(BF16)
    for copy in range(1, Y):
        copies_ref[copy] = copies_ref[0]
    ids = ids_here[...]
    positions = lax.broadcasted_iota(jnp.int32, ids.shape, 1)
    end_place = jnp.min(jnp.where(ids == jnp.max(ids), positions, ids.shape[1]))
    states = states_here[...].astype(F32)
    rows = lax.broadcasted_iota(jnp.int32, states.shape, 0)
    text_row = jnp.sum(jnp.where(rows == end_place, states, 0.0), axis=0, keepdims=True)
    text = jnp.concatenate([text_here[...].astype(F32), jnp.zeros((4, E), F32)], axis=0)
    place = lax.broadcasted_iota(jnp.int32, text.shape, 0)
    text = jnp.where(place < 12, text, jnp.where(place == 12, text_row, 0.0))
    packed_ref[:, W_TEXT : W_TEXT + E] = text.astype(BF16)


def temporal_kernel(
    spatial_ref, gain_ref, weights_ref, out_ref, pool_ref, qkv, outs, packed, mixed, sems
):
    copies_qkv = gather_rows(weights_ref, QKV, qkv, sems.at[0])
    copies_out = gather_rows(weights_ref, OUT, outs, sems.at[1])
    for copy in copies_qkv + copies_out:
        copy.start()
    rows = spatial_ref.shape[0]
    spatial = spatial_ref[...].astype(F32)
    normed = layer_norm(spatial, gain_ref[...]).astype(BF16)
    for copy in copies_qkv:
        copy.wait()
    packed[...] = dot(normed, qkv[...].reshape(D, 3 * WIDTH)).astype(BF16)
    patches = rows // FRAMES
    place = lax.broadcasted_iota(jnp.int32, (rows, rows), 0) % patches
    attend(packed, mixed, place == lax.broadcasted_iota(jnp.int32, (rows, rows), 1) % patches)
    for copy in copies_out:
        copy.wait()
    half = D // 2
    for side, weight in enumerate(out_halves(outs[...])):
        columns = slice(side * half, (side + 1) * half)
        output = (spatial_ref[:, columns].astype(F32) + dot(mixed[...], weight)).astype(BF16)
        out_ref[:, columns] = output
        total = jnp.sum(output.astype(F32), axis=0, keepdims=True)
        for chunk in range(half // 128):
            pool_ref[:, side * (half // 128) + chunk, :] = jnp.broadcast_to(
                total[:, chunk * 128 : (chunk + 1) * 128], (FRAMES, 128)
            )


def spread_kernel(parts_ref, every_ref):
    mine = jnp.sum(parts_ref[...], axis=0) * (1.0 / (8 * 256))
    every_ref[...] = jnp.broadcast_to(mine[None], every_ref.shape)


def text_kernel(
    gain_ref, weights_ref, pool_ref, mapped_ref, weight_ref, video_ref, gathered, sems
):
    copies = gather_rows(weights_ref, W_TEXT, gathered, sems.at[0])
    copies_video = gather_rows(weights_ref, W_VIDEO, video_ref, sems.at[1])
    for copy in copies + copies_video:
        copy.start()
    for copy in copies:
        copy.wait()
    packed = gathered[...].reshape(D, E)
    column = lax.broadcasted_iota(jnp.int32, (DT, D), 1)
    place = column % 16
    row = jnp.where(place < 12, (column // 16) * 12 + place, -1)
    pick = (row == lax.broadcasted_iota(jnp.int32, (DT, D), 0)).astype(BF16)
    weight = dot(pick, packed).astype(BF16)
    weight_ref[...] = weight
    column = lax.broadcasted_iota(jnp.int32, (64, D), 1)
    pick = (column == 16 * lax.broadcasted_iota(jnp.int32, (64, D), 0) + 12).astype(BF16)
    pool = dot(pick, packed)
    pool_ref[...] = pool
    mapped_ref[...] = exact(dot, layer_norm(pool, gain_ref[...]), weight)
    for copy in copies_video:
        copy.wait()


def unit_rows(values):
    return values * lax.rsqrt(jnp.sum(values * values, axis=-1, keepdims=True) + UNIT_EPS)


def unit_back(mapped, grad):
    scale = lax.rsqrt(jnp.sum(mapped * mapped, axis=-1, keepdims=True) + UNIT_EPS)
    along = jnp.sum(mapped * grad, axis=-1, keepdims=True)
    return scale * grad - mapped * (scale * scale * scale * along)


def norm_back(values, gain, grad):
    center = values - jnp.mean(values, axis=-1, keepdims=True)
    scale = lax.rsqrt(jnp.mean(center * center, axis=-1, keepdims=True) + NORM_EPS)
    grad = grad * gain
    unit = center * scale
    along = jnp.mean(grad * unit, axis=-1, keepdims=True)
    return scale * (grad - jnp.mean(grad, axis=-1, keepdims=True) - unit * along)


def loss_kernel(
    place_ref,
    scale_ref,
    pairs_ref,
    pooled_ref,
    text_pool_ref,
    text_mapped_ref,
    text_weight_ref,
    gain_video_ref,
    gain_text_ref,
    video_weight_ref,
    video_loss_ref,
    text_loss_ref,
    grad_pooled_ref,
    grad_text_ref,
    pooled_all,
):
    me = place_ref[0]
    scale = scale_ref[0]
    for chunk in range(D // 128):
        pooled_all[:, chunk * 128 : (chunk + 1) * 128] = pooled_ref[:, chunk, :]
    gain = gain_video_ref[...]
    normed = layer_norm(pooled_all[...], gain)
    weight = video_weight_ref[...].reshape(D, E)
    mapped = exact(dot, normed, weight)
    video = unit_rows(mapped)
    text_mapped = text_mapped_ref[...]
    text = unit_rows(text_mapped)
    logits = scale * lax.dot_general(
        video, text, (((1,), (1,)), ((), ())), precision=lax.Precision.HIGHEST,
        preferred_element_type=F32,
    )
    count = logits.shape[0]
    rows = lax.broadcasted_iota(jnp.int32, (count, count), 0)
    columns = lax.broadcasted_iota(jnp.int32, (count, count), 1)
    match = pairs_ref[...] == columns
    row_top = jnp.max(logits, axis=1, keepdims=True)
    row_exp = jnp.exp(logits - row_top)
    row_sum = jnp.sum(row_exp, axis=1, keepdims=True)
    col_top = jnp.max(logits, axis=0, keepdims=True)
    col_exp = jnp.exp(logits - col_top)
    col_sum = jnp.sum(col_exp, axis=0, keepdims=True)
    positive = jnp.where(match, logits, 0.0)
    video_loss = 0.5 * (row_top + jnp.log(row_sum) - jnp.sum(positive, axis=1, keepdims=True))
    text_loss = 0.5 * (col_top + jnp.log(col_sum) - jnp.sum(positive, axis=0, keepdims=True))
    mine_row = lax.broadcasted_iota(jnp.int32, (count, 1), 0) == me
    mine_col = lax.broadcasted_iota(jnp.int32, (1, count), 1) == me
    video_loss_ref[0] = jnp.sum(jnp.where(mine_row, video_loss, 0.0))
    text_loss_ref[0] = jnp.sum(jnp.where(mine_col, text_loss, 0.0))
    slope = (0.5 * scale) * (row_exp / row_sum + col_exp / col_sum - 2.0 * match.astype(F32))
    row_slope = jnp.sum(jnp.where(rows == me, slope, 0.0), axis=0, keepdims=True)
    row_slope = jnp.sum(jnp.where(rows == columns, row_slope, 0.0), axis=1, keepdims=True)
    col_slope = jnp.sum(jnp.where(columns == me, slope, 0.0), axis=1, keepdims=True)
    grad_video = jnp.sum(row_slope * text, axis=0, keepdims=True)
    grad_caption = jnp.sum(col_slope * video, axis=0, keepdims=True)
    mine_mapped = jnp.sum(jnp.where(mine_row, mapped, 0.0), axis=0, keepdims=True)
    mine_text_mapped = jnp.sum(jnp.where(mine_row, text_mapped, 0.0), axis=0, keepdims=True)
    mine_pooled = jnp.sum(jnp.where(mine_row, pooled_all[...], 0.0), axis=0, keepdims=True)
    mine_text_pool = jnp.sum(jnp.where(mine_row, text_pool_ref[...], 0.0), axis=0, keepdims=True)
    back = exact_row(dot_t, unit_back(mine_mapped, grad_video), weight)
    grad_pooled_ref[...] = norm_back(mine_pooled, gain, back)
    back = exact_row(dot_t, unit_back(mine_text_mapped, grad_caption), text_weight_ref[...])
    grad_text_ref[...] = norm_back(mine_text_pool, gain_text_ref[...], back)


def call(kernel, out_shape, in_spaces, scratch, out_spaces=None, vmem=VMEM_LIMIT, flops=0):
    many = isinstance(out_shape, (tuple, list))
    out_spaces = out_spaces or ([pltpu.VMEM] * (len(out_shape) if many else 1))
    out_specs = [pl.BlockSpec(memory_space=space) for space in out_spaces]
    return pl.pallas_call(
        kernel,
        out_shape=out_shape,
        in_specs=[pl.BlockSpec(memory_space=space) for space in in_spaces],
        out_specs=out_specs if many else out_specs[0],
        scratch_shapes=scratch,
        compiler_params=pltpu.CompilerParams(vmem_limit_bytes=vmem),
        cost_estimate=pl.CostEstimate(flops=flops, bytes_accessed=0, transcendentals=0),
    )


def shape(dims, dtype):
    return jax.ShapeDtypeStruct(dims, dtype)


def send_all(copies, groups):
    return lax.all_to_all(copies, "dp", 0, 0, tiled=True, axis_index_groups=groups)


def on_device(
    video_tokens,
    text_states,
    caption_ids,
    pair_index,
    logit_scale,
    gain_spatial,
    gain_temporal,
    gain_video,
    gain_text,
    w_qkv_spatial,
    w_out_spatial,
    w_qkv_temporal,
    w_out_temporal,
    w_video,
    w_text,
):
    V, S, A = pltpu.VMEM, pltpu.SMEM, pl.ANY
    DMA = pltpu.SemaphoreType.DMA
    halves = (X, Y, 2, 16)
    tokens = video_tokens.reshape(256, D)
    place = lax.axis_index("dp").astype(jnp.int32).reshape(1)
    packed, own = call(
        pack_kernel,
        (shape((16, PACKED_T), BF16), shape((Y, 16, PACKED_S), BF16)),
        (A,) * 8,
        [
            pltpu.VMEM(caption_ids.shape, jnp.int32),
            pltpu.VMEM(text_states.shape[1:], BF16),
            pltpu.VMEM(w_text.shape, BF16),
            pltpu.VMEM(w_out_spatial.shape, BF16),
            pltpu.VMEM(w_out_temporal.shape, BF16),
            DMA((8,)),
        ],
        vmem=VMEM_WHOLE,
    )(
        caption_ids,
        text_states.reshape(text_states.shape[1:]),
        w_qkv_temporal,
        w_text,
        w_out_spatial,
        w_out_temporal,
        w_video,
        w_qkv_spatial,
    )
    barrier = lax.optimization_barrier
    gather = functools.partial(lax.all_gather, axis_name="dp", axis=0, tiled=True)
    own = send_all(own, ROWS_OF_Y)
    packed = gather(packed, axis_index_groups=ROWS_OF_X)
    own, packed = barrier((own, packed))
    weights = gather(packed, axis_index_groups=ROWS_OF_YC).reshape(Y, 2, X, 16, PACKED_T)
    permute = functools.partial(lax.ppermute, axis_name="dp")
    mine, late_tokens = barrier((own.reshape(BLOCK, PACKED_S), tokens))
    below, above = permute(mine, perm=X_UP), permute(mine, perm=X_DOWN)
    mine_other = permute(mine, perm=OTHER_CORE)
    where = jnp.concatenate([place // (2 * Y), place % 2])
    *normed, pick = call(
        norm_kernel,
        (shape((256, D // 2), BF16),) * 2 + (shape((WIDTH, WIDTH), BF16),),
        (S, V, V),
        [],
        flops=1 << 30,
    )(where, late_tokens, gain_spatial.reshape(1, D))
    below, above, low, high, normed, pick = barrier(
        (below, above, below[: BLOCK // 2], above[BLOCK // 2 :], normed, pick)
    )
    low, high = permute(low, perm=X_UP), permute(high, perm=X_DOWN)
    near, far = [mine, mine_other], []
    for block in (below, above):
        near += [block, permute(block, perm=OTHER_CORE)]
    for block in (low, high):
        far += [block, permute(block, perm=OTHER_CORE)]
    spatial = call(
        spatial_kernel,
        shape((256, D), BF16),
        (V,) * 14,
        [pltpu.VMEM((256, 3 * WIDTH), BF16), pltpu.VMEM((256, WIDTH), BF16)],
        vmem=VMEM_SMALL,
    )(tokens, *normed, pick, *near, *far)
    spatial = lax.all_to_all(spatial.reshape(FRAMES, 32, D), "frame", 0, 0, tiled=True)
    layer_out, pool = call(
        temporal_kernel,
        (shape((256, D), BF16), shape((FRAMES, 8, 128), F32)),
        (V, V, A),
        [
            pltpu.VMEM(halves + (3 * WIDTH,), BF16),
            pltpu.VMEM(halves + (D // 2,), BF16),
            pltpu.VMEM((256, 3 * WIDTH), BF16),
            pltpu.VMEM((256, WIDTH), BF16),
            DMA((2, 2 * Y)),
        ],
    )(spatial.reshape(256, D), gain_temporal.reshape(1, D), weights)
    text_pool, text_mapped, text_weight, video_weight = call(
        text_kernel,
        (
            shape((64, DT), F32),
            shape((64, E), F32),
            shape((DT, E), BF16),
            shape(halves + (E,), BF16),
        ),
        (V, A),
        [pltpu.VMEM(halves + (E,), BF16), DMA((2, 2 * Y))],
    )(gain_text.reshape(1, DT), weights)
    pool = lax.all_to_all(pool, "frame", 0, 0, tiled=True)
    pool = call(spread_kernel, shape((64, 8, 128), F32), (V,), [])(pool)
    pooled = lax.all_to_all(pool, "dp", 0, 0, tiled=True)
    video_loss, text_loss, grad_pooled, grad_text = call(
        loss_kernel,
        (shape((1,), F32), shape((1,), F32), shape((1, D), F32), shape((1, DT), F32)),
        (S, S, V, V, V, V, V, V, V, V),
        [pltpu.VMEM((64, D), F32)],
        (S, S, V, V),
        vmem=VMEM_SMALL,
    )(
        place,
        logit_scale,
        pair_index.reshape(64, 1),
        pooled,
        text_pool,
        text_mapped,
        text_weight,
        gain_video.reshape(1, D),
        gain_text.reshape(1, DT),
        video_weight,
    )
    return (layer_out.reshape(1, 8, 32, D), video_loss, text_loss, grad_pooled, grad_text)


def solution(mesh):
    placed = (
        P("dp", "frame", None, None),
        P("dp", None, None),
        P("dp", None),
        P(),
        P(),
        P(),
        P(),
        P(),
        P(),
        P("dp", None),
        P("dp", None),
        P("dp", None),
        P("dp", None),
        P("dp", None),
        P("dp", None),
    )
    return jax.shard_map(
        on_device,
        mesh=mesh,
        in_specs=placed,
        out_specs=(P("dp", None, "frame", None), P("dp"), P("dp"), P("dp", None), P("dp", None)),
        check_vma=False,
    )
```

```python
import functools

import jax
import jax.numpy as jnp
from jax import lax
from jax.experimental import pallas as pl
from jax.experimental.pallas import tpu as pltpu
from jax.sharding import PartitionSpec as P

HEADS = 8
HD = 64
WIDTH = HEADS * HD
D = 1024
DT = 768
E = 768
NORM_EPS = 1e-05
UNIT_EPS = 1e-06
F32 = jnp.float32
BF16 = jnp.bfloat16
MIB = 1024 * 1024
VMEM_LIMIT = 48 * MIB
VMEM_WHOLE = 63 * MIB
VMEM_SMALL = 24 * MIB

QKV = 0
OUT = 1536
PACKED_S = 2048
W_TEXT = 2048
W_VIDEO = 2816
PACKED_T = 3584

X, Y = 4, 8
ROWS_OF_X = [[(x * Y + y) * 2 + c for x in range(X)] for y in range(Y) for c in range(2)]
ROWS_OF_Y = [[(x * Y + y) * 2 + c for y in range(Y)] for x in range(X) for c in range(2)]
ROWS_OF_YC = [[(x * Y + y) * 2 + c for y in range(Y) for c in range(2)] for x in range(X)]
OTHER_CORE = [(i, i ^ 1) for i in range(2 * X * Y)]
X_UP = [(i, (i + 2 * Y) % (2 * X * Y)) for i in range(2 * X * Y)]
X_DOWN = [(i, (i - 2 * Y) % (2 * X * Y)) for i in range(2 * X * Y)]
STEPS = (0, X - 1, 1, 2)
BLOCK = Y * 16
FRAMES = 8


def dot(a, b):
    return lax.dot_general(a, b, (((1,), (0,)), ((), ())), preferred_element_type=F32)


def dot_t(a, b):
    return lax.dot_general(a, b, (((1,), (1,)), ((), ())), preferred_element_type=F32)


def pieces(a):
    first = a.astype(BF16)
    rest = a - first.astype(F32)
    second = rest.astype(BF16)
    third = (rest - second.astype(F32)).astype(BF16)
    return first, second, third


def exact(dot_fn, a, weight):
    rows = a.shape[0]
    parts = dot_fn(jnp.concatenate(pieces(a), axis=0), weight)
    return parts[2 * rows :] + parts[rows : 2 * rows] + parts[:rows]


def exact_row(dot_fn, a, weight):
    rows = lax.broadcasted_iota(jnp.int32, (16, a.shape[1]), 0)
    first, second, third = (piece.astype(F32) for piece in pieces(a))
    block = jnp.where(rows == 0, third, jnp.where(rows == 1, second, jnp.where(rows == 2, first, 0.0)))
    return jnp.sum(dot_fn(block.astype(BF16), weight), axis=0, keepdims=True)


def layer_norm(values, gain):
    center = values - jnp.mean(values, axis=-1, keepdims=True)
    spread = jnp.mean(center * center, axis=-1, keepdims=True)
    return center * lax.rsqrt(spread + NORM_EPS) * gain


def attend_pair(query, key, value, mask):
    low = lax.broadcasted_iota(jnp.int32, query.shape, 1) < HD
    mixed = []
    for lanes in (low, ~low):
        scores = dot_t(jnp.where(lanes, query, jnp.zeros_like(query)), key) * (HD**-0.5)
        if mask is not None:
            scores = jnp.where(mask, scores, -1e30)
        weight = jnp.exp(scores - jnp.max(scores, axis=-1, keepdims=True))
        probs = weight * (1.0 / jnp.sum(weight, axis=-1, keepdims=True))
        mixed.append(dot(probs.astype(BF16), value))
    return jnp.where(low, mixed[0], mixed[1]).astype(BF16)


def attend(packed_ref, mixed_ref, mask):
    for at in range(0, WIDTH, 2 * HD):
        query, key, value = (
            packed_ref[:, part * WIDTH + at : part * WIDTH + at + 2 * HD] for part in range(3)
        )
        mixed_ref[:, at : at + 2 * HD] = attend_pair(query, key, value, mask)


def out_halves(gathered):
    halves = gathered.astype(F32).reshape(64, 2, 8, D // 2)
    return [halves[:, side].reshape(WIDTH, D // 2).astype(BF16) for side in range(2)]


def sorted_rows(place_ref, half, depth, column):
    block = column // (Y * depth)
    step = jnp.zeros_like(block)
    for number, value in enumerate(STEPS):
        step = jnp.where(block == number, value, step)
    x = (place_ref[0] + step) % X
    core = place_ref[1] if half == 0 else 1 - place_ref[1]
    y = column // depth % Y
    return ((x * Y + y) * 2 + core) * depth + column % depth


def norm_kernel(place_ref, tokens_ref, gain_ref, own_ref, other_ref, pick_ref):
    normed = layer_norm(tokens_ref[...].astype(F32), gain_ref[...]).astype(BF16)
    for half, target in enumerate((own_ref, other_ref)):
        row = lax.broadcasted_iota(jnp.int32, (D, D // 2), 0)
        column = lax.broadcasted_iota(jnp.int32, (D, D // 2), 1)
        pick = row == sorted_rows(place_ref, half, 16, column)
        target[...] = dot(normed, pick.astype(BF16)).astype(BF16)
        row = lax.broadcasted_iota(jnp.int32, (WIDTH, WIDTH // 2), 0)
        column = lax.broadcasted_iota(jnp.int32, (WIDTH, WIDTH // 2), 1)
        pick = row == sorted_rows(place_ref, half, 8, column)
        pick_ref[:, half * (WIDTH // 2) : (half + 1) * (WIDTH // 2)] = pick.astype(BF16)


def spatial_kernel(tokens_ref, own_ref, other_ref, pick_ref, *rest):
    block_refs, (spatial_ref, packed, mixed) = rest[:-3], rest[-3:]
    block_refs = block_refs[0::2] + block_refs[1::2]
    normed = jnp.concatenate([own_ref[...], other_ref[...]], axis=1)
    weight = jnp.concatenate([ref[:, QKV : QKV + 3 * WIDTH] for ref in block_refs], axis=0)
    packed[...] = dot(normed, weight).astype(BF16)
    attend(packed, mixed, None)
    sorted_mixed = dot(mixed[...], pick_ref[...]).astype(BF16)
    halves = [
        ref[:, OUT : OUT + D // 2].astype(F32).reshape(ref.shape[0] // 16, 2, 8, D // 2)
        for ref in block_refs
    ]
    for side in range(2):
        columns = slice(side * (D // 2), (side + 1) * (D // 2))
        weight = jnp.concatenate([half[:, side].reshape(-1, D // 2) for half in halves], axis=0)
        spatial_ref[:, columns] = (
            tokens_ref[:, columns].astype(F32) + dot(sorted_mixed, weight.astype(BF16))
        ).astype(BF16)


def gather_rows(weights_ref, first, target, sems):
    width = target.shape[-1]
    return [
        pltpu.make_async_copy(
            weights_ref.at[y, c, :, :, first : first + width], target.at[:, y, c], sems.at[2 * y + c]
        )
        for y in range(Y)
        for c in range(2)
    ]


def pack_kernel(
    ids_ref, states_ref, qkv_ref, text_ref, out_s_ref, out_t_ref, video_ref, spatial_ref,
    packed_ref, copies_ref,
    ids_here, states_here, text_here, out_s_here, out_t_here, sems,
):
    pairs = (
        (spatial_ref, copies_ref.at[0, :, QKV : QKV + 3 * WIDTH]),
        (ids_ref, ids_here),
        (states_ref, states_here),
        (text_ref, text_here),
        (out_s_ref, out_s_here),
        (out_t_ref, out_t_here),
        (qkv_ref, packed_ref.at[:, QKV : QKV + 3 * WIDTH]),
        (video_ref, packed_ref.at[:, W_VIDEO : W_VIDEO + E]),
    )
    copies = [pltpu.make_async_copy(*pair, sems.at[i]) for i, pair in enumerate(pairs)]
    for copy in copies:
        copy.start()
    for copy in copies:
        copy.wait()
    for source, target in ((out_s_here, copies_ref.at[0]), (out_t_here, packed_ref)):
        rows = source[...].astype(F32)
        rows = jnp.concatenate([rows[:, : D // 2], rows[:, D // 2 :]], axis=0)
        target[:, OUT : OUT + D // 2] = rows.astype(BF16)
    for copy in range(1, Y):
        copies_ref[copy] = copies_ref[0]
    ids = ids_here[...]
    positions = lax.broadcasted_iota(jnp.int32, ids.shape, 1)
    end_place = jnp.min(jnp.where(ids == jnp.max(ids), positions, ids.shape[1]))
    states = states_here[...].astype(F32)
    rows = lax.broadcasted_iota(jnp.int32, states.shape, 0)
    text_row = jnp.sum(jnp.where(rows == end_place, states, 0.0), axis=0, keepdims=True)
    text = jnp.concatenate([text_here[...].astype(F32), jnp.zeros((4, E), F32)], axis=0)
    place = lax.broadcasted_iota(jnp.int32, text.shape, 0)
    text = jnp.where(place < 12, text, jnp.where(place == 12, text_row, 0.0))
    packed_ref[:, W_TEXT : W_TEXT + E] = text.astype(BF16)


def temporal_kernel(
    spatial_ref, gain_ref, weights_ref, out_ref, pool_ref, qkv, outs, packed, mixed, sems
):
    copies_qkv = gather_rows(weights_ref, QKV, qkv, sems.at[0])
    copies_out = gather_rows(weights_ref, OUT, outs, sems.at[1])
    for copy in copies_qkv + copies_out:
        copy.start()
    rows = spatial_ref.shape[0]
    spatial = spatial_ref[...].astype(F32)
    normed = layer_norm(spatial, gain_ref[...]).astype(BF16)
    for copy in copies_qkv:
        copy.wait()
    packed[...] = dot(normed, qkv[...].reshape(D, 3 * WIDTH)).astype(BF16)
    patches = rows // FRAMES
    place = lax.broadcasted_iota(jnp.int32, (rows, rows), 0) % patches
    attend(packed, mixed, place == lax.broadcasted_iota(jnp.int32, (rows, rows), 1) % patches)
    for copy in copies_out:
        copy.wait()
    half = D // 2
    for side, weight in enumerate(out_halves(outs[...])):
        columns = slice(side * half, (side + 1) * half)
        output = (spatial_ref[:, columns].astype(F32) + dot(mixed[...], weight)).astype(BF16)
        out_ref[:, columns] = output
        total = jnp.sum(output.astype(F32), axis=0, keepdims=True)
        for chunk in range(half // 128):
            pool_ref[:, side * (half // 128) + chunk, :] = jnp.broadcast_to(
                total[:, chunk * 128 : (chunk + 1) * 128], (FRAMES, 128)
            )


def spread_kernel(parts_ref, every_ref):
    mine = jnp.sum(parts_ref[...], axis=0) * (1.0 / (8 * 256))
    every_ref[...] = jnp.broadcast_to(mine[None], every_ref.shape)


def text_kernel(
    gain_ref, weights_ref, pool_ref, mapped_ref, weight_ref, video_ref, gathered, sems
):
    copies = gather_rows(weights_ref, W_TEXT, gathered, sems.at[0])
    copies_video = gather_rows(weights_ref, W_VIDEO, video_ref, sems.at[1])
    for copy in copies + copies_video:
        copy.start()
    for copy in copies:
        copy.wait()
    packed = gathered[...].reshape(D, E)
    column = lax.broadcasted_iota(jnp.int32, (DT, D), 1)
    place = column % 16
    row = jnp.where(place < 12, (column // 16) * 12 + place, -1)
    pick = (row == lax.broadcasted_iota(jnp.int32, (DT, D), 0)).astype(BF16)
    weight = dot(pick, packed).astype(BF16)
    weight_ref[...] = weight
    column = lax.broadcasted_iota(jnp.int32, (64, D), 1)
    pick = (column == 16 * lax.broadcasted_iota(jnp.int32, (64, D), 0) + 12).astype(BF16)
    pool = dot(pick, packed)
    pool_ref[...] = pool
    mapped_ref[...] = exact(dot, layer_norm(pool, gain_ref[...]), weight)
    for copy in copies_video:
        copy.wait()


def unit_rows(values):
    return values * lax.rsqrt(jnp.sum(values * values, axis=-1, keepdims=True) + UNIT_EPS)


def unit_back(mapped, grad):
    scale = lax.rsqrt(jnp.sum(mapped * mapped, axis=-1, keepdims=True) + UNIT_EPS)
    along = jnp.sum(mapped * grad, axis=-1, keepdims=True)
    return scale * grad - mapped * (scale * scale * scale * along)


def norm_back(values, gain, grad):
    center = values - jnp.mean(values, axis=-1, keepdims=True)
    scale = lax.rsqrt(jnp.mean(center * center, axis=-1, keepdims=True) + NORM_EPS)
    grad = grad * gain
    unit = center * scale
    along = jnp.mean(grad * unit, axis=-1, keepdims=True)
    return scale * (grad - jnp.mean(grad, axis=-1, keepdims=True) - unit * along)


def loss_kernel(
    place_ref,
    scale_ref,
    pairs_ref,
    pooled_ref,
    text_pool_ref,
    text_mapped_ref,
    text_weight_ref,
    gain_video_ref,
    gain_text_ref,
    video_weight_ref,
    video_loss_ref,
    text_loss_ref,
    grad_pooled_ref,
    grad_text_ref,
    pooled_all,
):
    me = place_ref[0]
    scale = scale_ref[0]
    for chunk in range(D // 128):
        pooled_all[:, chunk * 128 : (chunk + 1) * 128] = pooled_ref[:, chunk, :]
    gain = gain_video_ref[...]
    normed = layer_norm(pooled_all[...], gain)
    weight = video_weight_ref[...].reshape(D, E)
    mapped = exact(dot, normed, weight)
    video = unit_rows(mapped)
    text_mapped = text_mapped_ref[...]
    text = unit_rows(text_mapped)
    logits = scale * lax.dot_general(
        video, text, (((1,), (1,)), ((), ())), precision=lax.Precision.HIGHEST,
        preferred_element_type=F32,
    )
    count = logits.shape[0]
    rows = lax.broadcasted_iota(jnp.int32, (count, count), 0)
    columns = lax.broadcasted_iota(jnp.int32, (count, count), 1)
    match = pairs_ref[...] == columns
    row_top = jnp.max(logits, axis=1, keepdims=True)
    row_exp = jnp.exp(logits - row_top)
    row_sum = jnp.sum(row_exp, axis=1, keepdims=True)
    col_top = jnp.max(logits, axis=0, keepdims=True)
    col_exp = jnp.exp(logits - col_top)
    col_sum = jnp.sum(col_exp, axis=0, keepdims=True)
    positive = jnp.where(match, logits, 0.0)
    video_loss = 0.5 * (row_top + jnp.log(row_sum) - jnp.sum(positive, axis=1, keepdims=True))
    text_loss = 0.5 * (col_top + jnp.log(col_sum) - jnp.sum(positive, axis=0, keepdims=True))
    mine_row = lax.broadcasted_iota(jnp.int32, (count, 1), 0) == me
    mine_col = lax.broadcasted_iota(jnp.int32, (1, count), 1) == me
    video_loss_ref[0] = jnp.sum(jnp.where(mine_row, video_loss, 0.0))
    text_loss_ref[0] = jnp.sum(jnp.where(mine_col, text_loss, 0.0))
    slope = (0.5 * scale) * (row_exp / row_sum + col_exp / col_sum - 2.0 * match.astype(F32))
    row_slope = jnp.sum(jnp.where(rows == me, slope, 0.0), axis=0, keepdims=True)
    row_slope = jnp.sum(jnp.where(rows == columns, row_slope, 0.0), axis=1, keepdims=True)
    col_slope = jnp.sum(jnp.where(columns == me, slope, 0.0), axis=1, keepdims=True)
    grad_video = jnp.sum(row_slope * text, axis=0, keepdims=True)
    grad_caption = jnp.sum(col_slope * video, axis=0, keepdims=True)
    mine_mapped = jnp.sum(jnp.where(mine_row, mapped, 0.0), axis=0, keepdims=True)
    mine_text_mapped = jnp.sum(jnp.where(mine_row, text_mapped, 0.0), axis=0, keepdims=True)
    mine_pooled = jnp.sum(jnp.where(mine_row, pooled_all[...], 0.0), axis=0, keepdims=True)
    mine_text_pool = jnp.sum(jnp.where(mine_row, text_pool_ref[...], 0.0), axis=0, keepdims=True)
    back = exact_row(dot_t, unit_back(mine_mapped, grad_video), weight)
    grad_pooled_ref[...] = norm_back(mine_pooled, gain, back)
    back = exact_row(dot_t, unit_back(mine_text_mapped, grad_caption), text_weight_ref[...])
    grad_text_ref[...] = norm_back(mine_text_pool, gain_text_ref[...], back)


def call(kernel, out_shape, in_spaces, scratch, out_spaces=None, vmem=VMEM_LIMIT, flops=0):
    many = isinstance(out_shape, (tuple, list))
    out_spaces = out_spaces or ([pltpu.VMEM] * (len(out_shape) if many else 1))
    out_specs = [pl.BlockSpec(memory_space=space) for space in out_spaces]
    return pl.pallas_call(
        kernel,
        out_shape=out_shape,
        in_specs=[pl.BlockSpec(memory_space=space) for space in in_spaces],
        out_specs=out_specs if many else out_specs[0],
        scratch_shapes=scratch,
        compiler_params=pltpu.CompilerParams(vmem_limit_bytes=vmem),
        cost_estimate=pl.CostEstimate(flops=flops, bytes_accessed=0, transcendentals=0),
    )


def shape(dims, dtype):
    return jax.ShapeDtypeStruct(dims, dtype)


def send_all(copies, groups):
    return lax.all_to_all(copies, "dp", 0, 0, tiled=True, axis_index_groups=groups)


def on_device(
    video_tokens,
    text_states,
    caption_ids,
    pair_index,
    logit_scale,
    gain_spatial,
    gain_temporal,
    gain_video,
    gain_text,
    w_qkv_spatial,
    w_out_spatial,
    w_qkv_temporal,
    w_out_temporal,
    w_video,
    w_text,
):
    V, S, A = pltpu.VMEM, pltpu.SMEM, pl.ANY
    DMA = pltpu.SemaphoreType.DMA
    halves = (X, Y, 2, 16)
    tokens = video_tokens.reshape(256, D)
    place = lax.axis_index("dp").astype(jnp.int32).reshape(1)
    packed, own = call(
        pack_kernel,
        (shape((16, PACKED_T), BF16), shape((Y, 16, PACKED_S), BF16)),
        (A,) * 8,
        [
            pltpu.VMEM(caption_ids.shape, jnp.int32),
            pltpu.VMEM(text_states.shape[1:], BF16),
            pltpu.VMEM(w_text.shape, BF16),
            pltpu.VMEM(w_out_spatial.shape, BF16),
            pltpu.VMEM(w_out_temporal.shape, BF16),
            DMA((8,)),
        ],
        vmem=VMEM_WHOLE,
    )(
        caption_ids,
        text_states.reshape(text_states.shape[1:]),
        w_qkv_temporal,
        w_text,
        w_out_spatial,
        w_out_temporal,
        w_video,
        w_qkv_spatial,
    )
    barrier = lax.optimization_barrier
    gather = functools.partial(lax.all_gather, axis_name="dp", axis=0, tiled=True)
    own = send_all(own, ROWS_OF_Y)
    packed = gather(packed, axis_index_groups=ROWS_OF_X)
    own, packed = barrier((own, packed))
    weights = gather(packed, axis_index_groups=ROWS_OF_YC).reshape(Y, 2, X, 16, PACKED_T)
    permute = functools.partial(lax.ppermute, axis_name="dp")
    mine, late_tokens = barrier((own.reshape(BLOCK, PACKED_S), tokens))
    below, above = permute(mine, perm=X_UP), permute(mine, perm=X_DOWN)
    mine_other = permute(mine, perm=OTHER_CORE)
    where = jnp.concatenate([place // (2 * Y), place % 2])
    *normed, pick = call(
        norm_kernel,
        (shape((256, D // 2), BF16),) * 2 + (shape((WIDTH, WIDTH), BF16),),
        (S, V, V),
        [],
        flops=1 << 30,
    )(where, late_tokens, gain_spatial.reshape(1, D))
    below, low, normed, pick = barrier((below, below[: BLOCK // 2], normed, pick))
    above, high = barrier((above, above[BLOCK // 2 :]))
    low, high = permute(low, perm=X_UP), permute(high, perm=X_DOWN)
    near, far = [mine, mine_other], []
    for block in (below, above):
        near += [block, permute(block, perm=OTHER_CORE)]
    for block in (low, high):
        far += [block, permute(block, perm=OTHER_CORE)]
    spatial = call(
        spatial_kernel,
        shape((256, D), BF16),
        (V,) * 14,
        [pltpu.VMEM((256, 3 * WIDTH), BF16), pltpu.VMEM((256, WIDTH), BF16)],
        vmem=VMEM_SMALL,
    )(tokens, *normed, pick, *near, *far)
    spatial = lax.all_to_all(spatial.reshape(FRAMES, 32, D), "frame", 0, 0, tiled=True)
    layer_out, pool = call(
        temporal_kernel,
        (shape((256, D), BF16), shape((FRAMES, 8, 128), F32)),
        (V, V, A),
        [
            pltpu.VMEM(halves + (3 * WIDTH,), BF16),
            pltpu.VMEM(halves + (D // 2,), BF16),
            pltpu.VMEM((256, 3 * WIDTH), BF16),
            pltpu.VMEM((256, WIDTH), BF16),
            DMA((2, 2 * Y)),
        ],
    )(spatial.reshape(256, D), gain_temporal.reshape(1, D), weights)
    text_pool, text_mapped, text_weight, video_weight = call(
        text_kernel,
        (
            shape((64, DT), F32),
            shape((64, E), F32),
            shape((DT, E), BF16),
            shape(halves + (E,), BF16),
        ),
        (V, A),
        [pltpu.VMEM(halves + (E,), BF16), DMA((2, 2 * Y))],
    )(gain_text.reshape(1, DT), weights)
    pool = lax.all_to_all(pool, "frame", 0, 0, tiled=True)
    pool = call(spread_kernel, shape((64, 8, 128), F32), (V,), [])(pool)
    pooled = lax.all_to_all(pool, "dp", 0, 0, tiled=True)
    video_loss, text_loss, grad_pooled, grad_text = call(
        loss_kernel,
        (shape((1,), F32), shape((1,), F32), shape((1, D), F32), shape((1, DT), F32)),
        (S, S, V, V, V, V, V, V, V, V),
        [pltpu.VMEM((64, D), F32)],
        (S, S, V, V),
        vmem=VMEM_SMALL,
    )(
        place,
        logit_scale,
        pair_index.reshape(64, 1),
        pooled,
        text_pool,
        text_mapped,
        text_weight,
        gain_video.reshape(1, D),
        gain_text.reshape(1, DT),
        video_weight,
    )
    return (layer_out.reshape(1, 8, 32, D), video_loss, text_loss, grad_pooled, grad_text)


def solution(mesh):
    placed = (
        P("dp", "frame", None, None),
        P("dp", None, None),
        P("dp", None),
        P(),
        P(),
        P(),
        P(),
        P(),
        P(),
        P("dp", None),
        P("dp", None),
        P("dp", None),
        P("dp", None),
        P("dp", None),
        P("dp", None),
    )
    return jax.shard_map(
        on_device,
        mesh=mesh,
        in_specs=placed,
        out_specs=(P("dp", None, "frame", None), P("dp"), P("dp"), P("dp", None), P("dp", None)),
        check_vma=False,
    )
```

```python
import functools

import jax
import jax.numpy as jnp
from jax import lax
from jax.experimental import pallas as pl
from jax.experimental.pallas import tpu as pltpu
from jax.sharding import PartitionSpec as P

HEADS = 8
HD = 64
WIDTH = HEADS * HD
D = 1024
DT = 768
E = 768
NORM_EPS = 1e-05
UNIT_EPS = 1e-06
F32 = jnp.float32
BF16 = jnp.bfloat16
MIB = 1024 * 1024
VMEM_LIMIT = 48 * MIB
VMEM_WHOLE = 63 * MIB
VMEM_SMALL = 24 * MIB

QKV = 0
OUT = 1536
PACKED_S = 2048
W_TEXT = 2048
W_VIDEO = 2816
PACKED_T = 3584

X, Y = 4, 8
ROWS_OF_X = [[(x * Y + y) * 2 + c for x in range(X)] for y in range(Y) for c in range(2)]
ROWS_OF_Y = [[(x * Y + y) * 2 + c for y in range(Y)] for x in range(X) for c in range(2)]
ROWS_OF_YC = [[(x * Y + y) * 2 + c for y in range(Y) for c in range(2)] for x in range(X)]
OTHER_CORE = [(i, i ^ 1) for i in range(2 * X * Y)]
X_UP = [(i, (i + 2 * Y) % (2 * X * Y)) for i in range(2 * X * Y)]
X_DOWN = [(i, (i - 2 * Y) % (2 * X * Y)) for i in range(2 * X * Y)]
STEPS = (0, X - 1, 1, 2)
BLOCK = Y * 16
FRAMES = 8


def dot(a, b):
    return lax.dot_general(a, b, (((1,), (0,)), ((), ())), preferred_element_type=F32)


def dot_t(a, b):
    return lax.dot_general(a, b, (((1,), (1,)), ((), ())), preferred_element_type=F32)


def pieces(a):
    first = a.astype(BF16)
    rest = a - first.astype(F32)
    second = rest.astype(BF16)
    third = (rest - second.astype(F32)).astype(BF16)
    return first, second, third


def exact(dot_fn, a, weight):
    rows = a.shape[0]
    parts = dot_fn(jnp.concatenate(pieces(a), axis=0), weight)
    return parts[2 * rows :] + parts[rows : 2 * rows] + parts[:rows]


def exact_row(dot_fn, a, weight):
    rows = lax.broadcasted_iota(jnp.int32, (16, a.shape[1]), 0)
    first, second, third = (piece.astype(F32) for piece in pieces(a))
    block = jnp.where(rows == 0, third, jnp.where(rows == 1, second, jnp.where(rows == 2, first, 0.0)))
    return jnp.sum(dot_fn(block.astype(BF16), weight), axis=0, keepdims=True)


def layer_norm(values, gain):
    center = values - jnp.mean(values, axis=-1, keepdims=True)
    spread = jnp.mean(center * center, axis=-1, keepdims=True)
    return center * lax.rsqrt(spread + NORM_EPS) * gain


def attend_pair(query, key, value, mask):
    low = lax.broadcasted_iota(jnp.int32, query.shape, 1) < HD
    mixed = []
    for lanes in (low, ~low):
        scores = dot_t(jnp.where(lanes, query, jnp.zeros_like(query)), key) * (HD**-0.5)
        if mask is not None:
            scores = jnp.where(mask, scores, -1e30)
        weight = jnp.exp(scores - jnp.max(scores, axis=-1, keepdims=True))
        probs = weight * (1.0 / jnp.sum(weight, axis=-1, keepdims=True))
        mixed.append(dot(probs.astype(BF16), value))
    return jnp.where(low, mixed[0], mixed[1]).astype(BF16)


def attend(packed_ref, mixed_ref, mask):
    for at in range(0, WIDTH, 2 * HD):
        query, key, value = (
            packed_ref[:, part * WIDTH + at : part * WIDTH + at + 2 * HD] for part in range(3)
        )
        mixed_ref[:, at : at + 2 * HD] = attend_pair(query, key, value, mask)


def out_halves(gathered):
    halves = gathered.astype(F32).reshape(64, 2, 8, D // 2)
    return [halves[:, side].reshape(WIDTH, D // 2).astype(BF16) for side in range(2)]


def sorted_rows(place_ref, half, depth, column):
    block = column // (Y * depth)
    step = jnp.zeros_like(block)
    for number, value in enumerate(STEPS):
        step = jnp.where(block == number, value, step)
    x = (place_ref[0] + step) % X
    core = place_ref[1] if half == 0 else 1 - place_ref[1]
    y = column // depth % Y
    return ((x * Y + y) * 2 + core) * depth + column % depth


def norm_kernel(place_ref, tokens_ref, gain_ref, own_ref, other_ref, pick_ref):
    normed = layer_norm(tokens_ref[...].astype(F32), gain_ref[...]).astype(BF16)
    for half, target in enumerate((own_ref, other_ref)):
        row = lax.broadcasted_iota(jnp.int32, (D, D // 2), 0)
        column = lax.broadcasted_iota(jnp.int32, (D, D // 2), 1)
        pick = row == sorted_rows(place_ref, half, 16, column)
        target[...] = dot(normed, pick.astype(BF16)).astype(BF16)
        row = lax.broadcasted_iota(jnp.int32, (WIDTH, WIDTH // 2), 0)
        column = lax.broadcasted_iota(jnp.int32, (WIDTH, WIDTH // 2), 1)
        pick = row == sorted_rows(place_ref, half, 8, column)
        pick_ref[:, half * (WIDTH // 2) : (half + 1) * (WIDTH // 2)] = pick.astype(BF16)


def spatial_kernel(own_ref, other_ref, pick_ref, *rest):
    block_refs, (mixed_ref, weight_ref, packed, mixed) = rest[:-4], rest[-4:]
    block_refs = block_refs[0::2] + block_refs[1::2]
    normed = jnp.concatenate([own_ref[...], other_ref[...]], axis=1)
    weight = jnp.concatenate([ref[:, QKV : QKV + 3 * WIDTH] for ref in block_refs], axis=0)
    packed[...] = dot(normed, weight).astype(BF16)
    attend(packed, mixed, None)
    mixed_ref[...] = dot(mixed[...], pick_ref[...]).astype(BF16)
    halves = [
        ref[:, OUT : OUT + D // 2].astype(F32).reshape(ref.shape[0] // 16, 2, 8, D // 2)
        for ref in block_refs
    ]
    for side in range(2):
        weight = jnp.concatenate([half[:, side].reshape(-1, D // 2) for half in halves], axis=0)
        weight_ref[:, side * (D // 2) : (side + 1) * (D // 2)] = weight.astype(BF16)


def gather_rows(weights_ref, first, target, sems):
    width = target.shape[-1]
    return [
        pltpu.make_async_copy(
            weights_ref.at[y, c, :, :, first : first + width], target.at[:, y, c], sems.at[2 * y + c]
        )
        for y in range(Y)
        for c in range(2)
    ]


def pack_kernel(
    ids_ref, states_ref, qkv_ref, text_ref, out_s_ref, out_t_ref, video_ref, spatial_ref,
    packed_ref, copies_ref,
    ids_here, states_here, text_here, out_s_here, out_t_here, sems,
):
    pairs = (
        (spatial_ref, copies_ref.at[0, :, QKV : QKV + 3 * WIDTH]),
        (ids_ref, ids_here),
        (states_ref, states_here),
        (text_ref, text_here),
        (out_s_ref, out_s_here),
        (out_t_ref, out_t_here),
        (qkv_ref, packed_ref.at[:, QKV : QKV + 3 * WIDTH]),
        (video_ref, packed_ref.at[:, W_VIDEO : W_VIDEO + E]),
    )
    copies = [pltpu.make_async_copy(*pair, sems.at[i]) for i, pair in enumerate(pairs)]
    for copy in copies:
        copy.start()
    for copy in copies:
        copy.wait()
    for source, target in ((out_s_here, copies_ref.at[0]), (out_t_here, packed_ref)):
        rows = source[...].astype(F32)
        rows = jnp.concatenate([rows[:, : D // 2], rows[:, D // 2 :]], axis=0)
        target[:, OUT : OUT + D // 2] = rows.astype(BF16)
    for copy in range(1, Y):
        copies_ref[copy] = copies_ref[0]
    ids = ids_here[...]
    positions = lax.broadcasted_iota(jnp.int32, ids.shape, 1)
    end_place = jnp.min(jnp.where(ids == jnp.max(ids), positions, ids.shape[1]))
    states = states_here[...].astype(F32)
    rows = lax.broadcasted_iota(jnp.int32, states.shape, 0)
    text_row = jnp.sum(jnp.where(rows == end_place, states, 0.0), axis=0, keepdims=True)
    text = jnp.concatenate([text_here[...].astype(F32), jnp.zeros((4, E), F32)], axis=0)
    place = lax.broadcasted_iota(jnp.int32, text.shape, 0)
    text = jnp.where(place < 12, text, jnp.where(place == 12, text_row, 0.0))
    packed_ref[:, W_TEXT : W_TEXT + E] = text.astype(BF16)


def temporal_kernel(
    tokens_ref, mixed_ref, weight_ref, gain_ref, weights_ref, out_ref, pool_ref,
    qkv, outs, spatial_ref, packed, mixed, sems,
):
    copies_qkv = gather_rows(weights_ref, QKV, qkv, sems.at[0])
    copies_out = gather_rows(weights_ref, OUT, outs, sems.at[1])
    for copy in copies_qkv + copies_out:
        copy.start()
    rows = tokens_ref.shape[0]
    spatial = tokens_ref[...].astype(F32) + dot(mixed_ref[...], weight_ref[...])
    spatial_ref[...] = spatial.astype(BF16)
    normed = layer_norm(spatial_ref[...].astype(F32), gain_ref[...]).astype(BF16)
    for copy in copies_qkv:
        copy.wait()
    packed[...] = dot(normed, qkv[...].reshape(D, 3 * WIDTH)).astype(BF16)
    patches = rows // FRAMES
    place = lax.broadcasted_iota(jnp.int32, (rows, rows), 0) % patches
    attend(packed, mixed, place == lax.broadcasted_iota(jnp.int32, (rows, rows), 1) % patches)
    for copy in copies_out:
        copy.wait()
    half = D // 2
    for side, weight in enumerate(out_halves(outs[...])):
        columns = slice(side * half, (side + 1) * half)
        output = (spatial_ref[:, columns].astype(F32) + dot(mixed[...], weight)).astype(BF16)
        out_ref[:, columns] = output
        total = jnp.sum(output.astype(F32), axis=0, keepdims=True)
        for chunk in range(half // 128):
            pool_ref[:, side * (half // 128) + chunk, :] = jnp.broadcast_to(
                total[:, chunk * 128 : (chunk + 1) * 128], (FRAMES, 128)
            )


def spread_kernel(parts_ref, every_ref):
    mine = jnp.sum(parts_ref[...], axis=0) * (1.0 / (8 * 256))
    every_ref[...] = jnp.broadcast_to(mine[None], every_ref.shape)


def text_kernel(
    gain_ref, weights_ref, pool_ref, mapped_ref, weight_ref, video_ref, gathered, sems
):
    copies = gather_rows(weights_ref, W_TEXT, gathered, sems.at[0])
    copies_video = gather_rows(weights_ref, W_VIDEO, video_ref, sems.at[1])
    for copy in copies + copies_video:
        copy.start()
    for copy in copies:
        copy.wait()
    packed = gathered[...].reshape(D, E)
    column = lax.broadcasted_iota(jnp.int32, (DT, D), 1)
    place = column % 16
    row = jnp.where(place < 12, (column // 16) * 12 + place, -1)
    pick = (row == lax.broadcasted_iota(jnp.int32, (DT, D), 0)).astype(BF16)
    weight = dot(pick, packed).astype(BF16)
    weight_ref[...] = weight
    column = lax.broadcasted_iota(jnp.int32, (64, D), 1)
    pick = (column == 16 * lax.broadcasted_iota(jnp.int32, (64, D), 0) + 12).astype(BF16)
    pool = dot(pick, packed)
    pool_ref[...] = pool
    mapped_ref[...] = exact(dot, layer_norm(pool, gain_ref[...]), weight)
    for copy in copies_video:
        copy.wait()


def unit_rows(values):
    return values * lax.rsqrt(jnp.sum(values * values, axis=-1, keepdims=True) + UNIT_EPS)


def unit_back(mapped, grad):
    scale = lax.rsqrt(jnp.sum(mapped * mapped, axis=-1, keepdims=True) + UNIT_EPS)
    along = jnp.sum(mapped * grad, axis=-1, keepdims=True)
    return scale * grad - mapped * (scale * scale * scale * along)


def norm_back(values, gain, grad):
    center = values - jnp.mean(values, axis=-1, keepdims=True)
    scale = lax.rsqrt(jnp.mean(center * center, axis=-1, keepdims=True) + NORM_EPS)
    grad = grad * gain
    unit = center * scale
    along = jnp.mean(grad * unit, axis=-1, keepdims=True)
    return scale * (grad - jnp.mean(grad, axis=-1, keepdims=True) - unit * along)


def loss_kernel(
    place_ref,
    scale_ref,
    pairs_ref,
    pooled_ref,
    text_pool_ref,
    text_mapped_ref,
    text_weight_ref,
    gain_video_ref,
    gain_text_ref,
    video_weight_ref,
    video_loss_ref,
    text_loss_ref,
    grad_pooled_ref,
    grad_text_ref,
    pooled_all,
):
    me = place_ref[0]
    scale = scale_ref[0]
    for chunk in range(D // 128):
        pooled_all[:, chunk * 128 : (chunk + 1) * 128] = pooled_ref[:, chunk, :]
    gain = gain_video_ref[...]
    normed = layer_norm(pooled_all[...], gain)
    weight = video_weight_ref[...].reshape(D, E)
    mapped = exact(dot, normed, weight)
    video = unit_rows(mapped)
    text_mapped = text_mapped_ref[...]
    text = unit_rows(text_mapped)
    logits = scale * lax.dot_general(
        video, text, (((1,), (1,)), ((), ())), precision=lax.Precision.HIGHEST,
        preferred_element_type=F32,
    )
    count = logits.shape[0]
    rows = lax.broadcasted_iota(jnp.int32, (count, count), 0)
    columns = lax.broadcasted_iota(jnp.int32, (count, count), 1)
    match = pairs_ref[...] == columns
    row_top = jnp.max(logits, axis=1, keepdims=True)
    row_exp = jnp.exp(logits - row_top)
    row_sum = jnp.sum(row_exp, axis=1, keepdims=True)
    col_top = jnp.max(logits, axis=0, keepdims=True)
    col_exp = jnp.exp(logits - col_top)
    col_sum = jnp.sum(col_exp, axis=0, keepdims=True)
    positive = jnp.where(match, logits, 0.0)
    video_loss = 0.5 * (row_top + jnp.log(row_sum) - jnp.sum(positive, axis=1, keepdims=True))
    text_loss = 0.5 * (col_top + jnp.log(col_sum) - jnp.sum(positive, axis=0, keepdims=True))
    mine_row = lax.broadcasted_iota(jnp.int32, (count, 1), 0) == me
    mine_col = lax.broadcasted_iota(jnp.int32, (1, count), 1) == me
    video_loss_ref[0] = jnp.sum(jnp.where(mine_row, video_loss, 0.0))
    text_loss_ref[0] = jnp.sum(jnp.where(mine_col, text_loss, 0.0))
    slope = (0.5 * scale) * (row_exp / row_sum + col_exp / col_sum - 2.0 * match.astype(F32))
    row_slope = jnp.sum(jnp.where(rows == me, slope, 0.0), axis=0, keepdims=True)
    row_slope = jnp.sum(jnp.where(rows == columns, row_slope, 0.0), axis=1, keepdims=True)
    col_slope = jnp.sum(jnp.where(columns == me, slope, 0.0), axis=1, keepdims=True)
    grad_video = jnp.sum(row_slope * text, axis=0, keepdims=True)
    grad_caption = jnp.sum(col_slope * video, axis=0, keepdims=True)
    mine_mapped = jnp.sum(jnp.where(mine_row, mapped, 0.0), axis=0, keepdims=True)
    mine_text_mapped = jnp.sum(jnp.where(mine_row, text_mapped, 0.0), axis=0, keepdims=True)
    mine_pooled = jnp.sum(jnp.where(mine_row, pooled_all[...], 0.0), axis=0, keepdims=True)
    mine_text_pool = jnp.sum(jnp.where(mine_row, text_pool_ref[...], 0.0), axis=0, keepdims=True)
    back = exact_row(dot_t, unit_back(mine_mapped, grad_video), weight)
    grad_pooled_ref[...] = norm_back(mine_pooled, gain, back)
    back = exact_row(dot_t, unit_back(mine_text_mapped, grad_caption), text_weight_ref[...])
    grad_text_ref[...] = norm_back(mine_text_pool, gain_text_ref[...], back)


def call(kernel, out_shape, in_spaces, scratch, out_spaces=None, vmem=VMEM_LIMIT, flops=0):
    many = isinstance(out_shape, (tuple, list))
    out_spaces = out_spaces or ([pltpu.VMEM] * (len(out_shape) if many else 1))
    out_specs = [pl.BlockSpec(memory_space=space) for space in out_spaces]
    return pl.pallas_call(
        kernel,
        out_shape=out_shape,
        in_specs=[pl.BlockSpec(memory_space=space) for space in in_spaces],
        out_specs=out_specs if many else out_specs[0],
        scratch_shapes=scratch,
        compiler_params=pltpu.CompilerParams(vmem_limit_bytes=vmem),
        cost_estimate=pl.CostEstimate(flops=flops, bytes_accessed=0, transcendentals=0),
    )


def shape(dims, dtype):
    return jax.ShapeDtypeStruct(dims, dtype)


def send_all(copies, groups):
    return lax.all_to_all(copies, "dp", 0, 0, tiled=True, axis_index_groups=groups)


def on_device(
    video_tokens,
    text_states,
    caption_ids,
    pair_index,
    logit_scale,
    gain_spatial,
    gain_temporal,
    gain_video,
    gain_text,
    w_qkv_spatial,
    w_out_spatial,
    w_qkv_temporal,
    w_out_temporal,
    w_video,
    w_text,
):
    V, S, A = pltpu.VMEM, pltpu.SMEM, pl.ANY
    DMA = pltpu.SemaphoreType.DMA
    halves = (X, Y, 2, 16)
    tokens = video_tokens.reshape(256, D)
    place = lax.axis_index("dp").astype(jnp.int32).reshape(1)
    packed, own = call(
        pack_kernel,
        (shape((16, PACKED_T), BF16), shape((Y, 16, PACKED_S), BF16)),
        (A,) * 8,
        [
            pltpu.VMEM(caption_ids.shape, jnp.int32),
            pltpu.VMEM(text_states.shape[1:], BF16),
            pltpu.VMEM(w_text.shape, BF16),
            pltpu.VMEM(w_out_spatial.shape, BF16),
            pltpu.VMEM(w_out_temporal.shape, BF16),
            DMA((8,)),
        ],
        vmem=VMEM_WHOLE,
    )(
        caption_ids,
        text_states.reshape(text_states.shape[1:]),
        w_qkv_temporal,
        w_text,
        w_out_spatial,
        w_out_temporal,
        w_video,
        w_qkv_spatial,
    )
    barrier = lax.optimization_barrier
    gather = functools.partial(lax.all_gather, axis_name="dp", axis=0, tiled=True)
    own = send_all(own, ROWS_OF_Y)
    packed = gather(packed, axis_index_groups=ROWS_OF_X)
    own, packed = barrier((own, packed))
    weights = gather(packed, axis_index_groups=ROWS_OF_YC).reshape(Y, 2, X, 16, PACKED_T)
    permute = functools.partial(lax.ppermute, axis_name="dp")
    mine, late_tokens = barrier((own.reshape(BLOCK, PACKED_S), tokens))
    below, above = permute(mine, perm=X_UP), permute(mine, perm=X_DOWN)
    mine_other = permute(mine, perm=OTHER_CORE)
    by_patch = lax.all_to_all(late_tokens.reshape(FRAMES, 32, D), "frame", 0, 0, tiled=True)
    where = jnp.concatenate([place // (2 * Y), place % 2])
    *normed, pick = call(
        norm_kernel,
        (shape((256, D // 2), BF16),) * 2 + (shape((WIDTH, WIDTH), BF16),),
        (S, V, V),
        [],
        flops=1 << 30,
    )(where, late_tokens, gain_spatial.reshape(1, D))
    below, low, normed, pick = barrier((below, below[: BLOCK // 2], normed, pick))
    above, high = barrier((above, above[BLOCK // 2 :]))
    low, high = permute(low, perm=X_UP), permute(high, perm=X_DOWN)
    near, far = [mine, mine_other], []
    for block in (below, above):
        near += [block, permute(block, perm=OTHER_CORE)]
    for block in (low, high):
        far += [block, permute(block, perm=OTHER_CORE)]
    mixed, out_spatial = call(
        spatial_kernel,
        (shape((256, WIDTH), BF16), shape((WIDTH, D), BF16)),
        (V,) * 13,
        [pltpu.VMEM((256, 3 * WIDTH), BF16), pltpu.VMEM((256, WIDTH), BF16)],
        vmem=VMEM_SMALL,
    )(*normed, pick, *near, *far)
    mixed, by_patch = barrier((mixed, by_patch))
    mixed = lax.all_to_all(mixed.reshape(FRAMES, 32, WIDTH), "frame", 0, 0, tiled=True)
    layer_out, pool = call(
        temporal_kernel,
        (shape((256, D), BF16), shape((FRAMES, 8, 128), F32)),
        (V, V, V, V, A),
        [
            pltpu.VMEM(halves + (3 * WIDTH,), BF16),
            pltpu.VMEM(halves + (D // 2,), BF16),
            pltpu.VMEM((256, D), BF16),
            pltpu.VMEM((256, 3 * WIDTH), BF16),
            pltpu.VMEM((256, WIDTH), BF16),
            DMA((2, 2 * Y)),
        ],
    )(
        by_patch.reshape(256, D),
        mixed.reshape(256, WIDTH),
        out_spatial,
        gain_temporal.reshape(1, D),
        weights,
    )
    text_pool, text_mapped, text_weight, video_weight = call(
        text_kernel,
        (
            shape((64, DT), F32),
            shape((64, E), F32),
            shape((DT, E), BF16),
            shape(halves + (E,), BF16),
        ),
        (V, A),
        [pltpu.VMEM(halves + (E,), BF16), DMA((2, 2 * Y))],
    )(gain_text.reshape(1, DT), weights)
    pool = lax.all_to_all(pool, "frame", 0, 0, tiled=True)
    pool = call(spread_kernel, shape((64, 8, 128), F32), (V,), [])(pool)
    pooled = lax.all_to_all(pool, "dp", 0, 0, tiled=True)
    video_loss, text_loss, grad_pooled, grad_text = call(
        loss_kernel,
        (shape((1,), F32), shape((1,), F32), shape((1, D), F32), shape((1, DT), F32)),
        (S, S, V, V, V, V, V, V, V, V),
        [pltpu.VMEM((64, D), F32)],
        (S, S, V, V),
        vmem=VMEM_SMALL,
    )(
        place,
        logit_scale,
        pair_index.reshape(64, 1),
        pooled,
        text_pool,
        text_mapped,
        text_weight,
        gain_video.reshape(1, D),
        gain_text.reshape(1, DT),
        video_weight,
    )
    return (layer_out.reshape(1, 8, 32, D), video_loss, text_loss, grad_pooled, grad_text)


def solution(mesh):
    placed = (
        P("dp", "frame", None, None),
        P("dp", None, None),
        P("dp", None),
        P(),
        P(),
        P(),
        P(),
        P(),
        P(),
        P("dp", None),
        P("dp", None),
        P("dp", None),
        P("dp", None),
        P("dp", None),
        P("dp", None),
    )
    return jax.shard_map(
        on_device,
        mesh=mesh,
        in_specs=placed,
        out_specs=(P("dp", None, "frame", None), P("dp"), P("dp"), P("dp", None), P("dp", None)),
        check_vma=False,
    )
```

```python
import functools

import jax
import jax.numpy as jnp
from jax import lax
from jax.experimental import pallas as pl
from jax.experimental.pallas import tpu as pltpu
from jax.sharding import PartitionSpec as P

HEADS = 8
HD = 64
WIDTH = HEADS * HD
D = 1024
DT = 768
E = 768
NORM_EPS = 1e-05
UNIT_EPS = 1e-06
F32 = jnp.float32
BF16 = jnp.bfloat16
MIB = 1024 * 1024
VMEM_LIMIT = 48 * MIB
VMEM_WHOLE = 63 * MIB
VMEM_SMALL = 24 * MIB

QKV = 0
OUT = 1536
PACKED_S = 2048
W_TEXT = 2048
W_VIDEO = 2816
PACKED_T = 3584

X, Y = 4, 8
ROWS_OF_X = [[(x * Y + y) * 2 + c for x in range(X)] for y in range(Y) for c in range(2)]
ROWS_OF_Y = [[(x * Y + y) * 2 + c for y in range(Y)] for x in range(X) for c in range(2)]
ROWS_OF_YC = [[(x * Y + y) * 2 + c for y in range(Y) for c in range(2)] for x in range(X)]
OTHER_CORE = [(i, i ^ 1) for i in range(2 * X * Y)]
X_UP = [(i, (i + 2 * Y) % (2 * X * Y)) for i in range(2 * X * Y)]
X_DOWN = [(i, (i - 2 * Y) % (2 * X * Y)) for i in range(2 * X * Y)]
STEPS = (0, X - 1, 1, 2)
BLOCK = Y * 16
FRAMES = 8


def dot(a, b):
    return lax.dot_general(a, b, (((1,), (0,)), ((), ())), preferred_element_type=F32)


def dot_t(a, b):
    return lax.dot_general(a, b, (((1,), (1,)), ((), ())), preferred_element_type=F32)


def pieces(a):
    first = a.astype(BF16)
    rest = a - first.astype(F32)
    second = rest.astype(BF16)
    third = (rest - second.astype(F32)).astype(BF16)
    return first, second, third


def exact(dot_fn, a, weight):
    rows = a.shape[0]
    parts = dot_fn(jnp.concatenate(pieces(a), axis=0), weight)
    return parts[2 * rows :] + parts[rows : 2 * rows] + parts[:rows]


def exact_row(dot_fn, a, weight):
    rows = lax.broadcasted_iota(jnp.int32, (16, a.shape[1]), 0)
    first, second, third = (piece.astype(F32) for piece in pieces(a))
    block = jnp.where(rows == 0, third, jnp.where(rows == 1, second, jnp.where(rows == 2, first, 0.0)))
    return jnp.sum(dot_fn(block.astype(BF16), weight), axis=0, keepdims=True)


def layer_norm(values, gain):
    center = values - jnp.mean(values, axis=-1, keepdims=True)
    spread = jnp.mean(center * center, axis=-1, keepdims=True)
    return center * lax.rsqrt(spread + NORM_EPS) * gain


def attend_pair(query, key, value, mask):
    low = lax.broadcasted_iota(jnp.int32, query.shape, 1) < HD
    mixed = []
    for lanes in (low, ~low):
        scores = dot_t(jnp.where(lanes, query, jnp.zeros_like(query)), key) * (HD**-0.5)
        if mask is not None:
            scores = jnp.where(mask, scores, -1e30)
        weight = jnp.exp(scores - jnp.max(scores, axis=-1, keepdims=True))
        probs = weight * (1.0 / jnp.sum(weight, axis=-1, keepdims=True))
        mixed.append(dot(probs.astype(BF16), value))
    return jnp.where(low, mixed[0], mixed[1]).astype(BF16)


def attend(packed_ref, mixed_ref, mask):
    for at in range(0, WIDTH, 2 * HD):
        query, key, value = (
            packed_ref[:, part * WIDTH + at : part * WIDTH + at + 2 * HD] for part in range(3)
        )
        mixed_ref[:, at : at + 2 * HD] = attend_pair(query, key, value, mask)


def out_halves(gathered):
    halves = gathered.astype(F32).reshape(64, 2, 8, D // 2)
    return [halves[:, side].reshape(WIDTH, D // 2).astype(BF16) for side in range(2)]


def sorted_rows(place_ref, half, depth, column):
    block = column // (Y * depth)
    step = jnp.zeros_like(block)
    for number, value in enumerate(STEPS):
        step = jnp.where(block == number, value, step)
    x = (place_ref[0] + step) % X
    core = place_ref[1] if half == 0 else 1 - place_ref[1]
    y = column // depth % Y
    return ((x * Y + y) * 2 + core) * depth + column % depth


def norm_kernel(place_ref, tokens_ref, gain_ref, own_ref, other_ref, pick_ref):
    normed = layer_norm(tokens_ref[...].astype(F32), gain_ref[...]).astype(BF16)
    for half, target in enumerate((own_ref, other_ref)):
        row = lax.broadcasted_iota(jnp.int32, (D, D // 2), 0)
        column = lax.broadcasted_iota(jnp.int32, (D, D // 2), 1)
        pick = row == sorted_rows(place_ref, half, 16, column)
        target[...] = dot(normed, pick.astype(BF16)).astype(BF16)
        row = lax.broadcasted_iota(jnp.int32, (WIDTH, WIDTH // 2), 0)
        column = lax.broadcasted_iota(jnp.int32, (WIDTH, WIDTH // 2), 1)
        pick = row == sorted_rows(place_ref, half, 8, column)
        pick_ref[:, half * (WIDTH // 2) : (half + 1) * (WIDTH // 2)] = pick.astype(BF16)


def spatial_kernel(own_ref, other_ref, pick_ref, *rest):
    block_refs, (mixed_ref, weight_ref, packed, mixed) = rest[:-4], rest[-4:]
    block_refs = block_refs[0::2] + block_refs[1::2]
    normed = jnp.concatenate([own_ref[...], other_ref[...]], axis=1)
    weight = jnp.concatenate([ref[:, QKV : QKV + 3 * WIDTH] for ref in block_refs], axis=0)
    packed[...] = dot(normed, weight).astype(BF16)
    attend(packed, mixed, None)
    mixed_ref[...] = dot(mixed[...], pick_ref[...]).astype(BF16)
    halves = [
        ref[:, OUT : OUT + D // 2].astype(F32).reshape(ref.shape[0] // 16, 2, 8, D // 2)
        for ref in block_refs
    ]
    for side in range(2):
        weight = jnp.concatenate([half[:, side].reshape(-1, D // 2) for half in halves], axis=0)
        weight_ref[:, side * (D // 2) : (side + 1) * (D // 2)] = weight.astype(BF16)


def gather_rows(weights_ref, first, target, sems):
    width = target.shape[-1]
    return [
        pltpu.make_async_copy(
            weights_ref.at[y, c, :, :, first : first + width], target.at[:, y, c], sems.at[2 * y + c]
        )
        for y in range(Y)
        for c in range(2)
    ]


def pack_kernel(
    ids_ref, states_ref, qkv_ref, text_ref, out_s_ref, out_t_ref, video_ref, spatial_ref,
    packed_ref, copies_ref,
    ids_here, states_here, text_here, out_s_here, out_t_here, sems,
):
    pairs = (
        (spatial_ref, copies_ref.at[0, :, QKV : QKV + 3 * WIDTH]),
        (ids_ref, ids_here),
        (states_ref, states_here),
        (text_ref, text_here),
        (out_s_ref, out_s_here),
        (out_t_ref, out_t_here),
        (qkv_ref, packed_ref.at[:, QKV : QKV + 3 * WIDTH]),
        (video_ref, packed_ref.at[:, W_VIDEO : W_VIDEO + E]),
    )
    copies = [pltpu.make_async_copy(*pair, sems.at[i]) for i, pair in enumerate(pairs)]
    for copy in copies:
        copy.start()
    for copy in copies:
        copy.wait()
    for source, target in ((out_s_here, copies_ref.at[0]), (out_t_here, packed_ref)):
        rows = source[...].astype(F32)
        rows = jnp.concatenate([rows[:, : D // 2], rows[:, D // 2 :]], axis=0)
        target[:, OUT : OUT + D // 2] = rows.astype(BF16)
    for copy in range(1, Y):
        copies_ref[copy] = copies_ref[0]
    ids = ids_here[...]
    positions = lax.broadcasted_iota(jnp.int32, ids.shape, 1)
    end_place = jnp.min(jnp.where(ids == jnp.max(ids), positions, ids.shape[1]))
    states = states_here[...].astype(F32)
    rows = lax.broadcasted_iota(jnp.int32, states.shape, 0)
    text_row = jnp.sum(jnp.where(rows == end_place, states, 0.0), axis=0, keepdims=True)
    text = jnp.concatenate([text_here[...].astype(F32), jnp.zeros((4, E), F32)], axis=0)
    place = lax.broadcasted_iota(jnp.int32, text.shape, 0)
    text = jnp.where(place < 12, text, jnp.where(place == 12, text_row, 0.0))
    packed_ref[:, W_TEXT : W_TEXT + E] = text.astype(BF16)


def temporal_kernel(
    tokens_ref, mixed_ref, weight_ref, gain_ref, weights_ref, out_ref, pool_ref,
    qkv, outs, spatial_ref, packed, mixed, sems,
):
    copies_qkv = gather_rows(weights_ref, QKV, qkv, sems.at[0])
    copies_out = gather_rows(weights_ref, OUT, outs, sems.at[1])
    for copy in copies_qkv + copies_out:
        copy.start()
    rows = tokens_ref.shape[0]
    spatial = tokens_ref[...].astype(F32) + dot(mixed_ref[...], weight_ref[...])
    spatial_ref[...] = spatial.astype(BF16)
    normed = layer_norm(spatial_ref[...].astype(F32), gain_ref[...]).astype(BF16)
    for copy in copies_qkv:
        copy.wait()
    packed[...] = dot(normed, qkv[...].reshape(D, 3 * WIDTH)).astype(BF16)
    patches = rows // FRAMES
    place = lax.broadcasted_iota(jnp.int32, (rows, rows), 0) % patches
    attend(packed, mixed, place == lax.broadcasted_iota(jnp.int32, (rows, rows), 1) % patches)
    for copy in copies_out:
        copy.wait()
    half = D // 2
    for side, weight in enumerate(out_halves(outs[...])):
        columns = slice(side * half, (side + 1) * half)
        output = (spatial_ref[:, columns].astype(F32) + dot(mixed[...], weight)).astype(BF16)
        out_ref[:, columns] = output
        total = jnp.sum(output.astype(F32), axis=0, keepdims=True)
        for chunk in range(half // 128):
            pool_ref[:, side * (half // 128) + chunk, :] = jnp.broadcast_to(
                total[:, chunk * 128 : (chunk + 1) * 128], (FRAMES, 128)
            )


def spread_kernel(parts_ref, every_ref):
    mine = jnp.sum(parts_ref[...], axis=0) * (1.0 / (8 * 256))
    every_ref[...] = jnp.broadcast_to(mine[None], every_ref.shape)


def text_kernel(
    gain_ref, weights_ref, pool_ref, mapped_ref, weight_ref, video_ref, gathered, sems
):
    copies = gather_rows(weights_ref, W_TEXT, gathered, sems.at[0])
    copies_video = gather_rows(weights_ref, W_VIDEO, video_ref, sems.at[1])
    for copy in copies + copies_video:
        copy.start()
    for copy in copies:
        copy.wait()
    packed = gathered[...].reshape(D, E)
    column = lax.broadcasted_iota(jnp.int32, (DT, D), 1)
    place = column % 16
    row = jnp.where(place < 12, (column // 16) * 12 + place, -1)
    pick = (row == lax.broadcasted_iota(jnp.int32, (DT, D), 0)).astype(BF16)
    weight = dot(pick, packed).astype(BF16)
    weight_ref[...] = weight
    column = lax.broadcasted_iota(jnp.int32, (64, D), 1)
    pick = (column == 16 * lax.broadcasted_iota(jnp.int32, (64, D), 0) + 12).astype(BF16)
    pool = dot(pick, packed)
    pool_ref[...] = pool
    mapped_ref[...] = exact(dot, layer_norm(pool, gain_ref[...]), weight)
    for copy in copies_video:
        copy.wait()


def unit_rows(values):
    return values * lax.rsqrt(jnp.sum(values * values, axis=-1, keepdims=True) + UNIT_EPS)


def unit_back(mapped, grad):
    scale = lax.rsqrt(jnp.sum(mapped * mapped, axis=-1, keepdims=True) + UNIT_EPS)
    along = jnp.sum(mapped * grad, axis=-1, keepdims=True)
    return scale * grad - mapped * (scale * scale * scale * along)


def norm_back(values, gain, grad):
    center = values - jnp.mean(values, axis=-1, keepdims=True)
    scale = lax.rsqrt(jnp.mean(center * center, axis=-1, keepdims=True) + NORM_EPS)
    grad = grad * gain
    unit = center * scale
    along = jnp.mean(grad * unit, axis=-1, keepdims=True)
    return scale * (grad - jnp.mean(grad, axis=-1, keepdims=True) - unit * along)


def loss_kernel(
    place_ref,
    scale_ref,
    pairs_ref,
    pooled_ref,
    text_pool_ref,
    text_mapped_ref,
    text_weight_ref,
    gain_video_ref,
    gain_text_ref,
    video_weight_ref,
    video_loss_ref,
    text_loss_ref,
    grad_pooled_ref,
    grad_text_ref,
    pooled_all,
):
    me = place_ref[0]
    scale = scale_ref[0]
    for chunk in range(D // 128):
        pooled_all[:, chunk * 128 : (chunk + 1) * 128] = pooled_ref[:, chunk, :]
    gain = gain_video_ref[...]
    normed = layer_norm(pooled_all[...], gain)
    weight = video_weight_ref[...].reshape(D, E)
    mapped = exact(dot, normed, weight)
    video = unit_rows(mapped)
    text_mapped = text_mapped_ref[...]
    text = unit_rows(text_mapped)
    logits = scale * lax.dot_general(
        video, text, (((1,), (1,)), ((), ())), precision=lax.Precision.HIGHEST,
        preferred_element_type=F32,
    )
    count = logits.shape[0]
    rows = lax.broadcasted_iota(jnp.int32, (count, count), 0)
    columns = lax.broadcasted_iota(jnp.int32, (count, count), 1)
    match = pairs_ref[...] == columns
    row_top = jnp.max(logits, axis=1, keepdims=True)
    row_exp = jnp.exp(logits - row_top)
    row_sum = jnp.sum(row_exp, axis=1, keepdims=True)
    col_top = jnp.max(logits, axis=0, keepdims=True)
    col_exp = jnp.exp(logits - col_top)
    col_sum = jnp.sum(col_exp, axis=0, keepdims=True)
    positive = jnp.where(match, logits, 0.0)
    video_loss = 0.5 * (row_top + jnp.log(row_sum) - jnp.sum(positive, axis=1, keepdims=True))
    text_loss = 0.5 * (col_top + jnp.log(col_sum) - jnp.sum(positive, axis=0, keepdims=True))
    mine_row = lax.broadcasted_iota(jnp.int32, (count, 1), 0) == me
    mine_col = lax.broadcasted_iota(jnp.int32, (1, count), 1) == me
    video_loss_ref[0] = jnp.sum(jnp.where(mine_row, video_loss, 0.0))
    text_loss_ref[0] = jnp.sum(jnp.where(mine_col, text_loss, 0.0))
    slope = (0.5 * scale) * (row_exp / row_sum + col_exp / col_sum - 2.0 * match.astype(F32))
    row_slope = jnp.sum(jnp.where(rows == me, slope, 0.0), axis=0, keepdims=True)
    row_slope = jnp.sum(jnp.where(rows == columns, row_slope, 0.0), axis=1, keepdims=True)
    col_slope = jnp.sum(jnp.where(columns == me, slope, 0.0), axis=1, keepdims=True)
    grad_video = jnp.sum(row_slope * text, axis=0, keepdims=True)
    grad_caption = jnp.sum(col_slope * video, axis=0, keepdims=True)
    mine_mapped = jnp.sum(jnp.where(mine_row, mapped, 0.0), axis=0, keepdims=True)
    mine_text_mapped = jnp.sum(jnp.where(mine_row, text_mapped, 0.0), axis=0, keepdims=True)
    mine_pooled = jnp.sum(jnp.where(mine_row, pooled_all[...], 0.0), axis=0, keepdims=True)
    mine_text_pool = jnp.sum(jnp.where(mine_row, text_pool_ref[...], 0.0), axis=0, keepdims=True)
    back = exact_row(dot_t, unit_back(mine_mapped, grad_video), weight)
    grad_pooled_ref[...] = norm_back(mine_pooled, gain, back)
    back = exact_row(dot_t, unit_back(mine_text_mapped, grad_caption), text_weight_ref[...])
    grad_text_ref[...] = norm_back(mine_text_pool, gain_text_ref[...], back)


def call(kernel, out_shape, in_spaces, scratch, out_spaces=None, vmem=VMEM_LIMIT, flops=0):
    many = isinstance(out_shape, (tuple, list))
    out_spaces = out_spaces or ([pltpu.VMEM] * (len(out_shape) if many else 1))
    out_specs = [pl.BlockSpec(memory_space=space) for space in out_spaces]
    return pl.pallas_call(
        kernel,
        out_shape=out_shape,
        in_specs=[pl.BlockSpec(memory_space=space) for space in in_spaces],
        out_specs=out_specs if many else out_specs[0],
        scratch_shapes=scratch,
        compiler_params=pltpu.CompilerParams(vmem_limit_bytes=vmem),
        cost_estimate=pl.CostEstimate(flops=flops, bytes_accessed=0, transcendentals=0),
    )


def shape(dims, dtype):
    return jax.ShapeDtypeStruct(dims, dtype)


def send_all(copies, groups):
    return lax.all_to_all(copies, "dp", 0, 0, tiled=True, axis_index_groups=groups)


def on_device(
    video_tokens,
    text_states,
    caption_ids,
    pair_index,
    logit_scale,
    gain_spatial,
    gain_temporal,
    gain_video,
    gain_text,
    w_qkv_spatial,
    w_out_spatial,
    w_qkv_temporal,
    w_out_temporal,
    w_video,
    w_text,
):
    V, S, A = pltpu.VMEM, pltpu.SMEM, pl.ANY
    DMA = pltpu.SemaphoreType.DMA
    halves = (X, Y, 2, 16)
    tokens = video_tokens.reshape(256, D)
    place = lax.axis_index("dp").astype(jnp.int32).reshape(1)
    packed, own = call(
        pack_kernel,
        (shape((16, PACKED_T), BF16), shape((Y, 16, PACKED_S), BF16)),
        (A,) * 8,
        [
            pltpu.VMEM(caption_ids.shape, jnp.int32),
            pltpu.VMEM(text_states.shape[1:], BF16),
            pltpu.VMEM(w_text.shape, BF16),
            pltpu.VMEM(w_out_spatial.shape, BF16),
            pltpu.VMEM(w_out_temporal.shape, BF16),
            DMA((8,)),
        ],
        vmem=VMEM_WHOLE,
    )(
        caption_ids,
        text_states.reshape(text_states.shape[1:]),
        w_qkv_temporal,
        w_text,
        w_out_spatial,
        w_out_temporal,
        w_video,
        w_qkv_spatial,
    )
    barrier = lax.optimization_barrier
    gather = functools.partial(lax.all_gather, axis_name="dp", axis=0, tiled=True)
    own = send_all(own, ROWS_OF_Y)
    packed = gather(packed, axis_index_groups=ROWS_OF_X)
    own, packed = barrier((own, packed))
    weights = gather(packed, axis_index_groups=ROWS_OF_YC).reshape(Y, 2, X, 16, PACKED_T)
    permute = functools.partial(lax.ppermute, axis_name="dp")
    mine, late_tokens = barrier((own.reshape(BLOCK, PACKED_S), tokens))
    below, above = permute(mine, perm=X_UP), permute(mine, perm=X_DOWN)
    by_patch = lax.all_to_all(late_tokens.reshape(FRAMES, 32, D), "frame", 0, 0, tiled=True)
    where = jnp.concatenate([place // (2 * Y), place % 2])
    *normed, pick = call(
        norm_kernel,
        (shape((256, D // 2), BF16),) * 2 + (shape((WIDTH, WIDTH), BF16),),
        (S, V, V),
        [],
        flops=1 << 30,
    )(where, late_tokens, gain_spatial.reshape(1, D))
    below, low, normed, pick = barrier((below, below[: BLOCK // 2], normed, pick))
    above, high, swapped = barrier((above, above[BLOCK // 2 :], mine))
    low, high = permute(low, perm=X_UP), permute(high, perm=X_DOWN)
    near, far = [mine, permute(swapped, perm=OTHER_CORE)], []
    for block in (below, above):
        near += [block, permute(block, perm=OTHER_CORE)]
    for block in (low, high):
        far += [block, permute(block, perm=OTHER_CORE)]
    mixed, out_spatial = call(
        spatial_kernel,
        (shape((256, WIDTH), BF16), shape((WIDTH, D), BF16)),
        (V,) * 13,
        [pltpu.VMEM((256, 3 * WIDTH), BF16), pltpu.VMEM((256, WIDTH), BF16)],
        vmem=VMEM_SMALL,
    )(*normed, pick, *near, *far)
    mixed, by_patch = barrier((mixed, by_patch))
    mixed = lax.all_to_all(mixed.reshape(FRAMES, 32, WIDTH), "frame", 0, 0, tiled=True)
    layer_out, pool = call(
        temporal_kernel,
        (shape((256, D), BF16), shape((FRAMES, 8, 128), F32)),
        (V, V, V, V, A),
        [
            pltpu.VMEM(halves + (3 * WIDTH,), BF16),
            pltpu.VMEM(halves + (D // 2,), BF16),
            pltpu.VMEM((256, D), BF16),
            pltpu.VMEM((256, 3 * WIDTH), BF16),
            pltpu.VMEM((256, WIDTH), BF16),
            DMA((2, 2 * Y)),
        ],
    )(
        by_patch.reshape(256, D),
        mixed.reshape(256, WIDTH),
        out_spatial,
        gain_temporal.reshape(1, D),
        weights,
    )
    text_pool, text_mapped, text_weight, video_weight = call(
        text_kernel,
        (
            shape((64, DT), F32),
            shape((64, E), F32),
            shape((DT, E), BF16),
            shape(halves + (E,), BF16),
        ),
        (V, A),
        [pltpu.VMEM(halves + (E,), BF16), DMA((2, 2 * Y))],
    )(gain_text.reshape(1, DT), weights)
    pool = lax.all_to_all(pool, "frame", 0, 0, tiled=True)
    pool = call(spread_kernel, shape((64, 8, 128), F32), (V,), [])(pool)
    pooled = lax.all_to_all(pool, "dp", 0, 0, tiled=True)
    video_loss, text_loss, grad_pooled, grad_text = call(
        loss_kernel,
        (shape((1,), F32), shape((1,), F32), shape((1, D), F32), shape((1, DT), F32)),
        (S, S, V, V, V, V, V, V, V, V),
        [pltpu.VMEM((64, D), F32)],
        (S, S, V, V),
        vmem=VMEM_SMALL,
    )(
        place,
        logit_scale,
        pair_index.reshape(64, 1),
        pooled,
        text_pool,
        text_mapped,
        text_weight,
        gain_video.reshape(1, D),
        gain_text.reshape(1, DT),
        video_weight,
    )
    return (layer_out.reshape(1, 8, 32, D), video_loss, text_loss, grad_pooled, grad_text)


def solution(mesh):
    placed = (
        P("dp", "frame", None, None),
        P("dp", None, None),
        P("dp", None),
        P(),
        P(),
        P(),
        P(),
        P(),
        P(),
        P("dp", None),
        P("dp", None),
        P("dp", None),
        P("dp", None),
        P("dp", None),
        P("dp", None),
    )
    return jax.shard_map(
        on_device,
        mesh=mesh,
        in_specs=placed,
        out_specs=(P("dp", None, "frame", None), P("dp"), P("dp"), P("dp", None), P("dp", None)),
        check_vma=False,
    )
```
